32 devices in a mesh: expert: 16 (over z, y, x), fsdp: 2 (over core).
Axes of the slice: x: 2, y: 2, z: 4, core: 2. Of those that a mesh axis runs over, the one named last changes fastest.
Arguments:
- tokens: bfloat16 [4096, 2048], P(('expert', 'fsdp')), may hold values from -6 to 6
- segments: int32 [4096], P('expert'), may hold values from 0 to 47, as said below
- routes: int32 [4096, 6], P(('expert', 'fsdp')), may hold values from 0 to 15, all different within a row; in each aligned block of 128 rows (0 to 127, 128 to 255, ...) at most 96 rows name the same one
- norm_attn: bfloat16 [2048], P(('expert', 'fsdp')), may hold values from 0.5 to 1.5
- query_proj: bfloat16 [2048, 3072], P(('expert', 'fsdp')), may hold values from -0.125 to 0.125
- latent_proj: bfloat16 [2048, 576], P(('expert', 'fsdp')), may hold values from -0.125 to 0.125
- norm_latent: bfloat16 [512], P(('expert', 'fsdp')), may hold values from 0.5 to 1.5
- expand_proj: bfloat16 [512, 4096], P(('expert', 'fsdp')), may hold values from -0.25 to 0.25
- output_proj: bfloat16 [2048, 2048], P(('expert', 'fsdp')), may hold values from -1.0546875 to 1.0546875
- norm_ffn: bfloat16 [2048], P(('expert', 'fsdp')), may hold values from 0.5 to 1.5
- router: bfloat16 [2048, 16], P(('expert', 'fsdp')), may hold values from -0.06591797 to 0.06591797
- shared_gate: bfloat16 [2048, 2816], P(('expert', 'fsdp')), may hold values from -0.125 to 0.125
- shared_up: bfloat16 [2048, 2816], P(('expert', 'fsdp')), may hold values from -0.125 to 0.125
- shared_down: bfloat16 [2816, 2048], P(('expert', 'fsdp')), may hold values from -0.109375 to 0.109375
- expert_gate: bfloat16 [16, 2048, 1408], P('expert', 'fsdp'), may hold values from -0.125 to 0.125
- expert_up: bfloat16 [16, 2048, 1408], P('expert', 'fsdp'), may hold values from -0.125 to 0.125
- expert_down: bfloat16 [16, 1408, 2048], P('expert', 'fsdp'), may hold values from -0.15625 to 0.15625
- cotangent: bfloat16 [4096, 2048], P(('expert', 'fsdp')), may hold values from -6 to 6
Outputs:
- block_out: bfloat16 [4096, 2048], P(('expert', 'fsdp'))
- tokens_grad: bfloat16 [4096, 2048], P(('expert', 'fsdp'))
- norm_attn_grad: float32 [2048], P(('expert', 'fsdp'))
- query_proj_grad: float32 [2048, 3072], P(('expert', 'fsdp'))
- latent_proj_grad: float32 [2048, 576], P(('expert', 'fsdp'))
- norm_latent_grad: float32 [512], P(('expert', 'fsdp'))
- expand_proj_grad: float32 [512, 4096], P(('expert', 'fsdp'))
- output_proj_grad: float32 [2048, 2048], P(('expert', 'fsdp'))
- norm_ffn_grad: float32 [2048], P(('expert', 'fsdp'))
- router_grad: float32 [2048, 16], P(('expert', 'fsdp'))
- shared_gate_grad: float32 [2048, 2816], P(('expert', 'fsdp'))
- shared_up_grad: float32 [2048, 2816], P(('expert', 'fsdp'))
- shared_down_grad: float32 [2816, 2048], P(('expert', 'fsdp'))
- expert_gate_grad: float32 [16, 2048, 1408], P('expert', 'fsdp')
- expert_up_grad: float32 [16, 2048, 1408], P('expert', 'fsdp')
- expert_down_grad: float32 [16, 1408, 2048], P('expert', 'fsdp')
The draws below stay inside these ranges and needn't reach their ends.
Inputs may be any that keep to these rules, and one draw needn't show every extreme that they name: `segments`: within each sequence of 256 tokens the numbers never fall; sequence s holds documents 3 s, 3 s + 1, 3 s + 2, and the middle one begins among its first 128 tokens and ends among its last 128. `routes`: each row names 6 different experts; in each aligned block of 128 rows no expert is named more than 96 times, a bound that some block reaches.
All inputs are finite; a program needn't handle non-finite values.
Results may differ from the reference program's by a relative error of at most 0.019.
Values may be sent and summed in bfloat16 or wider, within the bound.
No kernel may reach another device: no remote copies, remote signals or barrier semaphores. Data moves between devices by JAX's collectives and lax.ppermute only.
A program may use at most 384 MiB of HBM per device.

```python
import math
from functools import partial
import jax
import jax.numpy as jnp
import numpy as np
from jax import lax

D = 2048
H = 16
DN = 128
DR = 64
DV = 128
KVR = 512
FF = 1408
TOPK = 6
SFF = 2816
SEQ_DEV = 128
EXPERTS = 16
SEQ = 256
TOKENS = 4096
CAP = 96


def draw_segments(key, part):
    key = jax.random.fold_in(key, 7)
    start_key, end_key = jax.random.split(key)
    groups = TOKENS // SEQ
    starts = jax.random.randint(start_key, (groups, 1), 1, SEQ_DEV)
    ends = SEQ - jax.random.randint(end_key, (groups, 1), 1, SEQ_DEV)
    places = jnp.arange(SEQ, dtype=jnp.int32)[None, :]
    inside = (places >= starts).astype(jnp.int32) + (places >= ends).astype(jnp.int32)
    return (inside + 3 * jnp.arange(groups, dtype=jnp.int32)[:, None]).reshape(-1).astype(jnp.int32)


def block_levels(rng, dims, cuts, least, largest):
    factor_of, own = 1.0, jax.random.fold_in(rng, 6)
    for dim, parts in cuts:
        heights = jnp.exp(jax.random.uniform(jax.random.fold_in(own, dim), (parts,), jnp.float32, least / len(cuts), largest / len(cuts)))
        factor_of = factor_of * jnp.repeat(heights, dims[dim] // parts).reshape([-1 if axis == dim else 1 for axis in range(len(dims))])
    return factor_of


def routed_block(own_key, own, number, rows, amount, top, most, lean):
    order = jax.random.permutation(own_key, amount)
    crowded, common = shares(amount, rows * top, most, lean, True), shares(amount, rows * top, most, lean, False)
    places = jnp.arange(amount)

    def named(tallies, offset_by):
        used = int((tallies > 0).sum())
        fixed = max(1, used // 4)
        shifted = fixed + (places - fixed + offset_by * (used - fixed)) % max(1, amount - fixed)
        return jnp.zeros((amount,), jnp.int32).at[order[jnp.where(places < fixed, places, shifted)]].set(jnp.asarray(tallies, jnp.int32))

    tallies = jnp.where(number % 4 == 0, named(crowded, number // 4), named(common, number - number // 4 - 1))
    mixed = jax.random.permutation(jax.random.fold_in(own, 3), amount)
    donor, taker = mixed[0:amount // 2 * 2:2], mixed[1:amount // 2 * 2:2]
    margin = jnp.minimum(tallies[donor] - 1, most - tallies[taker]) // 2
    margin = jnp.where((donor == order[0]) | (taker == order[0]) | (tallies[taker] == 0), 0, jnp.maximum(margin, 0))
    shifted = jax.random.randint(jax.random.fold_in(own, 4), (amount // 2,), 0, 1 << 20) % (margin + 1)
    tallies = tallies.at[donor].add(-shifted).at[taker].add(shifted)
    labels = jnp.searchsorted(jnp.cumsum(tallies), jnp.arange(rows * top), side="right").astype(jnp.int32)
    table = labels.reshape(top, rows).T
    table = table[jax.random.permutation(jax.random.fold_in(own, 1), rows)]
    offset_by = jax.random.randint(jax.random.fold_in(own, 2), (rows, 1), 0, top)
    return jnp.take_along_axis(table, (jnp.arange(top)[None, :] + offset_by) % top, axis=1)


def shares(amount, total, most, skew, full):
    weights = [(1 << 20) // math.isqrt(standing ** skew) + 1 for standing in range(1, amount + 1)]
    largest = most if full else min(most, max(-(-total // amount), total * weights[0] // sum(weights)))
    least = 1 if total - largest >= amount - 1 else 0
    counts, rest = [largest] + [least] * (amount - 1), total - largest - least * (amount - 1)
    while rest > 0:
        candidates = [i for i in range(1, amount) if counts[i] < largest] or [i for i in range(1, amount) if counts[i] < most]
        pool, left = sum([weights[i] for i in candidates]), rest
        for i in candidates:
            extra = min(most - counts[i], max(1, left * weights[i] // pool), rest)
            counts[i] = counts[i] + extra
            rest = rest - extra
    return np.array(counts)


def normal_values(own_key, dims, width, limit, shards=(), kind=jnp.bfloat16):
    values = width * jax.random.normal(own_key, dims, jnp.float32)
    if shards:
        values = values * block_levels(own_key, dims, shards, -0.22, 0.18)
    return jnp.clip(values, -limit, limit).astype(kind)


def setup_inputs(seed: int = 0) -> dict:
    splits = jax.random.split(jax.random.key(seed), 19)
    tokens = normal_values(splits[0], (TOKENS, D), 1.0, 6.0, ((0, 32),))
    segments = draw_segments(jax.random.fold_in(splits[18], 71), 0)
    routes_keys = jax.random.split(jax.random.fold_in(splits[2], 1), TOKENS // SEQ_DEV)
    routes_turns = jax.random.permutation(jax.random.fold_in(splits[2], 3), TOKENS // SEQ_DEV)
    routes = jax.vmap(lambda own, number: routed_block(jax.random.fold_in(splits[2], 2), own, number, SEQ_DEV, EXPERTS, TOPK, CAP, 2))(routes_keys, routes_turns).reshape((TOKENS, TOPK))
    norm_attn = jnp.clip(1.0 + 0.1 * jax.random.normal(splits[3], (D,), jnp.float32), 0.5, 1.5).astype(jnp.bfloat16)
    query_proj = normal_values(splits[4], (D, H * (DN + DR)), D ** -0.5, 0.125, ((0, 32),))
    latent_proj = normal_values(splits[5], (D, KVR + DR), D ** -0.5, 0.125, ((0, 32),))
    norm_latent = jnp.clip(1.0 + 0.1 * jax.random.normal(splits[6], (KVR,), jnp.float32), 0.5, 1.5).astype(jnp.bfloat16)
    expand_proj = normal_values(splits[7], (KVR, H * (DN + DV)), KVR ** -0.5, 0.25, ((0, 32),))
    output_proj = normal_values(splits[8], (H * DV, D), (8.0 / (H * DV) ** 0.5), 1.0546875, ((0, 32),))
    norm_ffn = jnp.clip(1.0 + 0.1 * jax.random.normal(splits[9], (D,), jnp.float32), 0.5, 1.5).astype(jnp.bfloat16)
    router = normal_values(splits[10], (D, EXPERTS), (0.5 / D ** 0.5), 0.06591797, ((0, 32),))
    shared_gate = normal_values(splits[11], (D, SFF), D ** -0.5, 0.125, ((0, 32),))
    shared_up = normal_values(splits[12], (D, SFF), D ** -0.5, 0.125, ((0, 32),))
    shared_down = normal_values(splits[13], (SFF, D), SFF ** -0.5, 0.109375, ((0, 32),))
    expert_gate = normal_values(splits[14], (EXPERTS, D, FF), D ** -0.5, 0.125, ((0, 16), (1, 2)))
    expert_up = normal_values(splits[15], (EXPERTS, D, FF), D ** -0.5, 0.125, ((0, 16), (1, 2)))
    expert_down = normal_values(splits[16], (EXPERTS, FF, D), FF ** -0.5, 0.15625, ((0, 16), (1, 2)))
    cotangent = normal_values(splits[17], (TOKENS, D), 1.0, 6.0, ((0, 32),))
    return {"tokens": tokens, "segments": segments, "routes": routes, "norm_attn": norm_attn, "query_proj": query_proj, "latent_proj": latent_proj, "norm_latent": norm_latent, "expand_proj": expand_proj, "output_proj": output_proj, "norm_ffn": norm_ffn, "router": router, "shared_gate": shared_gate, "shared_up": shared_up, "shared_down": shared_down, "expert_gate": expert_gate, "expert_up": expert_up, "expert_down": expert_down, "cotangent": cotangent}


NORM_EPS = 1e-06
ROPE_THETA = 50000.0
GATE_SCALE = 2.446
FULL_PRECISION = lax.Precision.HIGHEST

@jax.custom_vjp
def low(v):
    return lax.optimization_barrier(v.astype(jnp.bfloat16)).astype(jnp.float32)

@jax.custom_vjp
def low_back(v):
    return v

def low_keep(v):
    return (low(v), None)

def low_pass(kept, grad):
    return (grad,)

def back_keep(v):
    return (v, None)

def back_low(kept, grad):
    return (low(grad),)
low.defvjp(low_keep, low_pass)
low_back.defvjp(back_keep, back_low)

def matmul(left_side, right_side):
    return jnp.dot(left_side, right_side, precision=FULL_PRECISION)

def rms_scale(values, gain_vec):
    return values * lax.rsqrt(lax.optimization_barrier(jnp.mean(values * values, axis=-1, keepdims=True)) + NORM_EPS) * gain_vec

def rotate(values, cos_table, sin_table):
    middle = values.shape[-1] // 2
    lower_half = values[..., :middle]
    upper_half = values[..., middle:]
    return jnp.concatenate([lower_half * cos_table - upper_half * sin_table, upper_half * cos_table + lower_half * sin_table], axis=-1)

def rope_tables(positions):
    steps_float = jnp.arange(DR // 2).astype(jnp.float32) * (2.0 / DR)
    inverse = jnp.exp(-steps_float * math.log(ROPE_THETA))
    turned = positions.astype(jnp.float32)[:, None] * inverse[None, :]
    return (jnp.cos(turned), jnp.sin(turned))

def slot_tables(routes):
    blocks = routes.shape[0] // SEQ_DEV
    flat_routes = routes.reshape(blocks, SEQ_DEV * TOPK)
    onehot = (flat_routes[:, :, None] == jnp.arange(EXPERTS, dtype=jnp.int32)[None, None, :]).astype(jnp.int32)
    rank_of_pair = lax.optimization_barrier(jnp.sum((jnp.cumsum(onehot, axis=1) - 1) * onehot, axis=2))
    block_ids = jnp.arange(blocks, dtype=jnp.int32)[:, None]
    pair_slot = ((flat_routes * blocks + block_ids) * CAP + rank_of_pair).reshape(-1).astype(jnp.int32)
    pair_ids = jnp.arange(blocks * SEQ_DEV * TOPK, dtype=jnp.int32)
    slot_pair = jnp.full((EXPERTS * blocks * CAP,), -1, jnp.int32).at[pair_slot].set(pair_ids)
    return (pair_slot, slot_pair.reshape(EXPERTS, blocks * CAP))

def attend(pieces):
    query_nope, query_rope, key_nope, key_rope, values_in, doc_ids = pieces
    score_scale = (DN + DR) ** (-0.5)
    scores = jnp.einsum('thd,shd->hts', query_nope, key_nope, precision=FULL_PRECISION)
    scores = scores + jnp.einsum('thd,sd->hts', query_rope, key_rope, precision=FULL_PRECISION)
    scores = low_back(scores * score_scale)
    places = jnp.arange(SEQ, dtype=jnp.int32)
    allowed = (places[:, None] >= places[None, :]) & (doc_ids[:, None] == doc_ids[None, :])
    scores = jnp.where(allowed[None], scores, -1e+30)
    weights_attn = low(jax.nn.softmax(scores, axis=-1))
    return jnp.einsum('hts,shd->thd', weights_attn, values_in, precision=FULL_PRECISION)

def layer_forward(tokens_f, norm_attn, query_proj, latent_proj, norm_latent, expand_proj, output_proj, norm_ffn, router, shared_gate, shared_up, shared_down, expert_gate, expert_up, expert_down, segments=None, routes=None, pair_slot=None, slot_pair=None):
    groups = tokens_f.shape[0] // SEQ
    places = jnp.tile(jnp.arange(SEQ, dtype=jnp.int32), groups)
    cos_table, sin_table = rope_tables(places)
    normed = low(rms_scale(tokens_f, norm_attn))
    query_all = low_back(matmul(normed, query_proj)).reshape(-1, H, DN + DR)
    query_nope = low(query_all[..., :DN])
    query_rope = low(rotate(query_all[..., DN:], cos_table[:, None, :], sin_table[:, None, :]))
    latent = low_back(matmul(normed, latent_proj))
    latent_norm = low(rms_scale(latent[:, :KVR], norm_latent))
    key_rope = low(rotate(latent[:, KVR:], cos_table, sin_table))
    expanded = low(low_back(matmul(latent_norm, expand_proj))).reshape(-1, H, DN + DV)
    key_nope = expanded[..., :DN]
    values_all = expanded[..., DN:]
    attended = lax.map(jax.checkpoint(attend), (query_nope.reshape(groups, SEQ, H, DN), query_rope.reshape(groups, SEQ, H, DR), key_nope.reshape(groups, SEQ, H, DN), key_rope.reshape(groups, SEQ, DR), values_all.reshape(groups, SEQ, H, DV), segments.reshape(groups, SEQ)))
    attended = low(low_back(attended.reshape(-1, H * DV)))
    hidden = tokens_f + low_back(matmul(attended, output_proj))
    normed_ffn = low(rms_scale(hidden, norm_ffn))
    logits = low_back(matmul(normed_ffn, router))
    chosen = jnp.take_along_axis(jax.nn.sigmoid(logits), routes, axis=1)
    gate_weights = GATE_SCALE * chosen / lax.optimization_barrier(jnp.sum(chosen, axis=1, keepdims=True))
    shared_gate_act = low_back(matmul(normed_ffn, shared_gate))
    shared_up_act = low_back(matmul(normed_ffn, shared_up))
    shared_hidden = low(jax.nn.silu(shared_gate_act) * shared_up_act)
    shared_out = low_back(matmul(shared_hidden, shared_down))

    def expert_rows(pieces):
        slot_index, gate_matrix, up_matrix, down_matrix = pieces
        filled = slot_index >= 0
        source = low_back(jnp.where(filled[:, None], normed_ffn[jnp.maximum(slot_index, 0) // TOPK], 0.0))
        gate_act = low_back(matmul(source, gate_matrix))
        up_act = low_back(matmul(source, up_matrix))
        expert_hidden = low(jax.nn.silu(gate_act) * up_act)
        return low(low_back(matmul(expert_hidden, down_matrix)))
    expert_out = lax.map(jax.checkpoint(expert_rows), (slot_pair, expert_gate, expert_up, expert_down))
    picked = expert_out.reshape(-1, D)[pair_slot].reshape(-1, TOPK, D)
    routed = lax.optimization_barrier(jnp.sum(gate_weights[:, :, None] * picked, axis=1))
    return hidden + shared_out + routed

def reference(tokens, segments, routes, norm_attn, query_proj, latent_proj, norm_latent, expand_proj, output_proj, norm_ffn, router, shared_gate, shared_up, shared_down, expert_gate, expert_up, expert_down, cotangent):
    pair_slot, slot_pair = slot_tables(routes)
    weights = jax.tree.map(lambda array_in: array_in.astype(jnp.float32), (norm_attn, query_proj, latent_proj, norm_latent, expand_proj, output_proj, norm_ffn, router, shared_gate, shared_up, shared_down, expert_gate, expert_up, expert_down))
    forward = partial(layer_forward, segments=segments, routes=routes, pair_slot=pair_slot, slot_pair=slot_pair)
    output, pullback = jax.vjp(forward, tokens.astype(jnp.float32), *weights)
    gradients = pullback(cotangent.astype(jnp.float32))
    return (output.astype(jnp.bfloat16), gradients[0].astype(jnp.bfloat16), gradients[1], gradients[2], gradients[3], gradients[4], gradients[5], gradients[6], gradients[7], gradients[8], gradients[9], gradients[10], gradients[11], gradients[12], gradients[13], gradients[14])
```

```python
import math

import jax
import jax.numpy as jnp
from jax import lax
from jax.sharding import PartitionSpec as P

D = 2048
H = 16
DN = 128
DR = 64
DV = 128
KVR = 512
TOPK = 6
SEQ_DEV = 128

NORM_EPS = 1e-06
ROPE_THETA = 50000.0
GATE_SCALE = 2.446

BF16 = jnp.bfloat16
F32 = jnp.float32
BOTH = ("expert", "fsdp")

ORDER_QUERY = ((8, 4, 2, 1), (8, 1, 2, 4))
ORDER_OUTPUT = (1, 8, 4, 2)
ORDER_EXPAND = (8, 4, 2, 1)
ORDER_LATENT = (4, 8, 2, 1)
ORDER_SMALL = (1, 2, 4, 8)
ORDER_TOKENS = ((1, 8), (8, 1), (4, 2), (2, 4))
BACK_QUERY = ((2, 4, 8, 1), (4, 1, 2, 8))
BACK_OUTPUT = (1, 2, 4, 8)
BACK_EXPAND = (4, 2, 1, 8)
BACK_LATENT = (1, 2, 4, 8)


def rms_scale(values, gain_vec):
    return (
        values * lax.rsqrt(jnp.mean(values * values, axis=-1, keepdims=True) + NORM_EPS) * gain_vec
    )


def rotate(values, cos_table, sin_table):
    middle = values.shape[-1] // 2
    lower_half = values[..., :middle]
    upper_half = values[..., middle:]
    return jnp.concatenate(
        [
            lower_half * cos_table - upper_half * sin_table,
            upper_half * cos_table + lower_half * sin_table,
        ],
        axis=-1,
    )


def rope_tables(positions):
    steps_float = jnp.arange(DR // 2).astype(F32) * (2.0 / DR)
    inverse = jnp.exp(-steps_float * math.log(ROPE_THETA))
    turned = positions.astype(F32)[:, None] * inverse[None, :]
    return (jnp.cos(turned), jnp.sin(turned))


def product(left_side, right_side):
    return jnp.dot(left_side, right_side, preferred_element_type=F32)


def inner_rows(left_side, right_side):
    return lax.dot_general(
        left_side, right_side, (((0,), (0,)), ((), ())), preferred_element_type=F32
    )


def outer_cols(left_side, right_side):
    return lax.dot_general(
        left_side, right_side, (((1,), (1,)), ((), ())), preferred_element_type=F32
    )


def swiglu(gate_act, up_act):
    return jax.nn.silu(gate_act) * up_act


def after(value, *earlier):
    return lax.optimization_barrier((value, *earlier))[0]


class Chips:
    def __init__(self):
        self.n = lax.axis_size("expert")
        self.f = lax.axis_size("fsdp")
        self.chip = lax.axis_index("expert")
        self.core = lax.axis_index("fsdp")

    def bits(self, order):
        return tuple(m for m in order if (m if isinstance(m, int) else m[0]) < self.n)

    def exchange(self, value, mask):
        masks = (mask,) if isinstance(mask, int) else mask
        pairs = [
            (e * self.f + c, (e ^ masks[c % len(masks)]) * self.f + c)
            for e in range(self.n)
            for c in range(self.f)
        ]
        return lax.ppermute(value, BOTH, pairs)

    def other_core(self, value):
        return lax.ppermute(value, "fsdp", [(0, 1), (1, 0)])

    def gather_cores(self, value, axis=0):
        if self.f != 2:
            return lax.all_gather(value, "fsdp", axis=axis, tiled=True)
        other = self.other_core(value)
        first = self.core == 0
        return jnp.concatenate(
            [jnp.where(first, value, other), jnp.where(first, other, value)], axis=axis
        )

    def swap_cores(self, value, split, concat):
        if self.f != 2:
            return lax.all_to_all(value, "fsdp", split_axis=split, concat_axis=concat, tiled=True)
        size = value.shape[split] // 2
        keep = lax.dynamic_slice_in_dim(value, self.core * size, size, split)
        send = lax.dynamic_slice_in_dim(value, (1 - self.core) * size, size, split)
        other = self.other_core(send)
        first = self.core == 0
        return jnp.concatenate(
            [jnp.where(first, keep, other), jnp.where(first, other, keep)], axis=concat
        )

    def sum_cores(self, value):
        if self.f != 2:
            return lax.psum(value, "fsdp")
        return value + self.other_core(value)

    def scatter_cores(self, value):
        if self.f != 2:
            return lax.psum_scatter(value, "fsdp", scatter_dimension=0, tiled=True)
        size = value.shape[0] // 2
        keep = lax.dynamic_slice_in_dim(value, self.core * size, size, 0)
        send = lax.dynamic_slice_in_dim(value, (1 - self.core) * size, size, 0)
        return keep + self.other_core(send)

    def gather_chips(self, value, order):
        done = []
        for mask in self.bits(order):
            other = self.exchange(value, mask)
            place = sum(m > mask for m in done)
            high = (self.chip // mask) % 2 == 1
            value = jnp.stack(
                [jnp.where(high, other, value), jnp.where(high, value, other)], axis=place
            )
            done.append(mask)
        return value.reshape((self.n,) + value.shape[len(done) :])

    def halves(self, value, axis, mask):
        high = (self.chip // mask) % 2
        shape = value.shape
        split = value.reshape(
            shape[:axis] + (self.n // (2 * mask), 2, mask) + shape[axis + 1 :]
        )
        parts = [
            lax.dynamic_index_in_dim(split, bit, axis + 1, keepdims=False).reshape(
                shape[:axis] + (self.n // 2,) + shape[axis + 1 :]
            )
            for bit in (high, 1 - high)
        ]
        return parts

    def scatter_chips(self, value, order, done=()):
        left = [m for m in sorted(self.bits((8, 4, 2, 1)), reverse=True) if m not in done]
        for mask in self.bits(order):
            if mask in done:
                continue
            place = left.index(mask)
            high = (self.chip // mask) % 2
            rest = value.shape[1:]
            split = value.reshape((2,) * len(left) + rest)
            keep = lax.dynamic_index_in_dim(split, high, place, keepdims=False)
            send = lax.dynamic_index_in_dim(split, 1 - high, place, keepdims=False)
            left.remove(mask)
            other = self.exchange(send, mask)
            value = keep.astype(F32) + other.astype(F32)
            if left:
                value = value.astype(send.dtype)
            value = value.reshape((2 ** len(left),) + rest)
        return value[0]

    def weight_grad(self, rows, grads, order):
        mask = self.bits(order)[0]
        keep, send = self.halves(rows, 1, mask)
        count, width = keep.shape[1:]
        tokens = keep.shape[0]
        away = inner_rows(send.reshape(tokens, -1), grads).astype(BF16)
        other = self.exchange(away, mask)
        value = inner_rows(keep.reshape(tokens, -1), grads) + other.astype(F32)
        value = value.astype(BF16).reshape(count, width, -1)
        return self.scatter_chips(value, order, (mask,))

    def gather_tokens(self, value, order):
        order = self.bits(order)
        value = value[None]
        for masks in order[:-1]:
            value = jnp.concatenate([value, self.exchange(value, masks)], axis=0)
        return value, self.exchange(value, order[-1])

    def scatter_tokens(self, value, other, order):
        order = self.bits(order)
        value = value.astype(F32) + other.astype(F32)
        for masks in reversed(order[:-1]):
            half = value.shape[0] // 2
            value = value.astype(other.dtype)
            value = value[:half].astype(F32) + self.exchange(value[half:], masks).astype(F32)
        return value[0]


def body(
    tokens,
    segments,
    routes,
    norm_attn,
    query_proj,
    latent_proj,
    norm_latent,
    expand_proj,
    output_proj,
    norm_ffn,
    router,
    shared_gate,
    shared_up,
    shared_down,
    expert_gate,
    expert_up,
    expert_down,
    cotangent,
):
    chips = Chips()
    n, cores, chip, core = chips.n, chips.f, chips.chip, chips.core
    seq = SEQ_DEV * cores
    heads = H // cores
    shard = D // (n * cores)
    expert_count = n * expert_gate.shape[0]
    small_cut = (shard, 2 * shard, 2 * shard + norm_latent.shape[0])

    small = jnp.concatenate([norm_attn, norm_ffn, norm_latent, router.reshape(-1)])[None]
    small = chips.gather_chips(chips.gather_cores(small), ORDER_SMALL).reshape(n * cores, -1)
    gain_attn = small[:, : small_cut[0]].reshape(-1).astype(F32)
    gain_ffn = small[:, small_cut[0] : small_cut[1]].reshape(-1).astype(F32)
    gain_latent = small[:, small_cut[1] : small_cut[2]].reshape(-1).astype(F32)
    router_all = small[:, small_cut[2] :].reshape(D, -1)

    latent_own = chips.gather_chips(latent_proj, ORDER_LATENT)
    latent_weight = lax.all_gather(latent_own[:, None], "fsdp", axis=1, tiled=True).reshape(D, -1)
    query_own = chips.swap_cores(query_proj, 1, 0)
    query_cut = query_own.shape[1] // 2
    query_parts = [
        chips.gather_chips(part, order).reshape(D, -1)
        for part, order in zip((query_own[:, :query_cut], query_own[:, query_cut:]), ORDER_QUERY)
    ]
    expand_own = chips.swap_cores(expand_proj, 1, 0)
    expand_weight = chips.gather_chips(expand_own, ORDER_EXPAND).reshape(KVR, -1)
    output_own = chips.gather_chips(output_proj, ORDER_OUTPUT)
    output_weight = lax.all_gather(output_own[:, None], "fsdp", axis=1, tiled=True).reshape(-1, D)

    width = shared_gate.shape[1] // n
    shared_in = jnp.stack([shared_gate.reshape(shard, n, -1), shared_up.reshape(shard, n, -1)], 2)
    shared_in = lax.all_to_all(
        shared_in.transpose(1, 0, 2, 3).reshape(n * shard, 2 * width),
        "expert",
        split_axis=0,
        concat_axis=0,
        tiled=True,
    ).reshape(n, 1, shard, 2 * width)
    shared_in = lax.all_gather(shared_in, "fsdp", axis=1, tiled=True).reshape(D, 2 * width)
    shared_down_w = chips.gather_cores(shared_down)
    gate_full = lax.all_gather(expert_gate[0], "fsdp", axis=0, tiled=True)
    up_full = lax.all_gather(expert_up[0], "fsdp", axis=0, tiled=True)
    down_full = lax.all_gather(expert_down[0], "fsdp", axis=0, tiled=True)

    positions = jnp.arange(seq, dtype=jnp.int32)
    cos_table, sin_table = rope_tables(positions)
    inputs_f = tokens.astype(F32)
    normed_own = rms_scale(inputs_f, gain_attn).astype(BF16)
    normed = chips.gather_cores(normed_own)
    query_all = jnp.concatenate([product(normed, part) for part in query_parts], axis=1)
    query_all = query_all.reshape(seq, heads, DN + DR)
    query_nope = query_all[..., :DN].astype(BF16)
    query_rope = rotate(query_all[..., DN:], cos_table[:, None, :], sin_table[:, None, :]).astype(
        BF16
    )
    latent = product(normed, latent_weight)
    latent_norm = rms_scale(latent[:, :KVR], gain_latent).astype(BF16)
    key_rope = rotate(latent[:, KVR:], cos_table, sin_table).astype(BF16)
    expanded = product(latent_norm, expand_weight).astype(BF16).reshape(seq, heads, DN + DV)
    key_nope = expanded[..., :DN]
    values_all = expanded[..., DN:]
    allowed = (positions[:, None] >= positions[None, :]) & (segments[:, None] == segments[None, :])
    score_scale = (DN + DR) ** (-0.5)
    scores = jnp.einsum("thd,shd->hts", query_nope, key_nope, preferred_element_type=F32)
    scores = scores + jnp.einsum("thd,sd->hts", query_rope, key_rope, preferred_element_type=F32)
    scores = jnp.where(allowed[None], scores * score_scale, -1e30)
    shifted = jnp.exp(scores - jnp.max(scores, axis=-1, keepdims=True))
    probs = shifted / jnp.sum(shifted, axis=-1, keepdims=True)
    probs_low = probs.astype(BF16)
    attended = jnp.einsum("hts,shd->thd", probs_low, values_all, preferred_element_type=F32)
    attended = attended.reshape(seq, heads * DV).astype(BF16)
    attended = chips.gather_cores(attended, axis=1)
    attended_own = lax.dynamic_slice_in_dim(attended, core * SEQ_DEV, SEQ_DEV, 0)
    hidden = inputs_f + product(attended_own, output_weight)
    normed_ffn = rms_scale(hidden, gain_ffn).astype(BF16)

    parts = chips.gather_tokens(normed_ffn, ORDER_TOKENS)
    routes_all = jnp.concatenate(chips.gather_tokens(routes, ORDER_TOKENS), axis=0)
    cot_first, cot_last = chips.gather_tokens(cotangent, ORDER_TOKENS)
    logits = product(normed_ffn, router_all)
    route_hot = (
        routes[:, :, None] == jnp.arange(expert_count, dtype=jnp.int32)[None, None, :]
    ).astype(F32)

    def gate_values(logit_in):
        chosen = jnp.sum(route_hot * jax.nn.sigmoid(logit_in)[:, None, :], axis=2)
        return GATE_SCALE * chosen / jnp.sum(chosen, axis=1, keepdims=True)

    gate_weights, gate_pull = jax.vjp(gate_values, logits)
    gate_dense = jnp.sum(route_hot * gate_weights[:, :, None], axis=1)
    gate_all = jnp.concatenate(chips.gather_tokens(gate_dense, ORDER_TOKENS), axis=0)
    gate_here = lax.dynamic_index_in_dim(gate_all, chip, 2, keepdims=False)
    capacity = 2 * SEQ_DEV * TOPK // expert_count
    named = jnp.any(routes_all == chip, axis=2)
    rank = jnp.cumsum(named.astype(jnp.int32), axis=1) - 1
    slot_hot = (
        (rank[:, None, :] == jnp.arange(capacity, dtype=jnp.int32)[None, :, None])
        & named[:, None, :]
    ).astype(BF16)
    half = n // 2

    def pick(hot, rows):
        return (
            jnp.einsum("bct,btd->bcd", hot, rows, preferred_element_type=F32)
            .astype(BF16)
            .reshape(half * capacity, D)
        )

    def place(hot, rows):
        return jnp.einsum(
            "bct,bcd->btd", hot, rows.reshape(half, capacity, D), preferred_element_type=F32
        ).reshape(half * SEQ_DEV, D)

    def forward(rows, cot, hot, gate):
        source = pick(hot, rows)
        cot_slots = pick(hot, cot).astype(F32)
        gate_slots = jnp.sum(hot.astype(F32) * gate[:, None, :], axis=2).reshape(-1, 1)
        gate_act = product(source, gate_full)
        up_act = product(source, up_full)
        hidden_act = swiglu(gate_act, up_act).astype(BF16)
        slots_out = product(hidden_act, down_full).astype(BF16).astype(F32)
        grad_slots = jnp.sum(slots_out * cot_slots, axis=1).reshape(half, capacity, 1)
        grad_gate = jnp.sum(hot.astype(F32) * grad_slots, axis=1)
        flat = rows.reshape(-1, D)
        shared_act = product(flat, shared_in)
        shared_hidden = swiglu(shared_act[:, :width], shared_act[:, width:]).astype(BF16)
        out = place(hot, (slots_out * gate_slots).astype(BF16))
        out = (out + product(shared_hidden, shared_down_w)).astype(BF16)
        cot_flat = cot.reshape(-1, D)
        hidden_back = outer_cols((gate_slots * cot_slots).astype(BF16), down_full)
        shared_back = outer_cols(cot_flat, shared_down_w)
        kept = (
            source, (gate_slots * cot_slots).astype(BF16), gate_act, up_act, hidden_act, flat,
            cot_flat, shared_act, shared_hidden, hidden_back, shared_back,
        )
        return out, grad_gate, kept

    def backward(hot, kept):
        gate_act, up_act, shared_act, hidden_back, shared_back = (kept[i] for i in (2, 3, 7, 9, 10))
        _, pull = jax.vjp(swiglu, gate_act, up_act)
        gate_back, up_back = (v.astype(BF16) for v in pull(hidden_back))
        source_back = outer_cols(gate_back, gate_full) + outer_cols(up_back, up_full)
        _, shared_pull = jax.vjp(swiglu, shared_act[:, :width], shared_act[:, width:])
        acts_back = jnp.concatenate(shared_pull(shared_back), axis=1).astype(BF16)
        back = place(hot, source_back.astype(BF16)) + outer_cols(acts_back, shared_in)
        return back.astype(BF16), gate_back, up_back, acts_back

    out_first, gate_first, kept_first = forward(
        parts[0], cot_first, slot_hot[:half], gate_here[:half]
    )
    out_last, gate_last, kept_last = forward(parts[1], cot_last, slot_hot[half:], gate_here[half:])
    back_last, *acts_last = backward(slot_hot[half:], kept_last)
    sent_back = chips.exchange(back_last, chips.bits(ORDER_TOKENS)[-1])
    back_first, *acts_first = backward(slot_hot[:half], kept_first)
    shape = (half, SEQ_DEV, D)
    ffn_grad = chips.scatter_tokens(
        back_first.reshape(shape), sent_back.reshape(shape), ORDER_TOKENS
    )
    sent_out = chips.exchange(out_last, chips.bits(ORDER_TOKENS)[-1])
    block_sum = chips.scatter_tokens(out_first.reshape(shape), sent_out.reshape(shape), ORDER_TOKENS)
    block_out = (hidden + block_sum).astype(BF16)

    hot_expert = (jnp.arange(expert_count, dtype=jnp.int32) == chip).astype(F32)
    gate_first = gate_first[..., None] * hot_expert
    gate_last = gate_last[..., None] * hot_expert
    gate_sum = chips.scatter_tokens(
        gate_first, chips.exchange(gate_last, chips.bits(ORDER_TOKENS)[-1]), ORDER_TOKENS
    )
    gate_grad = jnp.sum(route_hot * gate_sum[:, None, :], axis=2)
    logit_grad = gate_pull(gate_grad)[0].astype(BF16)
    router_grad = inner_rows(normed_ffn, logit_grad)
    ffn_grad = ffn_grad + outer_cols(logit_grad, router_all)

    def joined(i):
        return jnp.concatenate([kept_first[i], kept_last[i]], axis=0)

    def joined_acts(i):
        return jnp.concatenate([acts_first[i], acts_last[i]], axis=0)

    def expert_grad(rows, grads):
        return lax.psum_scatter(
            inner_rows(rows, grads).astype(BF16), "fsdp", scatter_dimension=0, tiled=True
        ).astype(F32)[None]

    source, slots_grad, hidden_act = joined(0), joined(1), joined(4)
    gate_grad_w = expert_grad(source, joined_acts(0))
    up_grad_w = expert_grad(source, joined_acts(1))
    down_grad_w = expert_grad(hidden_act, slots_grad)
    shared_in_grad = inner_rows(joined(5), joined_acts(2)).astype(BF16)
    shared_in_grad = lax.all_to_all(
        shared_in_grad, BOTH, split_axis=0, concat_axis=0, tiled=True
    ).reshape(n, cores, shard, 2, width)
    shared_in_grad = jnp.sum(shared_in_grad.astype(F32), axis=1).transpose(2, 1, 0, 3)
    shared_in_grad = shared_in_grad.reshape(2, shard, n * width)
    shared_down_grad = chips.scatter_cores(inner_rows(joined(8), joined(6)))

    _, norm_pull = jax.vjp(rms_scale, hidden, gain_ffn)
    hidden_part, gain_ffn_grad = norm_pull(ffn_grad)
    hidden_grad = cotangent.astype(F32) + hidden_part
    attn_grad_own = hidden_grad.astype(BF16)
    attn_grad = chips.gather_cores(attn_grad_own)
    attended_grad = chips.swap_cores(
        outer_cols(attn_grad_own, output_weight).astype(BF16), 1, 0
    ).reshape(seq, heads, DV)
    attended_part = lax.dynamic_index_in_dim(
        attended.reshape(seq, n, cores, shard), core, 2, keepdims=False
    )
    output_grad = chips.weight_grad(attended_part, attn_grad, BACK_OUTPUT)
    prob_grad = jnp.einsum("thd,shd->hts", attended_grad, values_all, preferred_element_type=F32)
    weighted = jnp.sum(probs * prob_grad, axis=-1, keepdims=True)
    score_grad = (probs * (prob_grad - weighted)).astype(BF16)
    query_nope_grad = score_scale * jnp.einsum(
        "hts,shd->thd", score_grad, key_nope, preferred_element_type=F32
    )
    query_rope_grad = score_scale * jnp.einsum(
        "hts,sd->thd", score_grad, key_rope, preferred_element_type=F32
    )
    key_nope_grad = score_scale * jnp.einsum(
        "hts,thd->shd", score_grad, query_nope, preferred_element_type=F32
    )
    key_rope_grad = score_scale * jnp.einsum(
        "hts,thd->sd", score_grad, query_rope, preferred_element_type=F32
    )
    values_grad = jnp.einsum(
        "hts,thd->shd", probs_low, attended_grad, preferred_element_type=F32
    )
    expanded_grad = jnp.concatenate([key_nope_grad, values_grad], axis=2)
    expanded_grad = expanded_grad.reshape(seq, heads * (DN + DV)).astype(BF16)
    latent_back = chips.sum_cores(
        jnp.concatenate([outer_cols(expanded_grad, expand_weight), key_rope_grad], axis=1)
    )
    _, latent_pull = jax.vjp(rms_scale, latent[:, :KVR], gain_latent)
    latent_nope_grad, gain_latent_grad = latent_pull(latent_back[:, :KVR])
    gain_latent_grad = gain_latent_grad / cores
    latent_rope_grad = rotate(latent_back[:, KVR:], cos_table, -sin_table)
    latent_grad = jnp.concatenate([latent_nope_grad, latent_rope_grad], axis=1).astype(BF16)
    query_back = jnp.concatenate(
        [query_nope_grad, rotate(query_rope_grad, cos_table[:, None, :], -sin_table[:, None, :])],
        axis=2,
    )
    query_back = query_back.reshape(seq, heads * (DN + DR)).astype(BF16)

    normed_chips = normed.reshape(seq, n, D // n)
    query_grad = jnp.concatenate(
        [
            chips.weight_grad(normed_chips, part, order)
            for part, order in zip(
                (query_back[:, :query_cut], query_back[:, query_cut:]), BACK_QUERY
            )
        ],
        axis=1,
    )
    query_grad = chips.swap_cores(query_grad, 0, 1)
    expand_grad = chips.weight_grad(latent_norm.reshape(seq, n, KVR // n), expanded_grad, BACK_EXPAND)
    expand_grad = chips.swap_cores(expand_grad, 0, 1)
    normed_part = lax.dynamic_index_in_dim(
        normed.reshape(seq, n, cores, shard), core, 2, keepdims=False
    )
    latent_weight_grad = chips.weight_grad(normed_part, latent_grad, BACK_LATENT)

    normed_grad = outer_cols(query_back[:, :query_cut], query_parts[0]) + outer_cols(
        query_back[:, query_cut:], query_parts[1]
    )
    latent_grad_own = lax.dynamic_slice_in_dim(latent_grad, core * SEQ_DEV, SEQ_DEV, 0)
    normed_grad = chips.scatter_cores(normed_grad) + outer_cols(latent_grad_own, latent_weight)
    _, first_pull = jax.vjp(rms_scale, inputs_f, gain_attn)
    input_part, gain_attn_grad = first_pull(normed_grad)
    tokens_grad = (hidden_grad + input_part).astype(BF16)

    small_grad = jnp.concatenate(
        [
            gain_attn_grad.reshape(n * cores, -1),
            gain_ffn_grad.reshape(n * cores, -1),
            gain_latent_grad.reshape(n * cores, -1),
            router_grad.reshape(n * cores, -1),
        ],
        axis=1,
    )
    small_grad = chips.scatter_chips(small_grad.reshape(n, cores, -1), ORDER_SMALL[::-1])
    small_grad = chips.scatter_cores(small_grad).reshape(-1)
    return (
        block_out,
        tokens_grad,
        small_grad[: small_cut[0]],
        query_grad,
        latent_weight_grad,
        small_grad[small_cut[1] : small_cut[2]],
        expand_grad,
        output_grad,
        small_grad[small_cut[0] : small_cut[1]],
        small_grad[small_cut[2] :].reshape(shard, -1),
        shared_in_grad[0],
        shared_in_grad[1],
        shared_down_grad,
        gate_grad_w,
        up_grad_w,
        down_grad_w,
    )


def solution(mesh):
    rows = P(("expert", "fsdp"), None)
    flat = P(("expert", "fsdp"))
    experts = P("expert", "fsdp", None)
    return jax.shard_map(
        body,
        mesh=mesh,
        in_specs=(
            rows, P("expert"), rows, flat, rows, rows, flat, rows, rows, flat, rows, rows, rows,
            rows, experts, experts, experts, rows,
        ),
        out_specs=(
            rows, rows, flat, rows, rows, flat, rows, rows, flat, rows, rows, rows, rows, experts,
            experts, experts,
        ),
        check_vma=False,
    )
```

```python
import math

import jax
import jax.numpy as jnp
from jax import lax
from jax.experimental import pallas as pl
from jax.experimental.pallas import tpu as pltpu
from jax.sharding import PartitionSpec as P

D = 2048
H = 16
DN = 128
DR = 64
DV = 128
KVR = 512
TOPK = 6
SEQ_DEV = 128

NORM_EPS = 1e-06
ROPE_THETA = 50000.0
GATE_SCALE = 2.446

BF16 = jnp.bfloat16
F32 = jnp.float32
BOTH = ("expert", "fsdp")

ORDER_QUERY = ((8, 4, 1, 2), (8, 2, 4, 1))
ORDER_EXPAND = (8, 1, 2, 4)
ORDER_LATENT = (8, 1, 2, 4)
ORDER_SMALL = (1, 2, 4, 8)
ORDER_OUTPUT = ((8, 1, 4, 2), (8, 2, 1, 4))
TOKEN_GROUPS = (48, 48, 32)
ORDER_TOKENS = ((8, 2, 1, 4), (8, 1, 4, 2), (8, 4, 2, 1))
BACK_QUERY = ((1, 4, 2, 8), (4, 2, 1, 8))
BACK_EXPAND = (2, 1, 4, 8)
BACK_LATENT = (2, 1, 4, 8)
BACK_OUTPUT = ((4, 1, 2, 8), (2, 4, 1, 8))


def rms_scale(values, gain_vec):
    return (
        values * lax.rsqrt(jnp.mean(values * values, axis=-1, keepdims=True) + NORM_EPS) * gain_vec
    )


def rotate(values, cos_table, sin_table):
    middle = values.shape[-1] // 2
    lower_half = values[..., :middle]
    upper_half = values[..., middle:]
    return jnp.concatenate(
        [
            lower_half * cos_table - upper_half * sin_table,
            upper_half * cos_table + lower_half * sin_table,
        ],
        axis=-1,
    )


def rope_tables(positions):
    steps_float = jnp.arange(DR // 2).astype(F32) * (2.0 / DR)
    inverse = jnp.exp(-steps_float * math.log(ROPE_THETA))
    turned = positions.astype(F32)[:, None] * inverse[None, :]
    return (jnp.cos(turned), jnp.sin(turned))


def product(left_side, right_side):
    return jnp.dot(left_side, right_side, preferred_element_type=F32)


def inner_rows(left_side, right_side):
    return lax.dot_general(
        left_side, right_side, (((0,), (0,)), ((), ())), preferred_element_type=F32
    )


def outer_cols(left_side, right_side):
    return lax.dot_general(
        left_side, right_side, (((1,), (1,)), ((), ())), preferred_element_type=F32
    )


def together(*values):
    return lax.optimization_barrier(values)


def swiglu(gate_act, up_act):
    return jax.nn.silu(gate_act) * up_act


WIDE = 512
LANES = 128
VMEM_BYTES = 60 * 2**20


def whole_in_vmem():
    return pl.BlockSpec(memory_space=pltpu.VMEM)


def spans(size):
    return [(start, min(WIDE, size - start)) for start in range(0, size, WIDE)]


def weight_copies(in_hbm, down_hbm, in_refs, down_ref, sems):
    ff = in_hbm[0].shape[1]
    count = 0
    by_span = [[] for _ in spans(down_ref.shape[0])]

    def copy(source, target):
        nonlocal count
        count += 1
        return pltpu.make_async_copy(source, target, sems.at[count - 1])

    for extra, joined in zip(in_hbm[1::2], in_refs):
        by_span[-1].append(copy(extra, joined.at[:, pl.ds(ff, extra.shape[1])]))
    for k, (start, size) in enumerate(spans(ff)):
        for expert, joined in zip(in_hbm[0::2], in_refs):
            there = pl.ds(start, size)
            by_span[k].append(copy(expert.at[:, there], joined.at[:, there]))
    down = [
        copy(down_hbm[0], down_ref.at[pl.ds(0, ff), :]),
        copy(down_hbm[1], down_ref.at[pl.ds(ff, down_hbm[1].shape[0]), :]),
    ]
    return by_span, down


def gated(gate, start, size, ff):
    units = lax.broadcasted_iota(jnp.int32, (1, size), 1) + start
    return jnp.where(units < ff, gate, 1.0)


def row_groups(refs):
    start = 0
    for ref in refs:
        yield ref, pl.ds(start, ref.shape[0])
        start += ref.shape[0]


def forward_kernel(*refs):
    groups = len(TOKEN_GROUPS)
    rows_refs = refs[:groups]
    member_ref, own_ref, gate_w, gate_x, up_w, up_x, down_w, down_x = refs[groups : groups + 8]
    out_refs = refs[groups + 8 : 2 * groups + 8]
    logits_ref, gate_act_ref, up_act_ref, hidden_ref = refs[2 * groups + 8 : 2 * groups + 12]
    gate_all, up_all, down_all, sems = refs[2 * groups + 12 :]
    by_span, down = weight_copies(
        (gate_w, gate_x, up_w, up_x), (down_w, down_x), (gate_all, up_all), down_all, sems
    )
    for copy in by_span[-1] + sum(by_span[:-1], []) + down:
        copy.start()
    ff, units = gate_w.shape[1], down_all.shape[0]
    width = down_all.shape[1]
    order = list(zip(spans(units), by_span))
    order = order[-1:] + order[:-1]
    for rows_ref, here in row_groups(rows_refs):
        first = here.start == 0
        for k, ((start, size), copies) in enumerate(order):
            there = pl.ds(start, size)
            if first:
                for copy in copies:
                    copy.wait()
            gate_act = product(rows_ref[...], gate_all[:, there])
            up_act = product(rows_ref[...], up_all[:, there])
            if k == 0:
                logits_ref[here, :] = gate_act
                chosen = member_ref[here, :] / (1.0 + jnp.exp(-gate_act))
                own = jnp.sum(chosen * own_ref[...], axis=1, keepdims=True)
                gate = GATE_SCALE * own / jnp.sum(chosen, axis=1, keepdims=True)
            gate_act_ref[here, there] = gate_act.astype(BF16)
            up_act_ref[here, there] = up_act.astype(BF16)
            hidden = swiglu(gate_act, up_act) * gated(gate, start, size, ff)
            hidden_ref[here, there] = hidden.astype(BF16)
    for copy in down:
        copy.wait()
    for out_ref, here in row_groups(out_refs):
        for start, size in spans(width):
            there = pl.ds(start, size)
            out_ref[:, there] = product(hidden_ref[here, :], down_all[:, there]).astype(BF16)


def backward_kernel(*refs):
    groups = len(TOKEN_GROUPS)
    cot_refs = refs[:groups]
    member_ref, own_ref, logits_ref, gate_act_ref, up_act_ref = refs[groups : groups + 5]
    gate_w, gate_x, up_w, up_x, down_w, down_x = refs[groups + 5 : groups + 11]
    back_refs = refs[groups + 11 : 2 * groups + 11]
    gate_back_ref, up_back_ref, gate_all, up_all, down_all, sems = refs[2 * groups + 11 :]
    by_span, down = weight_copies(
        (gate_w, gate_x, up_w, up_x), (down_w, down_x), (gate_all, up_all), down_all, sems
    )
    for copy in down + sum(by_span, []):
        copy.start()
    ff, units = gate_w.shape[1], down_all.shape[0]
    width = down_all.shape[1]
    for copy in down:
        copy.wait()
    for cot_ref, here in row_groups(cot_refs):
        sigmoid = 1.0 / (1.0 + jnp.exp(-logits_ref[here, :]))
        chosen = member_ref[here, :] * sigmoid
        own = jnp.sum(chosen * own_ref[...], axis=1, keepdims=True)
        all_chosen = jnp.sum(chosen, axis=1, keepdims=True)
        gate = GATE_SCALE * own / all_chosen
        gate_grad = jnp.zeros_like(gate)
        for start, size in spans(units):
            there = pl.ds(start, size)
            last = start + size == units
            hidden_back = outer_cols(cot_ref[...], down_all[there, :])
            gate_act = gate_act_ref[here, there].astype(F32)
            up_act = up_act_ref[here, there].astype(F32)
            sig = 1.0 / (1.0 + jnp.exp(-gate_act))
            silu = gate_act * sig
            column = lax.broadcasted_iota(jnp.int32, (1, size), 1) + start
            term = jnp.where(column < ff, silu * up_act * hidden_back, 0.0)
            gate_grad = gate_grad + jnp.sum(term, axis=1, keepdims=True)
            scaled = hidden_back * gated(gate, start, size, ff)
            up_back_ref[here, there] = (scaled * silu).astype(BF16)
            gate_back = scaled * up_act * (sig + silu * (1.0 - sig))
            if last:
                named = jnp.sum(member_ref[here, :] * own_ref[...], axis=1, keepdims=True)
                logit_back = GATE_SCALE * named * gate_grad * chosen * (1.0 - sigmoid)
                logit_back = logit_back * (own_ref[...] - own / all_chosen) / all_chosen
                gate_back = jnp.where(member_ref[here, :] > 0.0, logit_back, gate_back)
            gate_back_ref[here, there] = gate_back.astype(BF16)
    for copy in sum(by_span, []):
        copy.wait()
    for back_ref, here in row_groups(back_refs):
        for start, size in spans(width):
            there = pl.ds(start, size)
            back = outer_cols(gate_back_ref[here, :], gate_all[there, :])
            back = back + outer_cols(up_back_ref[here, :], up_all[there, :])
            back_ref[:, there] = back.astype(BF16)


def expert_call(kernel, out_shapes, arrays, weights):
    width, ff = weights[0].shape
    units = ff + weights[1].shape[1]
    tokens = sum(rows.shape[0] for rows in arrays[: len(TOKEN_GROUPS)])
    return pl.pallas_call(
        kernel,
        out_shape=out_shapes,
        in_specs=[whole_in_vmem() for _ in arrays]
        + [pl.BlockSpec(memory_space=pl.ANY) for _ in weights],
        out_specs=[whole_in_vmem() for _ in out_shapes],
        scratch_shapes=[
            pltpu.VMEM((width, units), BF16),
            pltpu.VMEM((width, units), BF16),
            pltpu.VMEM((units, width), BF16),
            pltpu.SemaphoreType.DMA((2 * len(spans(ff)) + 4,)),
        ],
        compiler_params=pltpu.CompilerParams(vmem_limit_bytes=VMEM_BYTES),
        cost_estimate=pl.CostEstimate(
            flops=6 * tokens * width * units,
            bytes_accessed=6 * width * units + 12 * tokens * width,
            transcendentals=tokens * units,
        ),
    )(*arrays, *weights)


def expert_forward(rows, member, own, weights):
    tokens = member.shape[0]
    units = weights[0].shape[1] + weights[1].shape[1]
    shapes = [jax.ShapeDtypeStruct(v.shape, BF16) for v in rows]
    shapes.append(jax.ShapeDtypeStruct(member.shape, F32))
    shapes += [jax.ShapeDtypeStruct((tokens, units), BF16)] * 3
    results = expert_call(forward_kernel, shapes, (*rows, member, own), weights)
    return results[: len(rows)], results[len(rows) :]


def expert_backward(cot, member, own, logits, gate_act, up_act, weights):
    shapes = [jax.ShapeDtypeStruct(v.shape, BF16) for v in cot]
    shapes += [jax.ShapeDtypeStruct(gate_act.shape, BF16)] * 2
    results = expert_call(
        backward_kernel, shapes, (*cot, member, own, logits, gate_act, up_act), weights
    )
    return results[: len(cot)], results[len(cot) :]


def in_weights_kernel(*refs):
    groups = 2 * len(TOKEN_GROUPS)
    rows, grads, outs = refs[:groups], refs[groups : groups + 4], refs[groups + 4 : groups + 8]
    turned = refs[-1]
    for ref, here in row_groups(rows):
        turned[:, here] = ref[...].T
    tokens = grads[0].shape[0]
    ff = outs[0].shape[1]
    for first, last, joined in ((grads[0], grads[1], outs[:2]), (grads[2], grads[3], outs[2:])):
        for out, begin in zip(joined, (0, ff)):
            for start, size in spans(out.shape[1]):
                there = pl.ds(begin + start, size)
                value = product(turned[:, pl.ds(0, tokens)], first[:, there])
                value = value + product(turned[:, pl.ds(tokens, tokens)], last[:, there])
                out[:, pl.ds(start, size)] = value.astype(out.dtype)


def in_weights(rows, gate_back, up_back, ff):
    tokens, units = gate_back[0].shape
    width = rows[0].shape[1]
    whole = pl.BlockSpec((tokens, units), lambda i: (0, 0), pipeline_mode=pl.Buffered(1))
    outs = [((width, ff), BF16), ((width, units - ff), F32)] * 2
    return pl.pallas_call(
        in_weights_kernel,
        grid=(width // WIDE,),
        out_shape=[jax.ShapeDtypeStruct(*out) for out in outs],
        in_specs=[pl.BlockSpec((v.shape[0], WIDE), lambda i: (0, i)) for v in rows] + [whole] * 4,
        out_specs=[pl.BlockSpec((WIDE, shape[1]), lambda i: (i, 0)) for shape, _ in outs],
        scratch_shapes=[pltpu.VMEM((WIDE, 2 * tokens), BF16)],
        compiler_params=pltpu.CompilerParams(vmem_limit_bytes=VMEM_BYTES),
        cost_estimate=pl.CostEstimate(
            flops=8 * tokens * width * units,
            bytes_accessed=4 * tokens * (width + 2 * units) + 4 * width * units,
            transcendentals=0,
        ),
    )(*rows, *gate_back, *up_back)


def down_weights_kernel(hidden_first, hidden_last, *refs):
    groups = 2 * len(TOKEN_GROUPS)
    cot, (out, extra_out), turned = refs[:groups], refs[groups : groups + 2], refs[-1]
    tokens = hidden_first.shape[0]

    @pl.when(pl.program_id(0) == 0)
    def _():
        turned[:, pl.ds(0, tokens)] = hidden_first[...].T
        turned[:, pl.ds(tokens, tokens)] = hidden_last[...].T

    for ref, begin in ((out, 0), (extra_out, out.shape[0])):
        for start, size in spans(ref.shape[0]):
            there = pl.ds(begin + start, size)
            value = sum(product(turned[there, here], group[...]) for group, here in row_groups(cot))
            ref[pl.ds(start, size), :] = value.astype(ref.dtype)


def down_weights(hidden, cot, ff):
    tokens, units = hidden[0].shape
    width = cot[0].shape[1]
    whole = pl.BlockSpec((tokens, units), lambda i: (0, 0), pipeline_mode=pl.Buffered(1))
    outs = [((ff, width), BF16), ((units - ff, width), F32)]
    return pl.pallas_call(
        down_weights_kernel,
        grid=(width // WIDE,),
        out_shape=[jax.ShapeDtypeStruct(*out) for out in outs],
        in_specs=[whole] * 2 + [pl.BlockSpec((v.shape[0], WIDE), lambda i: (0, i)) for v in cot],
        out_specs=[pl.BlockSpec((shape[0], WIDE), lambda i: (0, i)) for shape, _ in outs],
        scratch_shapes=[pltpu.VMEM((units, 2 * tokens), BF16)],
        compiler_params=pltpu.CompilerParams(vmem_limit_bytes=VMEM_BYTES),
        cost_estimate=pl.CostEstimate(
            flops=4 * tokens * width * units,
            bytes_accessed=4 * tokens * (width + units) + 2 * width * units,
            transcendentals=0,
        ),
    )(*hidden, *cot)


class Chips:
    def __init__(self):
        self.n = lax.axis_size("expert")
        self.f = lax.axis_size("fsdp")
        self.chip = lax.axis_index("expert")
        self.core = lax.axis_index("fsdp")

    def bits(self, order):
        return tuple(m for m in order if (m if isinstance(m, int) else m[0]) < self.n)

    def exchange(self, value, mask):
        masks = (mask,) if isinstance(mask, int) else mask
        pairs = [
            (e * self.f + c, (e ^ masks[c % len(masks)]) * self.f + c)
            for e in range(self.n)
            for c in range(self.f)
        ]
        return lax.ppermute(value, BOTH, pairs)

    def other_core(self, value):
        return lax.ppermute(value, "fsdp", [(0, 1), (1, 0)])

    def gather_cores(self, value, axis=0):
        if self.f != 2:
            return lax.all_gather(value, "fsdp", axis=axis, tiled=True)
        other = self.other_core(value)
        first = self.core == 0
        return jnp.concatenate(
            [jnp.where(first, value, other), jnp.where(first, other, value)], axis=axis
        )

    def swap_cores(self, value, split, concat):
        if self.f != 2:
            return lax.all_to_all(value, "fsdp", split_axis=split, concat_axis=concat, tiled=True)
        size = value.shape[split] // 2
        first = self.core == 0
        low = lax.slice_in_dim(value, 0, size, axis=split)
        high = lax.slice_in_dim(value, size, 2 * size, axis=split)
        keep = jnp.where(first, low, high)
        other = self.other_core(jnp.where(first, high, low))
        return jnp.concatenate(
            [jnp.where(first, keep, other), jnp.where(first, other, keep)], axis=concat
        )

    def sum_cores(self, value):
        if self.f != 2:
            return lax.psum(value, "fsdp")
        return value + self.other_core(value)

    def scatter_cores(self, value, axis=0):
        if self.f != 2:
            return lax.psum_scatter(value, "fsdp", scatter_dimension=axis, tiled=True)
        size = value.shape[axis] // 2
        first = self.core == 0
        low = lax.slice_in_dim(value, 0, size, axis=axis)
        high = lax.slice_in_dim(value, size, 2 * size, axis=axis)
        return jnp.where(first, low, high) + self.other_core(jnp.where(first, high, low))

    def lockstep(self, *streams):
        results = [None] * len(streams)
        waiting = {}

        def advance(i, other):
            try:
                waiting[i] = streams[i].send(other)
            except StopIteration as stop:
                waiting.pop(i, None)
                results[i] = stop.value

        for i in range(len(streams)):
            advance(i, None)
        while waiting:
            names = list(waiting)
            over = [i for i in range(len(streams)) if i not in waiting]
            values, kept = together([waiting[i][0] for i in names], [results[i] for i in over])
            for i, result in zip(over, kept):
                results[i] = result
            masks = [waiting[i][1] for i in names]
            others = [v if m is None else self.exchange(v, m) for v, m in zip(values, masks)]
            for i, other in zip(names, others):
                advance(i, other)
        return together(*results)

    def gather_chips(self, value, order):
        done = []
        for mask in self.bits(order):
            other = yield value, mask
            place = sum(m > mask for m in done)
            high = (self.chip // mask) % 2 == 1
            value = jnp.stack(
                [jnp.where(high, other, value), jnp.where(high, value, other)], axis=place
            )
            done.append(mask)
        return value.reshape((self.n,) + value.shape[len(done) :])

    def halves(self, value, mask, width):
        high = (self.chip // mask) % 2 == 1
        run = mask * width
        low_runs = [value[:, i : i + run] for i in range(0, self.n * width, 2 * run)]
        high_runs = [value[:, i : i + run] for i in range(run, self.n * width, 2 * run)]
        pairs = list(zip(low_runs, high_runs))
        keep = [jnp.where(high, h, l) for l, h in pairs]
        send = [jnp.where(high, l, h) for l, h in pairs]
        return jnp.concatenate(keep, axis=1), jnp.concatenate(send, axis=1)

    def scatter_chips(self, value, order, done=()):
        left = [m for m in sorted(self.bits((8, 4, 2, 1)), reverse=True) if m not in done]
        for mask in self.bits(order):
            if mask in done:
                continue
            place = left.index(mask)
            high = (self.chip // mask) % 2
            rest = value.shape[1:]
            split = value.reshape((2,) * len(left) + rest)
            keep = lax.dynamic_index_in_dim(split, high, place, keepdims=False)
            send = lax.dynamic_index_in_dim(split, 1 - high, place, keepdims=False)
            left.remove(mask)
            other = yield send, mask
            value = keep.astype(F32) + other.astype(F32)
            if left:
                value = value.astype(send.dtype)
            value = value.reshape((2 ** len(left),) + rest)
        return value[0]

    def weight_grad(self, rows, grads, order):
        mask = self.bits(order)[0]
        width = rows.shape[1] // self.n
        keep, send = self.halves(rows, mask, width)
        away = inner_rows(send, grads).astype(BF16)
        other = yield away, mask
        value = inner_rows(keep, grads) + other.astype(F32)
        value = value.astype(BF16).reshape(self.n // 2, width, -1)
        return (yield from self.scatter_chips(value, order, (mask,)))

    def gather_groups(self, value, idle=0):
        start = 0
        for size, order in zip(TOKEN_GROUPS, ORDER_TOKENS):
            yield self.gather_tokens(value[start : start + size], order, idle)
            start += size

    def gather_tokens(self, value, order, idle):
        for _ in range(idle):
            yield (), None
        value = value[None]
        for mask in self.bits(order)[:-1]:
            other = yield value, mask
            value = jnp.concatenate([value, other], axis=0)
        return value

    def last_groups(self, groups):
        for value, order in zip(groups, ORDER_TOKENS):
            yield self.last_exchange(value, self.bits(order)[-1])

    def last_exchange(self, value, mask):
        return (yield value, mask)

    def scatter_groups(self, groups, others):
        for value, other, order in zip(groups, others, ORDER_TOKENS):
            yield self.scatter_tokens(value, other, order)

    def scatter_tokens(self, value, other, order):
        order = self.bits(order)
        value = value.astype(F32) + other.astype(F32)
        for masks in reversed(order[:-1]):
            half = value.shape[0] // 2
            value = value.astype(other.dtype)
            received = yield value[half:], masks
            value = value[:half].astype(F32) + received.astype(F32)
        return value[0]


def body(
    tokens,
    segments,
    routes,
    norm_attn,
    query_proj,
    latent_proj,
    norm_latent,
    expand_proj,
    output_proj,
    norm_ffn,
    router,
    shared_gate,
    shared_up,
    shared_down,
    expert_gate,
    expert_up,
    expert_down,
    cotangent,
):
    chips = Chips()
    n, cores, chip, core = chips.n, chips.f, chips.chip, chips.core
    seq = SEQ_DEV * cores
    heads = H // cores
    shard = D // (n * cores)
    expert_count = n * expert_gate.shape[0]
    small_cut = (shard, 2 * shard, 2 * shard + norm_latent.shape[0])

    small = jnp.concatenate([norm_attn, norm_ffn, norm_latent, router.reshape(-1)])[None]
    query_own = chips.swap_cores(query_proj, 1, 0)
    query_cut = query_own.shape[1] // 2
    expand_own = chips.swap_cores(expand_proj, 1, 0)
    width = shared_gate.shape[1] // n

    def shared_weights():
        weights = (shared_gate, shared_up)
        for _ in range(4):
            weights = yield weights, None
        shared_gate_in, shared_up_in = weights
        shared_in = jnp.stack(
            [shared_gate_in.reshape(shard, n, -1), shared_up_in.reshape(shard, n, -1)], 2
        )
        shared_in = lax.all_to_all(
            shared_in.transpose(1, 0, 2, 3).reshape(n * shard, 2 * width),
            "expert",
            split_axis=0,
            concat_axis=0,
            tiled=True,
        ).reshape(n, 1, shard, 2 * width)
        return shared_in

    small, query_first, query_last, expand_weight, latent_own, routes_all, shared_in = chips.lockstep(
        chips.gather_chips(chips.gather_cores(small), ORDER_SMALL),
        chips.gather_chips(query_own[:, :query_cut], ORDER_QUERY[0]),
        chips.gather_chips(query_own[:, query_cut:], ORDER_QUERY[1]),
        chips.gather_chips(expand_own, ORDER_EXPAND),
        chips.gather_chips(latent_proj, ORDER_LATENT),
        chips.gather_chips(routes, ORDER_SMALL),
        shared_weights(),
    )
    shared_in = lax.all_gather(shared_in, "fsdp", axis=1, tiled=True).reshape(D, 2 * width)
    output_own = chips.swap_cores(output_proj, 1, 0)
    output_cut = output_own.shape[1] // 2
    small, query_first, query_last, expand_weight, latent_own, output_own, cot_in, routes_all = together(
        small, query_first, query_last, expand_weight, latent_own, output_own, cotangent, routes_all
    )
    small = small.reshape(n * cores, -1)
    gain_attn = small[:, : small_cut[0]].reshape(-1).astype(F32)
    gain_ffn = small[:, small_cut[0] : small_cut[1]].reshape(-1).astype(F32)
    gain_latent = small[:, small_cut[1] : small_cut[2]].reshape(-1).astype(F32)
    router_all = small[:, small_cut[2] :].reshape(D, -1)
    extra = -(-(width + expert_count) // LANES) * LANES
    router_at = extra - LANES
    gate_extra = jnp.concatenate([shared_in[:, :width], router_all], axis=1)
    gate_extra = jnp.pad(gate_extra, ((0, 0), (0, extra - width - expert_count)))
    up_extra = jnp.pad(shared_in[:, width:], ((0, 0), (0, extra - width)))
    member_pad = (width - router_at, extra - width - expert_count)
    query_parts = [query_first.reshape(D, -1), query_last.reshape(D, -1)]
    expand_weight = expand_weight.reshape(KVR, -1)
    latent_weight = chips.gather_cores(latent_own[:, None], axis=1).reshape(D, -1)
    down_extra = jnp.pad(chips.gather_cores(shared_down), ((0, extra - width), (0, 0)))
    gate_full, up_full, down_full = (
        lax.all_gather(w[0], "fsdp", axis=0, tiled=True)
        for w in (expert_gate, expert_up, expert_down)
    )
    weights = (gate_full, gate_extra, up_full, up_extra, down_full, down_extra)
    ff = gate_full.shape[1]

    positions = jnp.arange(seq, dtype=jnp.int32)
    cos_table, sin_table = rope_tables(positions)
    inputs_f = tokens.astype(F32)
    score_scale = (DN + DR) ** (-0.5)

    def attention():
        yield (), None
        normed_own = rms_scale(inputs_f, gain_attn).astype(BF16)
        normed = chips.gather_cores(normed_own)
        latent = product(normed, latent_weight)
        query_all = jnp.concatenate([product(normed, part) for part in query_parts], axis=1)
        query_all = query_all.reshape(seq, heads, DN + DR)
        query_nope = query_all[..., :DN].astype(BF16)
        query_rope = rotate(
            query_all[..., DN:], cos_table[:, None, :], sin_table[:, None, :]
        ).astype(BF16)
        normed, latent, query_nope, query_rope = yield (
            (normed, latent, query_nope, query_rope),
            None,
        )
        latent_norm = rms_scale(latent[:, :KVR], gain_latent).astype(BF16)
        key_rope = rotate(latent[:, KVR:], cos_table, sin_table).astype(BF16)
        expanded = product(latent_norm, expand_weight).astype(BF16).reshape(seq, heads, DN + DV)
        key_nope = expanded[..., :DN]
        values_all = expanded[..., DN:]
        allowed = (positions[:, None] >= positions[None, :]) & (
            segments[:, None] == segments[None, :]
        )
        scores = jnp.einsum("thd,shd->hts", query_nope, key_nope, preferred_element_type=F32)
        scores = scores + jnp.einsum(
            "thd,sd->hts", query_rope, key_rope, preferred_element_type=F32
        )
        scores = jnp.where(allowed[None], scores * score_scale, -1e30)
        shifted = jnp.exp(scores - jnp.max(scores, axis=-1, keepdims=True))
        probs = shifted / jnp.sum(shifted, axis=-1, keepdims=True)
        latent_norm, key_rope, key_nope, values_all, probs = yield (
            (latent_norm, key_rope, key_nope, values_all, probs),
            None,
        )
        probs_low = probs.astype(BF16)
        attended = jnp.einsum("hts,shd->thd", probs_low, values_all, preferred_element_type=F32)
        attended = attended.reshape(seq, heads * DV).astype(BF16)
        attended = yield chips.gather_cores(attended, axis=1), None
        return (
            normed, latent, query_nope, query_rope, latent_norm, key_rope, key_nope, values_all,
            probs, probs_low, attended,
        )

    output_first, output_last, *cot_first, kept_attention = chips.lockstep(
        chips.gather_chips(output_own[:, :output_cut], ORDER_OUTPUT[0]),
        chips.gather_chips(output_own[:, output_cut:], ORDER_OUTPUT[1]),
        *chips.gather_groups(cot_in, idle=1),
        attention(),
    )
    (
        normed, latent, query_nope, query_rope, latent_norm, key_rope, key_nope, values_all,
        probs, probs_low, attended,
    ) = kept_attention
    output_parts = [output_first.reshape(D, -1), output_last.reshape(D, -1)]
    hidden = jnp.concatenate([product(attended, part) for part in output_parts], axis=1)
    hidden = inputs_f + chips.swap_cores(hidden, 0, 1)
    normed_ffn = rms_scale(hidden, gain_ffn).astype(BF16)

    half = n // 2

    def here_and_there(blocks):
        halves = []
        for last in (False, True):
            parts, start = [], 0
            for size, order in zip(TOKEN_GROUPS, ORDER_TOKENS):
                order = chips.bits(order)
                turns = [0]
                for mask in order[:-1]:
                    turns = turns + [t ^ mask for t in turns]
                turns = jnp.array([t ^ order[-1] if last else t for t in turns], jnp.int32)
                rows = jnp.take(blocks, chip ^ turns, axis=0)[:, start : start + size]
                parts.append(rows.reshape((half * size,) + rows.shape[2:]))
                start += size
            halves.append(jnp.concatenate(parts, axis=0))
        return halves

    members = []
    for routes_half in here_and_there(routes_all):
        member = jnp.any(
            routes_half[:, :, None] == jnp.arange(expert_count, dtype=jnp.int32), axis=1
        )
        members.append(jnp.pad(member.astype(F32), ((0, 0), member_pad)))
    own = (jnp.arange(expert_count, dtype=jnp.int32) == chip).astype(F32)
    own = jnp.pad(own, member_pad)[None]

    def flat(groups):
        return [v.reshape(-1, D) for v in groups]

    def blocks(groups):
        return [v.reshape(half, -1, D) for v in groups]

    def forward(groups, member):
        rows = flat(groups)
        out, (logits, gate_act, up_act, hidden_act) = expert_forward(rows, member, own, weights)
        return blocks(out), (rows, logits, gate_act, up_act, hidden_act)

    def backward(kept, groups, member):
        _, logits, gate_act, up_act, _ = kept
        cot = flat(groups)
        back, (gate_back, up_back) = expert_backward(
            cot, member, own, logits, gate_act, up_act, weights
        )
        return blocks(back), (cot, gate_back, up_back)

    def beside(function, *values):
        values = yield values, None
        return function(*values)

    rows_first = chips.lockstep(*chips.gather_groups(normed_ffn))
    *rows_last, (out_first, kept_first) = chips.lockstep(
        *chips.last_groups(rows_first), beside(forward, rows_first, members[0])
    )
    cot_first, rows_last = together(cot_first, rows_last)
    *cot_last, (out_last, kept_last) = chips.lockstep(
        *chips.last_groups(cot_first), beside(forward, rows_last, members[1])
    )
    *sent_out, (back_last, grads_last) = chips.lockstep(
        *chips.last_groups(out_last), beside(backward, kept_last, cot_last, members[1])
    )
    *sent_back, (back_first, grads_first) = chips.lockstep(
        *chips.last_groups(back_last), beside(backward, kept_first, cot_first, members[0])
    )

    def expert_grads(kept, grads):
        kept, grads = yield (kept, grads), None
        gate_w, gate_extra_w, up_w, up_extra_w = in_weights(
            [v for half_rows in kept for v in half_rows[0]],
            [half_grads[1] for half_grads in grads],
            [half_grads[2] for half_grads in grads],
            ff,
        )
        gate_w, gate_extra_w, up_w, up_extra_w, kept, grads = yield (
            (gate_w, gate_extra_w, up_w, up_extra_w, kept, grads),
            None,
        )
        down_w, down_extra_w = down_weights(
            [half_rows[4] for half_rows in kept], [v for half_grads in grads for v in half_grads[0]], ff
        )
        return gate_w, up_w, down_w, gate_extra_w, up_extra_w, down_extra_w

    *ffn_grad, expert_w = chips.lockstep(
        *chips.scatter_groups(back_first, sent_back),
        expert_grads((kept_first, kept_last), (grads_first, grads_last)),
    )
    ffn_grad = jnp.concatenate(ffn_grad, axis=0)
    gate_grad_w, up_grad_w, down_grad_w = (
        lax.psum_scatter(v, "fsdp", scatter_dimension=0, tiled=True).astype(F32)[None]
        for v in expert_w[:3]
    )
    gate_extra_w, up_extra_w, down_extra_w = expert_w[3:]
    router_grad = gate_extra_w[:, width : width + expert_count]
    shared_in_grad = jnp.concatenate([gate_extra_w[:, :width], up_extra_w[:, :width]], axis=1)
    shared_in_grad = chips.scatter_cores(shared_in_grad.reshape(n, cores * shard, 2 * width), 1)
    shared_in_grad = lax.all_to_all(
        shared_in_grad.astype(BF16), "expert", split_axis=0, concat_axis=0, tiled=True
    )
    shared_in_grad = shared_in_grad.astype(F32).reshape(n, shard, 2, width).transpose(2, 1, 0, 3)
    shared_in_grad = shared_in_grad.reshape(2, shard, n * width)
    shared_down_grad = chips.scatter_cores(down_extra_w[:width])

    _, norm_pull = jax.vjp(rms_scale, hidden, gain_ffn)
    hidden_part, gain_ffn_grad = norm_pull(ffn_grad)
    hidden_grad = cotangent.astype(F32) + hidden_part
    hidden_grad, out_first, sent_out = together(hidden_grad, out_first, sent_out)
    attn_grad_own = hidden_grad.astype(BF16)
    attn_grad = chips.swap_cores(attn_grad_own, 1, 0)

    def attention_back():
        yield (), None
        attended_grad = outer_cols(attn_grad[:, :output_cut], output_parts[0]) + outer_cols(
            attn_grad[:, output_cut:], output_parts[1]
        )
        attended_grad = chips.scatter_cores(attended_grad, 1).astype(BF16)
        attended_grad = attended_grad.reshape(seq, heads, DV)
        prob_grad = jnp.einsum("thd,shd->hts", attended_grad, values_all, preferred_element_type=F32)
        weighted = jnp.sum(probs * prob_grad, axis=-1, keepdims=True)
        score_grad = (probs * (prob_grad - weighted)).astype(BF16)
        query_nope_grad = score_scale * jnp.einsum(
            "hts,shd->thd", score_grad, key_nope, preferred_element_type=F32
        )
        query_rope_grad = score_scale * jnp.einsum(
            "hts,sd->thd", score_grad, key_rope, preferred_element_type=F32
        )
        key_nope_grad = score_scale * jnp.einsum(
            "hts,thd->shd", score_grad, query_nope, preferred_element_type=F32
        )
        key_rope_grad = score_scale * jnp.einsum(
            "hts,thd->sd", score_grad, query_rope, preferred_element_type=F32
        )
        values_grad = jnp.einsum(
            "hts,thd->shd", probs_low, attended_grad, preferred_element_type=F32
        )
        (query_nope_grad, query_rope_grad, key_nope_grad, key_rope_grad, values_grad) = yield (
            (query_nope_grad, query_rope_grad, key_nope_grad, key_rope_grad, values_grad),
            None,
        )
        expanded_grad = jnp.concatenate([key_nope_grad, values_grad], axis=2)
        expanded_grad = expanded_grad.reshape(seq, heads * (DN + DV)).astype(BF16)
        latent_back = chips.sum_cores(
            jnp.concatenate([outer_cols(expanded_grad, expand_weight), key_rope_grad], axis=1)
        )
        _, latent_pull = jax.vjp(rms_scale, latent[:, :KVR], gain_latent)
        latent_nope_grad, gain_latent_grad = latent_pull(latent_back[:, :KVR])
        gain_latent_grad = gain_latent_grad / cores
        latent_rope_grad = rotate(latent_back[:, KVR:], cos_table, -sin_table)
        latent_grad = jnp.concatenate([latent_nope_grad, latent_rope_grad], axis=1).astype(BF16)
        query_back = jnp.concatenate(
            [query_nope_grad, rotate(query_rope_grad, cos_table[:, None, :], -sin_table[:, None, :])],
            axis=2,
        )
        query_back = query_back.reshape(seq, heads * (DN + DR)).astype(BF16)
        query_back, expanded_grad, latent_grad, gain_latent_grad = yield (
            (query_back, expanded_grad, latent_grad, gain_latent_grad),
            None,
        )
        return query_back, expanded_grad, latent_grad, gain_latent_grad

    output_first_grad, output_last_grad, *block_sum, kept_back = chips.lockstep(
        chips.weight_grad(attended, attn_grad[:, :output_cut], BACK_OUTPUT[0]),
        chips.weight_grad(attended, attn_grad[:, output_cut:], BACK_OUTPUT[1]),
        *chips.scatter_groups(out_first, sent_out),
        attention_back(),
    )
    query_back, expanded_grad, latent_grad, gain_latent_grad = kept_back
    output_grad = jnp.concatenate([output_first_grad, output_last_grad], axis=1)
    output_grad = chips.swap_cores(output_grad, 0, 1)

    normed_part = lax.dynamic_index_in_dim(
        normed.reshape(seq, n, cores, shard), core, 2, keepdims=False
    ).reshape(seq, n * shard)
    query_first_grad, query_last_grad, expand_grad, latent_weight_grad = chips.lockstep(
        chips.weight_grad(normed, query_back[:, :query_cut], BACK_QUERY[0]),
        chips.weight_grad(normed, query_back[:, query_cut:], BACK_QUERY[1]),
        chips.weight_grad(latent_norm, expanded_grad, BACK_EXPAND),
        chips.weight_grad(normed_part, latent_grad, BACK_LATENT),
    )
    query_grad = jnp.concatenate([query_first_grad, query_last_grad], axis=1)
    query_grad = chips.swap_cores(query_grad, 0, 1)
    expand_grad = chips.swap_cores(expand_grad, 0, 1)

    normed_grad = outer_cols(query_back[:, :query_cut], query_parts[0]) + outer_cols(
        query_back[:, query_cut:], query_parts[1]
    )
    latent_grad_own = lax.dynamic_slice_in_dim(latent_grad, core * SEQ_DEV, SEQ_DEV, 0)
    normed_grad = chips.scatter_cores(normed_grad) + outer_cols(latent_grad_own, latent_weight)
    _, first_pull = jax.vjp(rms_scale, inputs_f, gain_attn)
    input_part, gain_attn_grad = first_pull(normed_grad)
    tokens_grad = (hidden_grad + input_part).astype(BF16)

    block_out = (hidden + jnp.concatenate(block_sum, axis=0)).astype(BF16)
    small_grad = jnp.concatenate(
        [
            gain_attn_grad.reshape(n * cores, -1),
            gain_ffn_grad.reshape(n * cores, -1),
            gain_latent_grad.reshape(n * cores, -1),
            router_grad.reshape(n * cores, -1),
        ],
        axis=1,
    )
    (small_grad,) = chips.lockstep(
        chips.scatter_chips(small_grad.reshape(n, cores, -1), ORDER_SMALL[::-1])
    )
    small_grad = chips.scatter_cores(small_grad).reshape(-1)
    return (
        block_out,
        tokens_grad,
        small_grad[: small_cut[0]],
        query_grad,
        latent_weight_grad,
        small_grad[small_cut[1] : small_cut[2]],
        expand_grad,
        output_grad,
        small_grad[small_cut[0] : small_cut[1]],
        small_grad[small_cut[2] :].reshape(shard, -1),
        shared_in_grad[0],
        shared_in_grad[1],
        shared_down_grad,
        gate_grad_w,
        up_grad_w,
        down_grad_w,
    )


def solution(mesh):
    rows = P(("expert", "fsdp"), None)
    flat = P(("expert", "fsdp"))
    experts = P("expert", "fsdp", None)
    return jax.shard_map(
        body,
        mesh=mesh,
        in_specs=(
            rows, P("expert"), rows, flat, rows, rows, flat, rows, rows, flat, rows, rows, rows,
            rows, experts, experts, experts, rows,
        ),
        out_specs=(
            rows, rows, flat, rows, rows, flat, rows, rows, flat, rows, rows, rows, rows, experts,
            experts, experts,
        ),
        check_vma=False,
    )
```

```python
import math

import jax
import jax.numpy as jnp
from jax import lax
from jax.experimental import pallas as pl
from jax.experimental.pallas import tpu as pltpu
from jax.sharding import PartitionSpec as P

D = 2048
H = 16
DN = 128
DR = 64
DV = 128
KVR = 512
TOPK = 6
SEQ_DEV = 128

NORM_EPS = 1e-06
ROPE_THETA = 50000.0
GATE_SCALE = 2.446

BF16 = jnp.bfloat16
F32 = jnp.float32
BOTH = ("expert", "fsdp")

ORDER_QUERY = ((8, 4, 1, 2), (8, 2, 4, 1))
ORDER_EXPAND = (8, 1, 2, 4)
ORDER_LATENT = (8, 1, 2, 4)
ORDER_OUTPUT = ((8, 2), (1, 4), (4, 1))
TOKEN_GROUPS = (48, 48, 32)
ORDER_TOKENS = ((2, 1, 4), (1, 4, 2), (4, 2, 1))
FIRST_TOKENS = 8
BACK_QUERY = ((1, 4, 2, 8), (4, 2, 1, 8))
BACK_EXPAND = (2, 1, 4, 8)
BACK_LATENT = (2, 1, 4, 8)
BACK_OUTPUT = ((4, 1), (1, 4), (2, 8))


def rms_scale(values, gain_vec):
    return (
        values * lax.rsqrt(jnp.mean(values * values, axis=-1, keepdims=True) + NORM_EPS) * gain_vec
    )


def rotate(values, cos_table, sin_table):
    middle = values.shape[-1] // 2
    lower_half = values[..., :middle]
    upper_half = values[..., middle:]
    return jnp.concatenate(
        [
            lower_half * cos_table - upper_half * sin_table,
            upper_half * cos_table + lower_half * sin_table,
        ],
        axis=-1,
    )


def rope_tables(positions):
    steps_float = jnp.arange(DR // 2).astype(F32) * (2.0 / DR)
    inverse = jnp.exp(-steps_float * math.log(ROPE_THETA))
    turned = positions.astype(F32)[:, None] * inverse[None, :]
    return (jnp.cos(turned), jnp.sin(turned))


def product(left_side, right_side):
    return jnp.dot(left_side, right_side, preferred_element_type=F32)


def inner_rows(left_side, right_side):
    return lax.dot_general(
        left_side, right_side, (((0,), (0,)), ((), ())), preferred_element_type=F32
    )


def outer_cols(left_side, right_side):
    return lax.dot_general(
        left_side, right_side, (((1,), (1,)), ((), ())), preferred_element_type=F32
    )


def together(*values):
    return lax.optimization_barrier(values)


def swiglu(gate_act, up_act):
    return jax.nn.silu(gate_act) * up_act


WIDE = 512
LANES = 128
VMEM_BYTES = 60 * 2**20


def whole_in_vmem():
    return pl.BlockSpec(memory_space=pltpu.VMEM)


def spans(size):
    return [(start, min(WIDE, size - start)) for start in range(0, size, WIDE)]


def weight_copies(in_hbm, down_hbm, in_refs, down_ref, sems):
    ff = in_hbm[0].shape[1]
    count = 0
    by_span = [[] for _ in spans(down_ref.shape[0])]

    def copy(source, target):
        nonlocal count
        count += 1
        return pltpu.make_async_copy(source, target, sems.at[count - 1])

    for extra, joined in zip(in_hbm[1::2], in_refs):
        by_span[-1].append(copy(extra, joined.at[:, pl.ds(ff, extra.shape[1])]))
    for k, (start, size) in enumerate(spans(ff)):
        for expert, joined in zip(in_hbm[0::2], in_refs):
            there = pl.ds(start, size)
            by_span[k].append(copy(expert.at[:, there], joined.at[:, there]))
    down = [
        copy(down_hbm[0], down_ref.at[pl.ds(0, ff), :]),
        copy(down_hbm[1], down_ref.at[pl.ds(ff, down_hbm[1].shape[0]), :]),
    ]
    return by_span, down


def gated(gate, start, size, ff):
    units = lax.broadcasted_iota(jnp.int32, (1, size), 1) + start
    return jnp.where(units < ff, gate, 1.0)


def row_groups(refs):
    start = 0
    for ref in refs:
        yield ref, pl.ds(start, ref.shape[0])
        start += ref.shape[0]


def forward_kernel(*refs):
    groups = len(TOKEN_GROUPS)
    rows_refs = refs[:groups]
    member_ref, own_ref, gate_w, gate_x, up_w, up_x, down_w, down_x = refs[groups : groups + 8]
    out_refs = refs[groups + 8 : 2 * groups + 8]
    logits_ref, gate_act_ref, up_act_ref, hidden_ref = refs[2 * groups + 8 : 2 * groups + 12]
    gate_all, up_all, down_all, sems = refs[2 * groups + 12 :]
    by_span, down = weight_copies(
        (gate_w, gate_x, up_w, up_x), (down_w, down_x), (gate_all, up_all), down_all, sems
    )
    for copy in by_span[-1] + sum(by_span[:-1], []) + down:
        copy.start()
    ff, units = gate_w.shape[1], down_all.shape[0]
    width = down_all.shape[1]
    order = list(zip(spans(units), by_span))
    order = order[-1:] + order[:-1]
    for rows_ref, here in row_groups(rows_refs):
        first = here.start == 0
        for k, ((start, size), copies) in enumerate(order):
            there = pl.ds(start, size)
            if first:
                for copy in copies:
                    copy.wait()
            gate_act = product(rows_ref[...], gate_all[:, there])
            up_act = product(rows_ref[...], up_all[:, there])
            if k == 0:
                logits_ref[here, :] = gate_act
                chosen = member_ref[here, :] / (1.0 + jnp.exp(-gate_act))
                own = jnp.sum(chosen * own_ref[...], axis=1, keepdims=True)
                gate = GATE_SCALE * own / jnp.sum(chosen, axis=1, keepdims=True)
            gate_act_ref[here, there] = gate_act.astype(BF16)
            up_act_ref[here, there] = up_act.astype(BF16)
            hidden = swiglu(gate_act, up_act) * gated(gate, start, size, ff)
            hidden_ref[here, there] = hidden.astype(BF16)
    for copy in down:
        copy.wait()
    for out_ref, here in row_groups(out_refs):
        for start, size in spans(width):
            there = pl.ds(start, size)
            out_ref[:, there] = product(hidden_ref[here, :], down_all[:, there]).astype(BF16)


def backward_kernel(*refs):
    groups = len(TOKEN_GROUPS)
    cot_refs = refs[:groups]
    member_ref, own_ref, logits_ref, gate_act_ref, up_act_ref = refs[groups : groups + 5]
    gate_w, gate_x, up_w, up_x, down_w, down_x = refs[groups + 5 : groups + 11]
    back_refs = refs[groups + 11 : 2 * groups + 11]
    gate_back_ref, up_back_ref, gate_all, up_all, down_all, sems = refs[2 * groups + 11 :]
    by_span, down = weight_copies(
        (gate_w, gate_x, up_w, up_x), (down_w, down_x), (gate_all, up_all), down_all, sems
    )
    for copy in down + sum(by_span, []):
        copy.start()
    ff, units = gate_w.shape[1], down_all.shape[0]
    width = down_all.shape[1]
    for copy in down:
        copy.wait()
    for cot_ref, here in row_groups(cot_refs):
        sigmoid = 1.0 / (1.0 + jnp.exp(-logits_ref[here, :]))
        chosen = member_ref[here, :] * sigmoid
        own = jnp.sum(chosen * own_ref[...], axis=1, keepdims=True)
        all_chosen = jnp.sum(chosen, axis=1, keepdims=True)
        gate = GATE_SCALE * own / all_chosen
        gate_grad = jnp.zeros_like(gate)
        for start, size in spans(units):
            there = pl.ds(start, size)
            last = start + size == units
            hidden_back = outer_cols(cot_ref[...], down_all[there, :])
            gate_act = gate_act_ref[here, there].astype(F32)
            up_act = up_act_ref[here, there].astype(F32)
            sig = 1.0 / (1.0 + jnp.exp(-gate_act))
            silu = gate_act * sig
            column = lax.broadcasted_iota(jnp.int32, (1, size), 1) + start
            term = jnp.where(column < ff, silu * up_act * hidden_back, 0.0)
            gate_grad = gate_grad + jnp.sum(term, axis=1, keepdims=True)
            scaled = hidden_back * gated(gate, start, size, ff)
            up_back_ref[here, there] = (scaled * silu).astype(BF16)
            gate_back = scaled * up_act * (sig + silu * (1.0 - sig))
            if last:
                named = jnp.sum(member_ref[here, :] * own_ref[...], axis=1, keepdims=True)
                logit_back = GATE_SCALE * named * gate_grad * chosen * (1.0 - sigmoid)
                logit_back = logit_back * (own_ref[...] - own / all_chosen) / all_chosen
                gate_back = jnp.where(member_ref[here, :] > 0.0, logit_back, gate_back)
            gate_back_ref[here, there] = gate_back.astype(BF16)
    for copy in sum(by_span, []):
        copy.wait()
    for back_ref, here in row_groups(back_refs):
        for start, size in spans(width):
            there = pl.ds(start, size)
            back = outer_cols(gate_back_ref[here, :], gate_all[there, :])
            back = back + outer_cols(up_back_ref[here, :], up_all[there, :])
            back_ref[:, there] = back.astype(BF16)


def expert_call(kernel, out_shapes, arrays, weights):
    width, ff = weights[0].shape
    units = ff + weights[1].shape[1]
    tokens = sum(rows.shape[0] for rows in arrays[: len(TOKEN_GROUPS)])
    return pl.pallas_call(
        kernel,
        out_shape=out_shapes,
        in_specs=[whole_in_vmem() for _ in arrays]
        + [pl.BlockSpec(memory_space=pl.ANY) for _ in weights],
        out_specs=[whole_in_vmem() for _ in out_shapes],
        scratch_shapes=[
            pltpu.VMEM((width, units), BF16),
            pltpu.VMEM((width, units), BF16),
            pltpu.VMEM((units, width), BF16),
            pltpu.SemaphoreType.DMA((2 * len(spans(ff)) + 4,)),
        ],
        compiler_params=pltpu.CompilerParams(vmem_limit_bytes=VMEM_BYTES),
        cost_estimate=pl.CostEstimate(
            flops=6 * tokens * width * units,
            bytes_accessed=6 * width * units + 12 * tokens * width,
            transcendentals=tokens * units,
        ),
    )(*arrays, *weights)


def expert_forward(rows, member, own, weights):
    tokens = member.shape[0]
    units = weights[0].shape[1] + weights[1].shape[1]
    shapes = [jax.ShapeDtypeStruct(v.shape, BF16) for v in rows]
    shapes.append(jax.ShapeDtypeStruct(member.shape, F32))
    shapes += [jax.ShapeDtypeStruct((tokens, units), BF16)] * 3
    results = expert_call(forward_kernel, shapes, (*rows, member, own), weights)
    return results[: len(rows)], results[len(rows) :]


def expert_backward(cot, member, own, logits, gate_act, up_act, weights):
    shapes = [jax.ShapeDtypeStruct(v.shape, BF16) for v in cot]
    shapes += [jax.ShapeDtypeStruct(gate_act.shape, BF16)] * 2
    results = expert_call(
        backward_kernel, shapes, (*cot, member, own, logits, gate_act, up_act), weights
    )
    return results[: len(cot)], results[len(cot) :]


def in_weights_kernel(*refs):
    groups = 2 * len(TOKEN_GROUPS)
    rows, (first, last), (out, extra_out), turned = (
        refs[:groups], refs[groups : groups + 2], refs[groups + 2 : groups + 4], refs[-1],
    )
    for ref, here in row_groups(rows):
        turned[:, here] = ref[...].T
    tokens = first.shape[0]
    for ref, begin in ((out, 0), (extra_out, out.shape[1])):
        for start, size in spans(ref.shape[1]):
            there = pl.ds(begin + start, size)
            value = product(turned[:, pl.ds(0, tokens)], first[:, there])
            value = value + product(turned[:, pl.ds(tokens, tokens)], last[:, there])
            ref[:, pl.ds(start, size)] = value.astype(ref.dtype)


def in_weights(rows, acts_back, ff):
    tokens, units = acts_back[0].shape
    width = rows[0].shape[1]
    whole = pl.BlockSpec((tokens, units), lambda i: (0, 0), pipeline_mode=pl.Buffered(1))
    outs = [((width, ff), BF16), ((width, units - ff), F32)]
    return pl.pallas_call(
        in_weights_kernel,
        grid=(width // WIDE,),
        out_shape=[jax.ShapeDtypeStruct(*out) for out in outs],
        in_specs=[pl.BlockSpec((v.shape[0], WIDE), lambda i: (0, i)) for v in rows] + [whole] * 2,
        out_specs=[pl.BlockSpec((WIDE, shape[1]), lambda i: (i, 0)) for shape, _ in outs],
        scratch_shapes=[pltpu.VMEM((WIDE, 2 * tokens), BF16)],
        compiler_params=pltpu.CompilerParams(vmem_limit_bytes=VMEM_BYTES),
        cost_estimate=pl.CostEstimate(
            flops=4 * tokens * width * units,
            bytes_accessed=4 * tokens * (width + units) + 2 * width * units,
            transcendentals=0,
        ),
    )(*rows, *acts_back)


def down_weights_kernel(hidden_first, hidden_last, *refs):
    groups = 2 * len(TOKEN_GROUPS)
    cot, (out, extra_out), turned = refs[:groups], refs[groups : groups + 2], refs[-1]
    tokens = hidden_first.shape[0]

    @pl.when(pl.program_id(0) == 0)
    def _():
        turned[:, pl.ds(0, tokens)] = hidden_first[...].T
        turned[:, pl.ds(tokens, tokens)] = hidden_last[...].T

    for ref, begin in ((out, 0), (extra_out, out.shape[0])):
        for start, size in spans(ref.shape[0]):
            there = pl.ds(begin + start, size)
            value = sum(product(turned[there, here], group[...]) for group, here in row_groups(cot))
            ref[pl.ds(start, size), :] = value.astype(ref.dtype)


def down_weights(hidden, cot, ff):
    tokens, units = hidden[0].shape
    width = cot[0].shape[1]
    whole = pl.BlockSpec((tokens, units), lambda i: (0, 0), pipeline_mode=pl.Buffered(1))
    outs = [((ff, width), BF16), ((units - ff, width), F32)]
    return pl.pallas_call(
        down_weights_kernel,
        grid=(width // WIDE,),
        out_shape=[jax.ShapeDtypeStruct(*out) for out in outs],
        in_specs=[whole] * 2 + [pl.BlockSpec((v.shape[0], WIDE), lambda i: (0, i)) for v in cot],
        out_specs=[pl.BlockSpec((shape[0], WIDE), lambda i: (0, i)) for shape, _ in outs],
        scratch_shapes=[pltpu.VMEM((units, 2 * tokens), BF16)],
        compiler_params=pltpu.CompilerParams(vmem_limit_bytes=VMEM_BYTES),
        cost_estimate=pl.CostEstimate(
            flops=4 * tokens * width * units,
            bytes_accessed=4 * tokens * (width + units) + 2 * width * units,
            transcendentals=0,
        ),
    )(*hidden, *cot)


class Chips:
    def __init__(self):
        self.n = lax.axis_size("expert")
        self.f = lax.axis_size("fsdp")
        self.chip = lax.axis_index("expert")
        self.core = lax.axis_index("fsdp")

    def bits(self, order):
        return tuple(m for m in order if (m if isinstance(m, int) else m[0]) < self.n)

    def exchange(self, value, mask):
        masks = (mask,) if isinstance(mask, int) else mask
        pairs = [
            (e * self.f + c, (e ^ masks[c % len(masks)]) * self.f + c)
            for e in range(self.n)
            for c in range(self.f)
        ]
        return lax.ppermute(value, BOTH, pairs)

    def other_core(self, value):
        return lax.ppermute(value, "fsdp", [(0, 1), (1, 0)])

    def gather_cores(self, value, axis=0):
        if self.f != 2:
            return lax.all_gather(value, "fsdp", axis=axis, tiled=True)
        other = self.other_core(value)
        first = self.core == 0
        return jnp.concatenate(
            [jnp.where(first, value, other), jnp.where(first, other, value)], axis=axis
        )

    def swap_cores(self, value, split, concat):
        if self.f != 2:
            return lax.all_to_all(value, "fsdp", split_axis=split, concat_axis=concat, tiled=True)
        size = value.shape[split] // 2
        first = self.core == 0
        low = lax.slice_in_dim(value, 0, size, axis=split)
        high = lax.slice_in_dim(value, size, 2 * size, axis=split)
        keep = jnp.where(first, low, high)
        other = self.other_core(jnp.where(first, high, low))
        return jnp.concatenate(
            [jnp.where(first, keep, other), jnp.where(first, other, keep)], axis=concat
        )

    def sum_cores(self, value):
        if self.f != 2:
            return lax.psum(value, "fsdp")
        return value + self.other_core(value)

    def scatter_cores(self, value, axis=0):
        if self.f != 2:
            return lax.psum_scatter(value, "fsdp", scatter_dimension=axis, tiled=True)
        size = value.shape[axis] // 2
        first = self.core == 0
        low = lax.slice_in_dim(value, 0, size, axis=axis)
        high = lax.slice_in_dim(value, size, 2 * size, axis=axis)
        return jnp.where(first, low, high) + self.other_core(jnp.where(first, high, low))

    def lockstep(self, *streams):
        results = [None] * len(streams)
        waiting = {}

        def advance(i, other):
            try:
                waiting[i] = streams[i].send(other)
            except StopIteration as stop:
                waiting.pop(i, None)
                results[i] = stop.value

        for i in range(len(streams)):
            advance(i, None)
        while waiting:
            names = list(waiting)
            over = [i for i in range(len(streams)) if i not in waiting]
            values, kept = together([waiting[i][0] for i in names], [results[i] for i in over])
            for i, result in zip(over, kept):
                results[i] = result
            masks = [waiting[i][1] for i in names]
            others = [v if m is None else self.exchange(v, m) for v, m in zip(values, masks)]
            for i, other in zip(names, others):
                advance(i, other)
        return together(*results)

    def gather_chips(self, value, order, state=()):
        done = list(state)
        for mask in self.bits(order):
            other = yield value, mask
            place = sum(m > mask for m in done)
            high = (self.chip // mask) % 2 == 1
            value = jnp.stack(
                [jnp.where(high, other, value), jnp.where(high, value, other)], axis=place
            )
            done.append(mask)
        if len(done) == len(self.bits((8, 4, 2, 1))):
            value = value.reshape((self.n,) + value.shape[len(done) :])
        return value

    def halves(self, value, mask, width):
        high = (self.chip // mask) % 2 == 1
        run = mask * width
        low_runs = [value[:, i : i + run] for i in range(0, self.n * width, 2 * run)]
        high_runs = [value[:, i : i + run] for i in range(run, self.n * width, 2 * run)]
        pairs = list(zip(low_runs, high_runs))
        keep = [jnp.where(high, h, l) for l, h in pairs]
        send = [jnp.where(high, l, h) for l, h in pairs]
        return jnp.concatenate(keep, axis=1), jnp.concatenate(send, axis=1)

    def scatter_chips(self, value, order, done=()):
        left = [m for m in sorted(self.bits((8, 4, 2, 1)), reverse=True) if m not in done]
        for mask in self.bits(order):
            place = left.index(mask)
            high = (self.chip // mask) % 2 == 1
            rest = value.shape[1:]
            split = value.reshape((2,) * len(left) + rest)
            lower = lax.index_in_dim(split, 0, place, keepdims=False)
            upper = lax.index_in_dim(split, 1, place, keepdims=False)
            keep = jnp.where(high, upper, lower)
            send = jnp.where(high, lower, upper)
            left.remove(mask)
            other = yield send.astype(BF16), mask
            value = keep.astype(F32) + other.astype(F32)
            if left:
                value = value.astype(BF16)
            value = value.reshape((2 ** len(left),) + rest)
        return value if left else value[0]

    def weight_grad(self, rows, grads, order):
        mask = self.bits(order)[0]
        width = rows.shape[1] // self.n
        keep, send = self.halves(rows, mask, width)
        away = inner_rows(send, grads).astype(BF16)
        other = yield away, mask
        value = inner_rows(keep, grads) + other.astype(F32)
        value = value.astype(BF16).reshape(self.n // 2, width, -1)
        return (yield from self.scatter_chips(value, order[1:], (mask,)))

    def gather_groups(self, value, states):
        for i, order in enumerate(ORDER_TOKENS):
            yield self.gather_tokens(value if i == 0 else None, i, order, states)

    def gather_tokens(self, value, i, order, states):
        if i == 0:
            states["rows"] = jnp.stack([value, (yield value, FIRST_TOKENS)])
        else:
            yield (), None
        start = sum(TOKEN_GROUPS[:i])
        value = states["rows"][:, start : start + TOKEN_GROUPS[i]]
        for mask in self.bits(order)[:-1]:
            other = yield value, mask
            value = jnp.concatenate([value, other], axis=0)
        return value

    def last_groups(self, groups):
        for value, order in zip(groups, ORDER_TOKENS):
            yield self.last_exchange(value, self.bits(order)[-1])

    def last_exchange(self, value, mask):
        return (yield value, mask)

    def scatter_groups(self, groups, others, states):
        for i, (value, other, order) in enumerate(zip(groups, others, ORDER_TOKENS)):
            yield self.scatter_tokens(value, other, i, order, states)

    def scatter_tokens(self, value, other, i, order, states):
        value = value.astype(F32) + other.astype(F32)
        for mask in reversed(self.bits(order)[:-1]):
            half = value.shape[0] // 2
            value = value.astype(BF16)
            received = yield value[half:], mask
            value = value[:half].astype(F32) + received.astype(F32)
        states[i] = value
        if i + 1 < len(TOKEN_GROUPS):
            yield (), None
            return ()
        value = jnp.concatenate([states[k] for k in range(len(TOKEN_GROUPS))], axis=1)
        received = yield value[1].astype(BF16), FIRST_TOKENS
        return value[0] + received.astype(F32)


def body(
    tokens,
    segments,
    routes,
    norm_attn,
    query_proj,
    latent_proj,
    norm_latent,
    expand_proj,
    output_proj,
    norm_ffn,
    router,
    shared_gate,
    shared_up,
    shared_down,
    expert_gate,
    expert_up,
    expert_down,
    cotangent,
):
    chips = Chips()
    n, cores, chip, core = chips.n, chips.f, chips.chip, chips.core
    seq = SEQ_DEV * cores
    heads = H // cores
    shard = D // (n * cores)
    expert_count = n * expert_gate.shape[0]
    small_cut = (shard, 2 * shard, 2 * shard + norm_latent.shape[0])

    tokens_seq = chips.gather_cores(tokens)
    small = jnp.concatenate([norm_attn, norm_ffn, norm_latent, router.reshape(-1)])
    query_own = chips.swap_cores(query_proj, 1, 0)
    query_cut = query_own.shape[1] // 2
    expand_own = chips.swap_cores(expand_proj, 1, 0)
    output_own = chips.swap_cores(output_proj, 1, 0)
    output_cut = output_own.shape[1] // 2
    width = shared_gate.shape[1] // n
    tiny = jnp.concatenate([chips.gather_cores(small[None]).reshape(-1), routes.astype(BF16).reshape(-1)])
    tiny_size = tiny.shape[0]
    columns = latent_proj.shape[1]
    tiny_rows = -(-tiny_size // columns)
    tiny = jnp.pad(tiny, (0, tiny_rows * columns - tiny_size)).reshape(tiny_rows, columns)
    latent_own = jnp.concatenate([latent_proj, tiny], axis=0)
    tokens_seq, query_own, expand_own, output_own, latent_own = together(
        tokens_seq, query_own, expand_own, output_own, latent_own
    )

    def shared_columns(*weights):
        weights = yield weights, None
        shared_in = jnp.stack([w.reshape(shard, n, -1) for w in weights], 2)
        shared_in = shared_in.transpose(1, 0, 2, 3).reshape(n * shard, 2 * width)
        for _ in range(3):
            shared_in = yield shared_in, None
        return lax.all_to_all(shared_in, "expert", split_axis=0, concat_axis=0, tiled=True)

    query_first, query_last, expand_weight, latent_own, shared_in = chips.lockstep(
        chips.gather_chips(query_own[:, :query_cut], ORDER_QUERY[0]),
        chips.gather_chips(query_own[:, query_cut:], ORDER_QUERY[1]),
        chips.gather_chips(expand_own, ORDER_EXPAND),
        chips.gather_chips(latent_own, ORDER_LATENT),
        shared_columns(shared_gate, shared_up),
    )
    (
        query_first, query_last, expand_weight, latent_own, shared_in, tokens_seq, output_own,
        cot_in,
    ) = together(
        query_first, query_last, expand_weight, latent_own, shared_in, tokens_seq, output_own,
        cotangent,
    )
    tiny = latent_own[:, shard:].reshape(n, -1)
    latent_own = latent_own[:, :shard]
    routes_all = tiny[:, cores * small.shape[0] : tiny_size].astype(jnp.int32)
    routes_all = routes_all.reshape(n, SEQ_DEV, TOPK)
    small = tiny[:, : cores * small.shape[0]].reshape(n * cores, -1)
    gain_attn = small[:, : small_cut[0]].reshape(-1).astype(F32)
    gain_ffn = small[:, small_cut[0] : small_cut[1]].reshape(-1).astype(F32)
    gain_latent = small[:, small_cut[1] : small_cut[2]].reshape(-1).astype(F32)
    query_parts = [query_first.reshape(D, -1), query_last.reshape(D, -1)]
    expand_weight = expand_weight.reshape(KVR, -1)
    latent_own_rows = latent_own.reshape(n * shard, -1)
    gate_full, up_full, down_full = (
        lax.all_gather(w[0], "fsdp", axis=0, tiled=True)
        for w in (expert_gate, expert_up, expert_down)
    )
    ff = gate_full.shape[1]

    def idle(rounds):
        for _ in range(rounds):
            yield (), None

    def shared_weights(value):
        value = yield value, None
        return lax.all_gather(
            value.reshape(n, 1, shard, 2 * width), "fsdp", axis=1, tiled=True
        ).reshape(D, 2 * width)

    outputs = {}

    def output_weights(part):
        if part == 0:
            value = yield from chips.gather_chips(output_own, ORDER_OUTPUT[0])
            outputs["first"] = value
        else:
            yield from idle(len(chips.bits(ORDER_OUTPUT[0])))
        value = outputs["first"][..., part * output_cut : (part + 1) * output_cut]
        order = chips.bits(ORDER_OUTPUT[1 + part])
        state = chips.bits(ORDER_OUTPUT[0])
        value = yield from chips.gather_chips(value, order[:-1], state)
        other = yield value, order[-1]
        return value, other

    half = n // 2

    extra = -(-(width + expert_count) // LANES) * LANES
    member_pad = (width + LANES - extra, extra - width - expert_count)

    def expert_members(routes_all):
        turns = []
        for last in (False, True):
            for order in ORDER_TOKENS:
                order = chips.bits((FIRST_TOKENS, *order))
                these = [0]
                for mask in order[:-1]:
                    these = these + [t ^ mask for t in these]
                turns += [t ^ order[-1] if last else t for t in these]
        blocks = routes_all.at[chip ^ jnp.array(turns, jnp.int32)].get(mode="promise_in_bounds")
        blocks = blocks.reshape(2, len(TOKEN_GROUPS), half, SEQ_DEV, TOPK)
        members = []
        for last in range(2):
            parts, start = [], 0
            for i, size in enumerate(TOKEN_GROUPS):
                parts.append(blocks[last, i, :, start : start + size].reshape(half * size, TOPK))
                start += size
            named = jnp.concatenate(parts, axis=0)[:, :, None]
            member = jnp.any(named == jnp.arange(expert_count, dtype=jnp.int32), axis=1)
            members.append(jnp.pad(member.astype(F32), ((0, 0), member_pad)))
        return members

    positions = jnp.arange(seq, dtype=jnp.int32)
    cos_table, sin_table = rope_tables(positions)
    inputs_f = tokens.astype(F32)
    score_scale = (DN + DR) ** (-0.5)

    def attention():
        rows = yield tokens_seq, None
        normed = rms_scale(rows.astype(F32), gain_attn).astype(BF16)
        normed_part = lax.dynamic_index_in_dim(
            normed.reshape(seq, n, cores, shard), core, 2, keepdims=False
        ).reshape(seq, n * shard)
        latent = chips.sum_cores(product(normed_part, latent_own_rows))
        query_all = jnp.concatenate([product(normed, part) for part in query_parts], axis=1)
        query_all = query_all.reshape(seq, heads, DN + DR)
        query_nope = query_all[..., :DN].astype(BF16)
        query_rope = rotate(
            query_all[..., DN:], cos_table[:, None, :], sin_table[:, None, :]
        ).astype(BF16)
        normed, normed_part, latent, query_nope, query_rope = yield (
            (normed, normed_part, latent, query_nope, query_rope),
            None,
        )
        latent_norm = rms_scale(latent[:, :KVR], gain_latent).astype(BF16)
        key_rope = rotate(latent[:, KVR:], cos_table, sin_table).astype(BF16)
        expanded = product(latent_norm, expand_weight).astype(BF16).reshape(seq, heads, DN + DV)
        key_nope = expanded[..., :DN]
        values_all = expanded[..., DN:]
        allowed = (positions[:, None] >= positions[None, :]) & (
            segments[:, None] == segments[None, :]
        )
        scores = jnp.einsum("thd,shd->hts", query_nope, key_nope, preferred_element_type=F32)
        scores = scores + jnp.einsum(
            "thd,sd->hts", query_rope, key_rope, preferred_element_type=F32
        )
        scores = jnp.where(allowed[None], scores * score_scale, -1e30)
        shifted = jnp.exp(scores - jnp.max(scores, axis=-1, keepdims=True))
        probs = shifted / jnp.sum(shifted, axis=-1, keepdims=True)
        latent_norm, key_rope, key_nope, values_all, probs = yield (
            (latent_norm, key_rope, key_nope, values_all, probs),
            None,
        )
        probs_low = probs.astype(BF16)
        attended = jnp.einsum("hts,shd->thd", probs_low, values_all, preferred_element_type=F32)
        attended = attended.reshape(seq, heads * DV).astype(BF16)
        attended = yield chips.gather_cores(attended, axis=1), None
        return (
            normed, normed_part, latent, query_nope, query_rope, latent_norm, key_rope, key_nope, values_all,
            probs, probs_low, attended,
        )

    def joined_output(parts):
        full = []
        for (own_part, other_part), order in zip(parts, ORDER_OUTPUT[1:]):
            mask = chips.bits(order)[-1]
            high = (chip // mask) % 2 == 1
            lower = jnp.where(high, other_part, own_part)
            upper = jnp.where(high, own_part, other_part)
            place = sum(m > mask for m in chips.bits((8, 4, 2, 1)))
            full.append(jnp.stack([lower, upper], axis=place).reshape(D, -1))
        return full

    def late_members(routes_all):
        yield from idle(3)
        routes_all = yield routes_all, None
        return expert_members(routes_all)

    states = {}
    *output_parts, kept_attention, shared_in, members, cot_zero, cot_one, cot_two = chips.lockstep(
        output_weights(0),
        output_weights(1),
        attention(),
        shared_weights(shared_in),
        late_members(routes_all),
        *chips.gather_groups(cot_in, states),
    )
    cot_first = [cot_zero, cot_one, cot_two]
    (
        normed, normed_part, latent, query_nope, query_rope, latent_norm, key_rope, key_nope, values_all,
        probs, probs_low, attended,
    ) = kept_attention
    hidden = []
    for (own_part, other_part), order in zip(output_parts, ORDER_OUTPUT[1:]):
        keep, send = chips.halves(attended, chips.bits(order)[-1], D // n)
        part = product(keep, own_part.reshape(D // 2, -1))
        hidden.append(part + product(send, other_part.reshape(D // 2, -1)))
    hidden = inputs_f + chips.swap_cores(jnp.concatenate(hidden, axis=1), 0, 1)
    normed_ffn = rms_scale(hidden, gain_ffn).astype(BF16)

    def beside(function, *values):
        values = yield values, None
        return function(*values)

    own = (jnp.arange(expert_count, dtype=jnp.int32) == chip).astype(F32)
    own = jnp.pad(own, member_pad)[None]

    def flat(groups):
        return [v.reshape(-1, D) for v in groups]

    def blocks(groups):
        return [v.reshape(half, -1, D) for v in groups]

    def forward(groups, member):
        rows = flat(groups)
        out, (logits, gate_act, up_act, hidden_act) = expert_forward(rows, member, own, weights)
        return blocks(out), (rows, logits, gate_act, up_act, hidden_act)

    def backward(kept, groups, member):
        _, logits, gate_act, up_act, _ = kept
        cot = flat(groups)
        back, (gate_back, up_back) = expert_backward(
            cot, member, own, logits, gate_act, up_act, weights
        )
        return blocks(back), (cot, gate_back, up_back)

    def extra_weights(shared_in, router_all, shared_down_own):
        gate_extra = jnp.concatenate([shared_in[:, :width], router_all], axis=1)
        gate_extra = jnp.pad(gate_extra, ((0, 0), (0, extra - width - expert_count)))
        up_extra = jnp.pad(shared_in[:, width:], ((0, 0), (0, extra - width)))
        down_extra = jnp.pad(chips.gather_cores(shared_down_own), ((0, extra - width), (0, 0)))
        return gate_full, gate_extra, up_full, up_extra, down_full, down_extra

    *rows_first, output_full, weights = chips.lockstep(
        *chips.gather_groups(normed_ffn, {}),
        beside(lambda *parts: joined_output(parts), *output_parts),
        beside(extra_weights, shared_in, small[:, small_cut[2] :].reshape(D, -1), shared_down),
    )
    *rows_last, (out_first, kept_first) = chips.lockstep(
        *chips.last_groups(rows_first), beside(forward, rows_first, members[0])
    )
    cot_first, rows_last = together(cot_first, rows_last)
    *cot_last, (out_last, kept_last) = chips.lockstep(
        *chips.last_groups(cot_first), beside(forward, rows_last, members[1])
    )
    *sent_out, (back_last, grads_last) = chips.lockstep(
        *chips.last_groups(out_last), beside(backward, kept_last, cot_last, members[1])
    )
    *sent_back, (back_first, grads_first) = chips.lockstep(
        *chips.last_groups(back_last), beside(backward, kept_first, cot_first, members[0])
    )

    def down_grads(hidden_acts, cots):
        yield from idle(2)
        hidden_acts, cots = yield (hidden_acts, cots), None
        return down_weights(hidden_acts, [v for groups in cots for v in groups], ff)

    *_, ffn_grad, (down_w, down_extra_w) = chips.lockstep(
        *chips.scatter_groups(back_first, sent_back, {}),
        down_grads((kept_first[4], kept_last[4]), (grads_first[0], grads_last[0])),
    )

    middle = {}

    def through_norm(ffn_grad):
        ffn_grad = yield ffn_grad, None
        _, norm_pull = jax.vjp(rms_scale, hidden, gain_ffn)
        hidden_part, gain_ffn_grad = norm_pull(ffn_grad)
        hidden_grad = cotangent.astype(F32) + hidden_part
        middle["attn_grad"] = chips.swap_cores(hidden_grad.astype(BF16), 1, 0)
        middle["hidden_grad"], middle["gain"] = yield (hidden_grad, gain_ffn_grad), None
        return middle["hidden_grad"], middle["gain"]

    def output_grads(part):
        yield from idle(1)
        grads = middle["attn_grad"][:, part * output_cut : (part + 1) * output_cut]
        order = chips.bits(BACK_OUTPUT[part])
        value = yield from chips.weight_grad(attended, grads, order)
        middle["output", part] = value
        if part == 0:
            yield from idle(2)
            return ()
        value = jnp.concatenate([middle["output", 0], value], axis=-1)
        return (yield from chips.scatter_chips(value, BACK_OUTPUT[2], order))

    def in_grads(rows, gate_back, up_back):
        rows = [v for groups in rows for v in groups]
        yield from idle(1)
        rows, gate_back = yield (rows, gate_back), None
        gate_w, gate_x = yield in_weights(rows, gate_back, ff), None
        middle["router_grad"] = gate_x[:, width : width + expert_count]
        gate_w = lax.psum_scatter(gate_w, "fsdp", scatter_dimension=0, tiled=True)
        gate_w, rows, up_back = yield (gate_w, rows, up_back), None
        up_w, up_x = in_weights(rows, up_back, ff)
        gate_w = gate_w.astype(F32)[None]
        gate_w, up_w, gate_x, up_x = yield (gate_w, up_w, gate_x, up_x), None
        up_w = lax.psum_scatter(up_w, "fsdp", scatter_dimension=0, tiled=True)
        shared = jnp.concatenate([gate_x[:, :width], up_x[:, :width]], axis=1)
        shared = chips.scatter_cores(shared.reshape(n, cores * shard, 2 * width), 1).astype(BF16)
        shared = yield shared, None
        shared = lax.all_to_all(shared, "expert", split_axis=0, concat_axis=0, tiled=True)
        shared, up_w = yield (shared, up_w), None
        shared = shared.astype(F32).reshape(n, shard, 2, width).transpose(2, 1, 0, 3)
        return (gate_w, up_w.astype(F32)[None]), shared.reshape(2, shard, n * width)

    def second_grads(down_w, down_extra_w):
        down_w, down_extra_w = yield (down_w, down_extra_w), None
        down_w = lax.psum_scatter(down_w, "fsdp", scatter_dimension=0, tiled=True)
        down_extra_w = chips.scatter_cores(down_extra_w[:width])
        down_w, down_extra_w = yield (down_w, down_extra_w), None
        yield from idle(1)
        down_w = yield down_w, None
        return down_w.astype(F32)[None], down_extra_w

    def attention_back():
        yield (), None
        attn_grad = middle["attn_grad"]
        attended_grad = outer_cols(attn_grad[:, :output_cut], output_full[0]) + outer_cols(
            attn_grad[:, output_cut:], output_full[1]
        )
        attended_grad = yield chips.scatter_cores(attended_grad, 1).astype(BF16), None
        attended_grad = attended_grad.reshape(seq, heads, DV)
        prob_grad = jnp.einsum("thd,shd->hts", attended_grad, values_all, preferred_element_type=F32)
        weighted = jnp.sum(probs * prob_grad, axis=-1, keepdims=True)
        score_grad = (probs * (prob_grad - weighted)).astype(BF16)
        query_nope_grad = score_scale * jnp.einsum(
            "hts,shd->thd", score_grad, key_nope, preferred_element_type=F32
        )
        query_rope_grad = score_scale * jnp.einsum(
            "hts,sd->thd", score_grad, key_rope, preferred_element_type=F32
        )
        key_nope_grad = score_scale * jnp.einsum(
            "hts,thd->shd", score_grad, query_nope, preferred_element_type=F32
        )
        key_rope_grad = score_scale * jnp.einsum(
            "hts,thd->sd", score_grad, query_rope, preferred_element_type=F32
        )
        values_grad = jnp.einsum(
            "hts,thd->shd", probs_low, attended_grad, preferred_element_type=F32
        )
        (query_nope_grad, query_rope_grad, key_nope_grad, key_rope_grad, values_grad) = yield (
            (query_nope_grad, query_rope_grad, key_nope_grad, key_rope_grad, values_grad),
            None,
        )
        expanded_grad = jnp.concatenate([key_nope_grad, values_grad], axis=2)
        expanded_grad = expanded_grad.reshape(seq, heads * (DN + DV)).astype(BF16)
        latent_back = chips.sum_cores(
            jnp.concatenate([outer_cols(expanded_grad, expand_weight), key_rope_grad], axis=1)
        )
        _, latent_pull = jax.vjp(rms_scale, latent[:, :KVR], gain_latent)
        latent_nope_grad, gain_latent_grad = latent_pull(latent_back[:, :KVR])
        gain_latent_grad = gain_latent_grad / cores
        latent_rope_grad = rotate(latent_back[:, KVR:], cos_table, -sin_table)
        latent_grad = jnp.concatenate([latent_nope_grad, latent_rope_grad], axis=1).astype(BF16)
        query_back = jnp.concatenate(
            [query_nope_grad, rotate(query_rope_grad, cos_table[:, None, :], -sin_table[:, None, :])],
            axis=2,
        )
        query_back = query_back.reshape(seq, heads * (DN + DR)).astype(BF16)
        middle["query_back"] = query_back
        middle["expanded_grad"] = expanded_grad
        middle["latent_grad"] = latent_grad
        middle["gain_latent_grad"] = gain_latent_grad
        yield (query_back, expanded_grad, latent_grad), None

    def projection_grads(rows, name, columns, order):
        yield from idle(3)
        return (yield from chips.weight_grad(rows, middle[name][:, columns], order))

    def input_grads():
        yield from idle(5)
        query_back, latent_grad, latent_rows = yield (
            (middle["query_back"], middle["latent_grad"], latent_own),
            None,
        )
        normed_grad = outer_cols(query_back[:, :query_cut], query_parts[0]) + outer_cols(
            query_back[:, query_cut:], query_parts[1]
        )
        latent_weight = chips.gather_cores(latent_rows[:, None], axis=1).reshape(D, -1)
        latent_grad_own = lax.dynamic_slice_in_dim(latent_grad, core * SEQ_DEV, SEQ_DEV, 0)
        normed_grad = chips.scatter_cores(normed_grad) + outer_cols(latent_grad_own, latent_weight)
        _, first_pull = jax.vjp(rms_scale, inputs_f, gain_attn)
        input_part, gain_attn_grad = first_pull(normed_grad)
        tokens_grad = (middle["hidden_grad"] + input_part).astype(BF16)
        tokens_grad, gain_attn_grad = yield (tokens_grad, gain_attn_grad), None
        small_grad = jnp.concatenate(
            [
                gain_attn_grad.reshape(n * cores, -1),
                middle["gain"].reshape(n * cores, -1),
                middle["gain_latent_grad"].reshape(n * cores, -1),
                middle["router_grad"].reshape(n * cores, -1),
            ],
            axis=1,
        )
        small_grad = lax.all_to_all(
            small_grad.reshape(n, -1), "expert", split_axis=0, concat_axis=0, tiled=True
        )
        small_grad = jnp.sum(small_grad, axis=0).reshape(cores, -1)
        return tokens_grad, chips.scatter_cores(small_grad).reshape(-1)

    (
        _, _, _, block_sum, _, _, output_grad, query_first_grad, query_last_grad, expand_grad,
        latent_weight_grad, in_grad, second_grad, input_grad,
    ) = chips.lockstep(
        through_norm(ffn_grad),
        *chips.scatter_groups(out_first, sent_out, {}),
        attention_back(),
        output_grads(0),
        output_grads(1),
        projection_grads(normed, "query_back", slice(0, query_cut), BACK_QUERY[0]),
        projection_grads(normed, "query_back", slice(query_cut, None), BACK_QUERY[1]),
        projection_grads(latent_norm, "expanded_grad", slice(None), BACK_EXPAND),
        projection_grads(normed_part, "latent_grad", slice(None), BACK_LATENT),
        in_grads(
            (kept_first[0], kept_last[0]),
            (grads_first[1], grads_last[1]),
            (grads_first[2], grads_last[2]),
        ),
        second_grads(down_w, down_extra_w),
        input_grads(),
    )
    (gate_grad_w, up_grad_w), shared_in_grad = in_grad
    down_grad_w, shared_down_grad = second_grad
    tokens_grad, small_grad = input_grad
    block_out = (hidden + block_sum).astype(BF16)
    output_grad = chips.swap_cores(output_grad, 0, 1)
    query_grad = jnp.concatenate([query_first_grad, query_last_grad], axis=1)
    query_grad = chips.swap_cores(query_grad, 0, 1)
    expand_grad = chips.swap_cores(expand_grad, 0, 1)
    return (
        block_out,
        tokens_grad,
        small_grad[: small_cut[0]],
        query_grad,
        latent_weight_grad,
        small_grad[small_cut[1] : small_cut[2]],
        expand_grad,
        output_grad,
        small_grad[small_cut[0] : small_cut[1]],
        small_grad[small_cut[2] :].reshape(shard, -1),
        shared_in_grad[0],
        shared_in_grad[1],
        shared_down_grad,
        gate_grad_w,
        up_grad_w,
        down_grad_w,
    )


def solution(mesh):
    rows = P(("expert", "fsdp"), None)
    flat = P(("expert", "fsdp"))
    experts = P("expert", "fsdp", None)
    return jax.shard_map(
        body,
        mesh=mesh,
        in_specs=(
            rows, P("expert"), rows, flat, rows, rows, flat, rows, rows, flat, rows, rows, rows,
            rows, experts, experts, experts, rows,
        ),
        out_specs=(
            rows, rows, flat, rows, rows, flat, rows, rows, flat, rows, rows, rows, rows, experts,
            experts, experts,
        ),
        check_vma=False,
    )
```

```python
import math

import jax
import jax.numpy as jnp
from jax import lax
from jax.experimental import pallas as pl
from jax.experimental.pallas import tpu as pltpu
from jax.sharding import PartitionSpec as P

D = 2048
H = 16
DN = 128
DR = 64
DV = 128
KVR = 512
TOPK = 6
SEQ_DEV = 128

NORM_EPS = 1e-06
ROPE_THETA = 50000.0
GATE_SCALE = 2.446

BF16 = jnp.bfloat16
F32 = jnp.float32
BOTH = ("expert", "fsdp")

ORDER_QUERY = ((8, 4, 1, 2), (8, 2, 4, 1))
ORDER_EXPAND = (8, 1, 2, 4)
ORDER_LATENT = (8, 1, 2, 4)
ORDER_OUTPUT = ((8, 2), (1, 4), (4, 1))
TOKEN_GROUPS = (48, 48, 32)
ORDER_TOKENS = ((2, 1, 4), (1, 4, 2), (4, 2, 1))
FIRST_TOKENS = 8
BACK_QUERY = ((1, 4, 2, 8), (4, 2, 1, 8))
BACK_EXPAND = (2, 1, 4, 8)
BACK_LATENT = (2, 1, 4, 8)
BACK_OUTPUT = ((4, 2), (2, 4), (1, 8))


def rms_scale(values, gain_vec):
    return (
        values * lax.rsqrt(jnp.mean(values * values, axis=-1, keepdims=True) + NORM_EPS) * gain_vec
    )


def rotate(values, cos_table, sin_table):
    middle = values.shape[-1] // 2
    lower_half = values[..., :middle]
    upper_half = values[..., middle:]
    return jnp.concatenate(
        [
            lower_half * cos_table - upper_half * sin_table,
            upper_half * cos_table + lower_half * sin_table,
        ],
        axis=-1,
    )


def rope_tables(positions):
    steps_float = jnp.arange(DR // 2).astype(F32) * (2.0 / DR)
    inverse = jnp.exp(-steps_float * math.log(ROPE_THETA))
    turned = positions.astype(F32)[:, None] * inverse[None, :]
    return (jnp.cos(turned), jnp.sin(turned))


def product(left_side, right_side):
    return jnp.dot(left_side, right_side, preferred_element_type=F32)


def inner_rows(left_side, right_side):
    return lax.dot_general(
        left_side, right_side, (((0,), (0,)), ((), ())), preferred_element_type=F32
    )


def outer_cols(left_side, right_side):
    return lax.dot_general(
        left_side, right_side, (((1,), (1,)), ((), ())), preferred_element_type=F32
    )


def together(*values):
    return lax.optimization_barrier(values)


def swiglu(gate_act, up_act):
    return jax.nn.silu(gate_act) * up_act


WIDE = 512
LANES = 128
VMEM_BYTES = 60 * 2**20


def whole_in_vmem():
    return pl.BlockSpec(memory_space=pltpu.VMEM)


def spans(size):
    return [(start, min(WIDE, size - start)) for start in range(0, size, WIDE)]


def weight_copies(in_hbm, down_hbm, in_refs, down_ref, sems):
    ff = in_hbm[0].shape[1]
    count = 0
    by_span = [[] for _ in spans(down_ref.shape[0])]

    def copy(source, target):
        nonlocal count
        count += 1
        return pltpu.make_async_copy(source, target, sems.at[count - 1])

    for extra, joined in zip(in_hbm[1::2], in_refs):
        by_span[-1].append(copy(extra, joined.at[:, pl.ds(ff, extra.shape[1])]))
    for k, (start, size) in enumerate(spans(ff)):
        for expert, joined in zip(in_hbm[0::2], in_refs):
            there = pl.ds(start, size)
            by_span[k].append(copy(expert.at[:, there], joined.at[:, there]))
    down = [
        copy(down_hbm[0], down_ref.at[pl.ds(0, ff), :]),
        copy(down_hbm[1], down_ref.at[pl.ds(ff, down_hbm[1].shape[0]), :]),
    ]
    return by_span, down


def gated(gate, start, size, ff):
    units = lax.broadcasted_iota(jnp.int32, (1, size), 1) + start
    return jnp.where(units < ff, gate, 1.0)


def row_groups(refs):
    start = 0
    for ref in refs:
        yield ref, pl.ds(start, ref.shape[0])
        start += ref.shape[0]


def forward_kernel(*refs):
    groups = len(TOKEN_GROUPS)
    rows_refs = refs[:groups]
    member_ref, own_ref, gate_w, gate_x, up_w, up_x, down_w, down_x = refs[groups : groups + 8]
    out_refs = refs[groups + 8 : 2 * groups + 8]
    logits_ref, gate_act_ref, up_act_ref, hidden_ref = refs[2 * groups + 8 : 2 * groups + 12]
    gate_all, up_all, down_all, sems = refs[2 * groups + 12 :]
    by_span, down = weight_copies(
        (gate_w, gate_x, up_w, up_x), (down_w, down_x), (gate_all, up_all), down_all, sems
    )
    for copy in by_span[-1] + sum(by_span[:-1], []) + down:
        copy.start()
    ff, units = gate_w.shape[1], down_all.shape[0]
    width = down_all.shape[1]
    order = list(zip(spans(units), by_span))
    order = order[-1:] + order[:-1]
    for rows_ref, here in row_groups(rows_refs):
        first = here.start == 0
        for k, ((start, size), copies) in enumerate(order):
            there = pl.ds(start, size)
            if first:
                for copy in copies:
                    copy.wait()
            gate_act = product(rows_ref[...], gate_all[:, there])
            up_act = product(rows_ref[...], up_all[:, there])
            if k == 0:
                logits_ref[here, :] = gate_act
                chosen = member_ref[here, :] / (1.0 + jnp.exp(-gate_act))
                own = jnp.sum(chosen * own_ref[...], axis=1, keepdims=True)
                gate = GATE_SCALE * own / jnp.sum(chosen, axis=1, keepdims=True)
            gate_act_ref[here, there] = gate_act.astype(BF16)
            up_act_ref[here, there] = up_act.astype(BF16)
            hidden = swiglu(gate_act, up_act) * gated(gate, start, size, ff)
            hidden_ref[here, there] = hidden.astype(BF16)
    for copy in down:
        copy.wait()
    for out_ref, here in row_groups(out_refs):
        for start, size in spans(width):
            there = pl.ds(start, size)
            out_ref[:, there] = product(hidden_ref[here, :], down_all[:, there]).astype(BF16)


def backward_kernel(*refs):
    groups = len(TOKEN_GROUPS)
    cot_refs = refs[:groups]
    member_ref, own_ref, logits_ref, gate_act_ref, up_act_ref = refs[groups : groups + 5]
    gate_w, gate_x, up_w, up_x, down_w, down_x = refs[groups + 5 : groups + 11]
    back_refs = refs[groups + 11 : 2 * groups + 11]
    gate_back_ref, up_back_ref, gate_all, up_all, down_all, sems = refs[2 * groups + 11 :]
    by_span, down = weight_copies(
        (gate_w, gate_x, up_w, up_x), (down_w, down_x), (gate_all, up_all), down_all, sems
    )
    for copy in down + sum(by_span, []):
        copy.start()
    ff, units = gate_w.shape[1], down_all.shape[0]
    width = down_all.shape[1]
    for copy in down:
        copy.wait()
    for cot_ref, here in row_groups(cot_refs):
        sigmoid = 1.0 / (1.0 + jnp.exp(-logits_ref[here, :]))
        chosen = member_ref[here, :] * sigmoid
        own = jnp.sum(chosen * own_ref[...], axis=1, keepdims=True)
        all_chosen = jnp.sum(chosen, axis=1, keepdims=True)
        gate = GATE_SCALE * own / all_chosen
        gate_grad = jnp.zeros_like(gate)
        for start, size in spans(units):
            there = pl.ds(start, size)
            last = start + size == units
            hidden_back = outer_cols(cot_ref[...], down_all[there, :])
            gate_act = gate_act_ref[here, there].astype(F32)
            up_act = up_act_ref[here, there].astype(F32)
            sig = 1.0 / (1.0 + jnp.exp(-gate_act))
            silu = gate_act * sig
            column = lax.broadcasted_iota(jnp.int32, (1, size), 1) + start
            term = jnp.where(column < ff, silu * up_act * hidden_back, 0.0)
            gate_grad = gate_grad + jnp.sum(term, axis=1, keepdims=True)
            scaled = hidden_back * gated(gate, start, size, ff)
            up_back_ref[here, there] = (scaled * silu).astype(BF16)
            gate_back = scaled * up_act * (sig + silu * (1.0 - sig))
            if last:
                named = jnp.sum(member_ref[here, :] * own_ref[...], axis=1, keepdims=True)
                logit_back = GATE_SCALE * named * gate_grad * chosen * (1.0 - sigmoid)
                logit_back = logit_back * (own_ref[...] - own / all_chosen) / all_chosen
                gate_back = jnp.where(member_ref[here, :] > 0.0, logit_back, gate_back)
            gate_back_ref[here, there] = gate_back.astype(BF16)
    for copy in sum(by_span, []):
        copy.wait()
    for back_ref, here in row_groups(back_refs):
        for start, size in spans(width):
            there = pl.ds(start, size)
            back = outer_cols(gate_back_ref[here, :], gate_all[there, :])
            back = back + outer_cols(up_back_ref[here, :], up_all[there, :])
            back_ref[:, there] = back.astype(BF16)


def expert_call(kernel, out_shapes, arrays, weights):
    width, ff = weights[0].shape
    units = ff + weights[1].shape[1]
    tokens = sum(rows.shape[0] for rows in arrays[: len(TOKEN_GROUPS)])
    return pl.pallas_call(
        kernel,
        out_shape=out_shapes,
        in_specs=[whole_in_vmem() for _ in arrays]
        + [pl.BlockSpec(memory_space=pl.ANY) for _ in weights],
        out_specs=[whole_in_vmem() for _ in out_shapes],
        scratch_shapes=[
            pltpu.VMEM((width, units), BF16),
            pltpu.VMEM((width, units), BF16),
            pltpu.VMEM((units, width), BF16),
            pltpu.SemaphoreType.DMA((2 * len(spans(ff)) + 4,)),
        ],
        compiler_params=pltpu.CompilerParams(vmem_limit_bytes=VMEM_BYTES),
        cost_estimate=pl.CostEstimate(
            flops=6 * tokens * width * units,
            bytes_accessed=6 * width * units + 12 * tokens * width,
            transcendentals=tokens * units,
        ),
    )(*arrays, *weights)


def expert_forward(rows, member, own, weights):
    tokens = member.shape[0]
    units = weights[0].shape[1] + weights[1].shape[1]
    shapes = [jax.ShapeDtypeStruct(v.shape, BF16) for v in rows]
    shapes.append(jax.ShapeDtypeStruct(member.shape, F32))
    shapes += [jax.ShapeDtypeStruct((tokens, units), BF16)] * 3
    results = expert_call(forward_kernel, shapes, (*rows, member, own), weights)
    return results[: len(rows)], results[len(rows) :]


def expert_backward(cot, member, own, logits, gate_act, up_act, weights):
    shapes = [jax.ShapeDtypeStruct(v.shape, BF16) for v in cot]
    shapes += [jax.ShapeDtypeStruct(gate_act.shape, BF16)] * 2
    results = expert_call(
        backward_kernel, shapes, (*cot, member, own, logits, gate_act, up_act), weights
    )
    return results[: len(cot)], results[len(cot) :]


def in_weights_kernel(*refs):
    groups = 2 * len(TOKEN_GROUPS)
    rows, (first, last), (out, extra_out), turned = (
        refs[:groups], refs[groups : groups + 2], refs[groups + 2 : groups + 4], refs[-1],
    )
    for ref, here in row_groups(rows):
        turned[:, here] = ref[...].T
    tokens = first.shape[0]
    for ref, begin in ((out, 0), (extra_out, out.shape[1])):
        for start, size in spans(ref.shape[1]):
            there = pl.ds(begin + start, size)
            value = product(turned[:, pl.ds(0, tokens)], first[:, there])
            value = value + product(turned[:, pl.ds(tokens, tokens)], last[:, there])
            ref[:, pl.ds(start, size)] = value.astype(ref.dtype)


def in_weights(rows, acts_back, ff):
    tokens, units = acts_back[0].shape
    width = rows[0].shape[1]
    whole = pl.BlockSpec((tokens, units), lambda i: (0, 0), pipeline_mode=pl.Buffered(1))
    outs = [((width, ff), BF16), ((width, units - ff), BF16)]
    return pl.pallas_call(
        in_weights_kernel,
        grid=(width // WIDE,),
        out_shape=[jax.ShapeDtypeStruct(*out) for out in outs],
        in_specs=[pl.BlockSpec((v.shape[0], WIDE), lambda i: (0, i)) for v in rows] + [whole] * 2,
        out_specs=[pl.BlockSpec((WIDE, shape[1]), lambda i: (i, 0)) for shape, _ in outs],
        scratch_shapes=[pltpu.VMEM((WIDE, 2 * tokens), BF16)],
        compiler_params=pltpu.CompilerParams(vmem_limit_bytes=VMEM_BYTES),
        cost_estimate=pl.CostEstimate(
            flops=4 * tokens * width * units,
            bytes_accessed=4 * tokens * (width + units) + 2 * width * units,
            transcendentals=0,
        ),
    )(*rows, *acts_back)


def down_weights_kernel(hidden_first, hidden_last, *refs):
    groups = 2 * len(TOKEN_GROUPS)
    cot, (out, extra_out), turned = refs[:groups], refs[groups : groups + 2], refs[-1]
    tokens = hidden_first.shape[0]

    @pl.when(pl.program_id(0) == 0)
    def _():
        turned[:, pl.ds(0, tokens)] = hidden_first[...].T
        turned[:, pl.ds(tokens, tokens)] = hidden_last[...].T

    for ref, begin in ((out, 0), (extra_out, out.shape[0])):
        for start, size in spans(ref.shape[0]):
            there = pl.ds(begin + start, size)
            value = sum(product(turned[there, here], group[...]) for group, here in row_groups(cot))
            ref[pl.ds(start, size), :] = value.astype(ref.dtype)


def down_weights(hidden, cot, ff):
    tokens, units = hidden[0].shape
    width = cot[0].shape[1]
    whole = pl.BlockSpec((tokens, units), lambda i: (0, 0), pipeline_mode=pl.Buffered(1))
    outs = [((ff, width), BF16), ((units - ff, width), F32)]
    return pl.pallas_call(
        down_weights_kernel,
        grid=(width // WIDE,),
        out_shape=[jax.ShapeDtypeStruct(*out) for out in outs],
        in_specs=[whole] * 2 + [pl.BlockSpec((v.shape[0], WIDE), lambda i: (0, i)) for v in cot],
        out_specs=[pl.BlockSpec((shape[0], WIDE), lambda i: (0, i)) for shape, _ in outs],
        scratch_shapes=[pltpu.VMEM((units, 2 * tokens), BF16)],
        compiler_params=pltpu.CompilerParams(vmem_limit_bytes=VMEM_BYTES),
        cost_estimate=pl.CostEstimate(
            flops=4 * tokens * width * units,
            bytes_accessed=4 * tokens * (width + units) + 2 * width * units,
            transcendentals=0,
        ),
    )(*hidden, *cot)


class Chips:
    def __init__(self):
        self.n = lax.axis_size("expert")
        self.f = lax.axis_size("fsdp")
        self.chip = lax.axis_index("expert")
        self.core = lax.axis_index("fsdp")

    def bits(self, order):
        return tuple(m for m in order if (m if isinstance(m, int) else m[0]) < self.n)

    def exchange(self, value, mask):
        masks = (mask,) if isinstance(mask, int) else mask
        pairs = [
            (e * self.f + c, (e ^ masks[c % len(masks)]) * self.f + c)
            for e in range(self.n)
            for c in range(self.f)
        ]
        return lax.ppermute(value, BOTH, pairs)

    def other_core(self, value):
        return lax.ppermute(value, "fsdp", [(0, 1), (1, 0)])

    def gather_cores(self, value, axis=0):
        if self.f != 2:
            return lax.all_gather(value, "fsdp", axis=axis, tiled=True)
        other = self.other_core(value)
        first = self.core == 0
        return jnp.concatenate(
            [jnp.where(first, value, other), jnp.where(first, other, value)], axis=axis
        )

    def swap_cores(self, value, split, concat):
        if self.f != 2:
            return lax.all_to_all(value, "fsdp", split_axis=split, concat_axis=concat, tiled=True)
        size = value.shape[split] // 2
        first = self.core == 0
        low = lax.slice_in_dim(value, 0, size, axis=split)
        high = lax.slice_in_dim(value, size, 2 * size, axis=split)
        keep = jnp.where(first, low, high)
        other = self.other_core(jnp.where(first, high, low))
        return jnp.concatenate(
            [jnp.where(first, keep, other), jnp.where(first, other, keep)], axis=concat
        )

    def sum_cores(self, value):
        if self.f != 2:
            return lax.psum(value, "fsdp")
        return value + self.other_core(value)

    def scatter_cores(self, value, axis=0):
        if self.f != 2:
            return lax.psum_scatter(value, "fsdp", scatter_dimension=axis, tiled=True)
        size = value.shape[axis] // 2
        first = self.core == 0
        low = lax.slice_in_dim(value, 0, size, axis=axis)
        high = lax.slice_in_dim(value, size, 2 * size, axis=axis)
        return jnp.where(first, low, high) + self.other_core(jnp.where(first, high, low))

    def lockstep(self, *streams):
        results = [None] * len(streams)
        waiting = {}

        def advance(i, other):
            try:
                waiting[i] = streams[i].send(other)
            except StopIteration as stop:
                waiting.pop(i, None)
                results[i] = stop.value

        for i in range(len(streams)):
            advance(i, None)
        while waiting:
            names = list(waiting)
            over = [i for i in range(len(streams)) if i not in waiting]
            values, kept = together([waiting[i][0] for i in names], [results[i] for i in over])
            for i, result in zip(over, kept):
                results[i] = result
            masks = [waiting[i][1] for i in names]
            others = [v if m is None else self.exchange(v, m) for v, m in zip(values, masks)]
            for i, other in zip(names, others):
                advance(i, other)
        return together(*results)

    def gather_chips(self, value, order, state=()):
        done = list(state)
        for mask in self.bits(order):
            other = yield value, mask
            place = sum(m > mask for m in done)
            high = (self.chip // mask) % 2 == 1
            value = jnp.stack(
                [jnp.where(high, other, value), jnp.where(high, value, other)], axis=place
            )
            done.append(mask)
        if len(done) == len(self.bits((8, 4, 2, 1))):
            value = value.reshape((self.n,) + value.shape[len(done) :])
        return value

    def halves(self, value, mask, width):
        high = (self.chip // mask) % 2 == 1
        run = mask * width
        low_runs = [value[:, i : i + run] for i in range(0, self.n * width, 2 * run)]
        high_runs = [value[:, i : i + run] for i in range(run, self.n * width, 2 * run)]
        pairs = list(zip(low_runs, high_runs))
        keep = [jnp.where(high, h, l) for l, h in pairs]
        send = [jnp.where(high, l, h) for l, h in pairs]
        return jnp.concatenate(keep, axis=1), jnp.concatenate(send, axis=1)

    def scatter_chips(self, value, order, done=()):
        left = [m for m in sorted(self.bits((8, 4, 2, 1)), reverse=True) if m not in done]
        for mask in self.bits(order):
            place = left.index(mask)
            high = (self.chip // mask) % 2 == 1
            rest = value.shape[1:]
            split = value.reshape((2,) * len(left) + rest)
            lower = lax.index_in_dim(split, 0, place, keepdims=False)
            upper = lax.index_in_dim(split, 1, place, keepdims=False)
            keep = jnp.where(high, upper, lower)
            send = jnp.where(high, lower, upper)
            left.remove(mask)
            other = yield send.astype(BF16), mask
            value = keep.astype(F32) + other.astype(F32)
            if left:
                value = value.astype(BF16)
            value = value.reshape((2 ** len(left),) + rest)
        return value if left else value[0]

    def first_halves(self, rows, order):
        return self.halves(rows, self.bits(order)[0], rows.shape[1] // self.n)

    def weight_grad(self, rows, grads, order):
        mask = self.bits(order)[0]
        keep, send = rows
        away = inner_rows(send, grads).astype(BF16)
        other = yield away, mask
        value = inner_rows(keep, grads) + other.astype(F32)
        value = value.astype(BF16).reshape(self.n // 2, -1, grads.shape[1])
        return (yield from self.scatter_chips(value, order[1:], (mask,)))

    def gather_groups(self, value, states):
        for i, order in enumerate(ORDER_TOKENS):
            yield self.gather_tokens(value if i == 0 else None, i, order, states)

    def gather_tokens(self, value, i, order, states):
        if i == 0:
            states["rows"] = jnp.stack([value, (yield value, FIRST_TOKENS)])
        else:
            yield (), None
        start = sum(TOKEN_GROUPS[:i])
        value = states["rows"][:, start : start + TOKEN_GROUPS[i]]
        for mask in self.bits(order)[:-1]:
            other = yield value, mask
            value = jnp.concatenate([value, other], axis=0)
        return value

    def last_groups(self, groups):
        for value, order in zip(groups, ORDER_TOKENS):
            yield self.last_exchange(value, self.bits(order)[-1])

    def last_exchange(self, value, mask):
        return (yield value, mask)

    def scatter_groups(self, groups, others, states):
        for i, (value, other, order) in enumerate(zip(groups, others, ORDER_TOKENS)):
            yield self.scatter_tokens(value, other, i, order, states)

    def scatter_tokens(self, value, other, i, order, states):
        value = value.astype(F32) + other.astype(F32)
        for mask in reversed(self.bits(order)[:-1]):
            half = value.shape[0] // 2
            value = value.astype(BF16)
            received = yield value[half:], mask
            value = value[:half].astype(F32) + received.astype(F32)
        states[i] = value
        if i + 1 < len(TOKEN_GROUPS):
            yield (), None
            return ()
        value = jnp.concatenate([states[k] for k in range(len(TOKEN_GROUPS))], axis=1)
        received = yield value[1].astype(BF16), FIRST_TOKENS
        return value[0] + received.astype(F32)


def body(
    tokens,
    segments,
    routes,
    norm_attn,
    query_proj,
    latent_proj,
    norm_latent,
    expand_proj,
    output_proj,
    norm_ffn,
    router,
    shared_gate,
    shared_up,
    shared_down,
    expert_gate,
    expert_up,
    expert_down,
    cotangent,
):
    chips = Chips()
    n, cores, chip, core = chips.n, chips.f, chips.chip, chips.core
    seq = SEQ_DEV * cores
    heads = H // cores
    shard = D // (n * cores)
    expert_count = n * expert_gate.shape[0]
    small_cut = (shard, 2 * shard, 2 * shard + norm_latent.shape[0])

    tokens_seq = chips.gather_cores(tokens)
    small = jnp.concatenate([norm_attn, norm_ffn, norm_latent, router.reshape(-1)])
    query_own = chips.swap_cores(query_proj, 1, 0)
    query_cut = query_own.shape[1] // 2
    expand_own = chips.swap_cores(expand_proj, 1, 0)
    output_own = chips.swap_cores(output_proj, 1, 0)
    output_cut = output_own.shape[1] // 2
    width = shared_gate.shape[1] // n
    tiny = jnp.concatenate([chips.gather_cores(small[None]).reshape(-1), routes.astype(BF16).reshape(-1)])
    tiny_size = tiny.shape[0]
    columns = latent_proj.shape[1]
    tiny_rows = -(-tiny_size // columns)
    tiny = jnp.pad(tiny, (0, tiny_rows * columns - tiny_size)).reshape(tiny_rows, columns)
    latent_own = jnp.concatenate([latent_proj, tiny], axis=0)
    tokens_seq, query_own, expand_own, output_own, latent_own = together(
        tokens_seq, query_own, expand_own, output_own, latent_own
    )

    def shared_columns(*weights):
        weights = yield weights, None
        shared_in = jnp.stack([w.reshape(shard, n, -1) for w in weights], 2)
        shared_in = shared_in.transpose(1, 0, 2, 3).reshape(n * shard, 2 * width)
        for _ in range(3):
            shared_in = yield shared_in, None
        return lax.all_to_all(shared_in, "expert", split_axis=0, concat_axis=0, tiled=True)

    query_first, query_last, expand_weight, latent_own, shared_in = chips.lockstep(
        chips.gather_chips(query_own[:, :query_cut], ORDER_QUERY[0]),
        chips.gather_chips(query_own[:, query_cut:], ORDER_QUERY[1]),
        chips.gather_chips(expand_own, ORDER_EXPAND),
        chips.gather_chips(latent_own, ORDER_LATENT),
        shared_columns(shared_gate, shared_up),
    )
    (
        query_first, query_last, expand_weight, latent_own, shared_in, tokens_seq, output_own,
        cot_in,
    ) = together(
        query_first, query_last, expand_weight, latent_own, shared_in, tokens_seq, output_own,
        cotangent,
    )
    tiny = latent_own[:, shard:].reshape(n, -1)
    latent_own = latent_own[:, :shard]
    routes_all = tiny[:, cores * small.shape[0] : tiny_size].astype(jnp.int32)
    routes_all = routes_all.reshape(n, SEQ_DEV, TOPK)
    small = tiny[:, : cores * small.shape[0]].reshape(n * cores, -1)
    gain_attn = small[:, : small_cut[0]].reshape(-1).astype(F32)
    gain_ffn = small[:, small_cut[0] : small_cut[1]].reshape(-1).astype(F32)
    gain_latent = small[:, small_cut[1] : small_cut[2]].reshape(-1).astype(F32)
    query_parts = [query_first.reshape(D, -1), query_last.reshape(D, -1)]
    expand_weight = expand_weight.reshape(KVR, -1)
    latent_own_rows = latent_own.reshape(n * shard, -1)
    gate_full, up_full, down_full = (
        lax.all_gather(w[0], "fsdp", axis=0, tiled=True)
        for w in (expert_gate, expert_up, expert_down)
    )
    ff = gate_full.shape[1]

    def idle(rounds):
        for _ in range(rounds):
            yield (), None

    def shared_weights(value):
        value = yield value, None
        return lax.all_gather(
            value.reshape(n, 1, shard, 2 * width), "fsdp", axis=1, tiled=True
        ).reshape(D, 2 * width)

    outputs = {}

    def output_weights(part):
        if part == 0:
            value = yield from chips.gather_chips(output_own, ORDER_OUTPUT[0])
            outputs["first"] = value
        else:
            yield from idle(len(chips.bits(ORDER_OUTPUT[0])))
        value = outputs["first"][..., part * output_cut : (part + 1) * output_cut]
        order = chips.bits(ORDER_OUTPUT[1 + part])
        state = chips.bits(ORDER_OUTPUT[0])
        value = yield from chips.gather_chips(value, order[:-1], state)
        other = yield value, order[-1]
        return value, other

    half = n // 2

    extra = -(-(width + expert_count) // LANES) * LANES
    member_pad = (width + LANES - extra, extra - width - expert_count)

    def expert_members(routes_all):
        turns = []
        for last in (False, True):
            for order in ORDER_TOKENS:
                order = chips.bits((FIRST_TOKENS, *order))
                these = [0]
                for mask in order[:-1]:
                    these = these + [t ^ mask for t in these]
                turns += [t ^ order[-1] if last else t for t in these]
        blocks = routes_all.at[chip ^ jnp.array(turns, jnp.int32)].get(mode="promise_in_bounds")
        blocks = blocks.reshape(2, len(TOKEN_GROUPS), half, SEQ_DEV, TOPK)
        members = []
        for last in range(2):
            parts, start = [], 0
            for i, size in enumerate(TOKEN_GROUPS):
                parts.append(blocks[last, i, :, start : start + size].reshape(half * size, TOPK))
                start += size
            named = jnp.concatenate(parts, axis=0)[:, :, None]
            member = jnp.any(named == jnp.arange(expert_count, dtype=jnp.int32), axis=1)
            members.append(jnp.pad(member.astype(F32), ((0, 0), member_pad)))
        return members

    positions = jnp.arange(seq, dtype=jnp.int32)
    cos_table, sin_table = rope_tables(positions)
    inputs_f = tokens.astype(F32)
    score_scale = (DN + DR) ** (-0.5)

    def attention():
        rows = yield tokens_seq, None
        normed = rms_scale(rows.astype(F32), gain_attn).astype(BF16)
        normed_part = lax.dynamic_index_in_dim(
            normed.reshape(seq, n, cores, shard), core, 2, keepdims=False
        ).reshape(seq, n * shard)
        latent = chips.sum_cores(product(normed_part, latent_own_rows))
        query_all = jnp.concatenate([product(normed, part) for part in query_parts], axis=1)
        query_all = query_all.reshape(seq, heads, DN + DR)
        query_nope = query_all[..., :DN].astype(BF16)
        query_rope = rotate(
            query_all[..., DN:], cos_table[:, None, :], sin_table[:, None, :]
        ).astype(BF16)
        normed, normed_part, latent, query_nope, query_rope = yield (
            (normed, normed_part, latent, query_nope, query_rope),
            None,
        )
        latent_norm = rms_scale(latent[:, :KVR], gain_latent).astype(BF16)
        key_rope = rotate(latent[:, KVR:], cos_table, sin_table).astype(BF16)
        expanded = product(latent_norm, expand_weight).astype(BF16).reshape(seq, heads, DN + DV)
        key_nope = expanded[..., :DN]
        values_all = expanded[..., DN:]
        allowed = (positions[:, None] >= positions[None, :]) & (
            segments[:, None] == segments[None, :]
        )
        scores = jnp.einsum("thd,shd->hts", query_nope, key_nope, preferred_element_type=F32)
        scores = scores + jnp.einsum(
            "thd,sd->hts", query_rope, key_rope, preferred_element_type=F32
        )
        scores = jnp.where(allowed[None], scores * score_scale, -1e30)
        shifted = jnp.exp(scores - jnp.max(scores, axis=-1, keepdims=True))
        probs = shifted / jnp.sum(shifted, axis=-1, keepdims=True)
        latent_norm, key_rope, key_nope, values_all, probs = yield (
            (latent_norm, key_rope, key_nope, values_all, probs),
            None,
        )
        probs_low = probs.astype(BF16)
        attended = jnp.einsum("hts,shd->thd", probs_low, values_all, preferred_element_type=F32)
        attended = attended.reshape(seq, heads * DV).astype(BF16)
        attended = yield chips.gather_cores(attended, axis=1), None
        return (
            normed, normed_part, latent, query_nope, query_rope, latent_norm, key_rope, key_nope, values_all,
            probs, probs_low, attended,
        )

    def joined_output(parts):
        full = []
        for (own_part, other_part), order in zip(parts, ORDER_OUTPUT[1:]):
            mask = chips.bits(order)[-1]
            high = (chip // mask) % 2 == 1
            lower = jnp.where(high, other_part, own_part)
            upper = jnp.where(high, own_part, other_part)
            place = sum(m > mask for m in chips.bits((8, 4, 2, 1)))
            full.append(jnp.stack([lower, upper], axis=place).reshape(D, -1))
        return full

    def late_members(routes_all):
        yield from idle(3)
        routes_all = yield routes_all, None
        return expert_members(routes_all)

    states = {}
    *output_parts, kept_attention, shared_in, members, cot_zero, cot_one, cot_two = chips.lockstep(
        output_weights(0),
        output_weights(1),
        attention(),
        shared_weights(shared_in),
        late_members(routes_all),
        *chips.gather_groups(cot_in, states),
    )
    cot_first = [cot_zero, cot_one, cot_two]
    (
        normed, normed_part, latent, query_nope, query_rope, latent_norm, key_rope, key_nope, values_all,
        probs, probs_low, attended,
    ) = kept_attention
    hidden = []
    for (own_part, other_part), order in zip(output_parts, ORDER_OUTPUT[1:]):
        keep, send = chips.halves(attended, chips.bits(order)[-1], D // n)
        part = product(keep, own_part.reshape(D // 2, -1))
        hidden.append(part + product(send, other_part.reshape(D // 2, -1)))
    hidden = inputs_f + chips.swap_cores(jnp.concatenate(hidden, axis=1), 0, 1)
    normed_ffn = rms_scale(hidden, gain_ffn).astype(BF16)

    def beside(function, *values):
        values = yield values, None
        return function(*values)

    own = (jnp.arange(expert_count, dtype=jnp.int32) == chip).astype(F32)
    own = jnp.pad(own, member_pad)[None]

    def flat(groups):
        return [v.reshape(-1, D) for v in groups]

    def blocks(groups):
        return [v.reshape(half, -1, D) for v in groups]

    def forward(groups, member):
        rows = flat(groups)
        out, (logits, gate_act, up_act, hidden_act) = expert_forward(rows, member, own, weights)
        return blocks(out), (rows, logits, gate_act, up_act, hidden_act)

    def backward(kept, groups, member):
        _, logits, gate_act, up_act, _ = kept
        cot = flat(groups)
        back, (gate_back, up_back) = expert_backward(
            cot, member, own, logits, gate_act, up_act, weights
        )
        return blocks(back), (cot, gate_back, up_back)

    def extra_weights(shared_in, router_all, shared_down_own):
        gate_extra = jnp.concatenate([shared_in[:, :width], router_all], axis=1)
        gate_extra = jnp.pad(gate_extra, ((0, 0), (0, extra - width - expert_count)))
        up_extra = jnp.pad(shared_in[:, width:], ((0, 0), (0, extra - width)))
        down_extra = jnp.pad(chips.gather_cores(shared_down_own), ((0, extra - width), (0, 0)))
        return gate_full, gate_extra, up_full, up_extra, down_full, down_extra

    def backward_halves(attended, normed, latent_norm, normed_part):
        return (
            [chips.first_halves(attended, order) for order in BACK_OUTPUT[:2]],
            [chips.first_halves(normed, order) for order in BACK_QUERY],
            chips.first_halves(latent_norm, BACK_EXPAND),
            chips.first_halves(normed_part, BACK_LATENT),
        )

    *rows_first, halves, output_full, weights = chips.lockstep(
        *chips.gather_groups(normed_ffn, {}),
        beside(backward_halves, attended, normed, latent_norm, normed_part),
        beside(lambda *parts: joined_output(parts), *output_parts),
        beside(extra_weights, shared_in, small[:, small_cut[2] :].reshape(D, -1), shared_down),
    )
    attended_halves, normed_halves, latent_halves, normed_part_halves = halves
    *rows_last, (out_first, kept_first) = chips.lockstep(
        *chips.last_groups(rows_first), beside(forward, rows_first, members[0])
    )
    cot_first, rows_last = together(cot_first, rows_last)
    *cot_last, (out_last, kept_last) = chips.lockstep(
        *chips.last_groups(cot_first), beside(forward, rows_last, members[1])
    )
    *sent_out, (back_last, grads_last) = chips.lockstep(
        *chips.last_groups(out_last), beside(backward, kept_last, cot_last, members[1])
    )
    *sent_back, (back_first, grads_first) = chips.lockstep(
        *chips.last_groups(back_last), beside(backward, kept_first, cot_first, members[0])
    )

    def down_grads(hidden_acts, cots):
        yield from idle(2)
        hidden_acts, cots = yield (hidden_acts, cots), None
        return down_weights(hidden_acts, [v for groups in cots for v in groups], ff)

    *_, ffn_grad, (down_w, down_extra_w) = chips.lockstep(
        *chips.scatter_groups(back_first, sent_back, {}),
        down_grads((kept_first[4], kept_last[4]), (grads_first[0], grads_last[0])),
    )

    middle = {}

    def through_norm(ffn_grad):
        ffn_grad = yield ffn_grad, None
        _, norm_pull = jax.vjp(rms_scale, hidden, gain_ffn)
        hidden_part, gain_ffn_grad = norm_pull(ffn_grad)
        hidden_grad = cotangent.astype(F32) + hidden_part
        middle["attn_grad"] = chips.swap_cores(hidden_grad.astype(BF16), 1, 0)
        middle["hidden_grad"], middle["gain"] = yield (hidden_grad, gain_ffn_grad), None
        return middle["hidden_grad"], middle["gain"]

    def output_grads(part):
        yield from idle(1)
        grads = middle["attn_grad"][:, part * output_cut : (part + 1) * output_cut]
        order = chips.bits(BACK_OUTPUT[part])
        value = yield from chips.weight_grad(attended_halves[part], grads, order)
        middle["output", part] = value
        if part == 0:
            yield from idle(2)
            return ()
        value = jnp.concatenate([middle["output", 0], value], axis=-1)
        return (yield from chips.scatter_chips(value, BACK_OUTPUT[2], order))

    def in_grads(rows, gate_back, up_back):
        rows = [v for groups in rows for v in groups]
        yield from idle(2)
        rows, gate_back = yield (rows, gate_back), None
        gate_w, gate_x = yield in_weights(rows, gate_back, ff), None
        middle["router_grad"] = gate_x[:, width : width + expert_count]
        gate_w = lax.psum_scatter(gate_w, "fsdp", scatter_dimension=0, tiled=True)
        rows, up_back = together(rows, up_back, gate_x)[:2]
        up_w, up_x = in_weights(rows, up_back, ff)
        gate_w, up_w, gate_x, up_x = yield (gate_w, up_w, gate_x, up_x), None
        gate_w = gate_w.astype(F32)[None]
        up_w = lax.psum_scatter(up_w, "fsdp", scatter_dimension=0, tiled=True)
        shared = jnp.concatenate([gate_x[:, :width], up_x[:, :width]], axis=1)
        shared = chips.scatter_cores(shared.reshape(n, cores * shard, 2 * width), 1)
        shared = yield shared, None
        shared = lax.all_to_all(shared, "expert", split_axis=0, concat_axis=0, tiled=True)
        shared, up_w = yield (shared, up_w), None
        shared = shared.astype(F32).reshape(n, shard, 2, width).transpose(2, 1, 0, 3)
        return (gate_w, up_w.astype(F32)[None]), shared.reshape(2, shard, n * width)

    def second_grads(down_w, down_extra_w):
        down_w, down_extra_w = yield (down_w, down_extra_w), None
        down_w = lax.psum_scatter(down_w, "fsdp", scatter_dimension=0, tiled=True)
        down_extra_w = chips.scatter_cores(down_extra_w[:width])
        down_w, down_extra_w = yield (down_w, down_extra_w), None
        yield from idle(1)
        down_w = yield down_w, None
        return down_w.astype(F32)[None], down_extra_w

    def attention_back():
        yield (), None
        attn_grad = middle["attn_grad"]
        attended_grad = outer_cols(attn_grad[:, :output_cut], output_full[0]) + outer_cols(
            attn_grad[:, output_cut:], output_full[1]
        )
        attended_grad = yield chips.scatter_cores(attended_grad, 1).astype(BF16), None
        attended_grad = attended_grad.reshape(seq, heads, DV)
        prob_grad = jnp.einsum("thd,shd->hts", attended_grad, values_all, preferred_element_type=F32)
        weighted = jnp.sum(probs * prob_grad, axis=-1, keepdims=True)
        score_grad = (probs * (prob_grad - weighted)).astype(BF16)
        query_nope_grad = score_scale * jnp.einsum(
            "hts,shd->thd", score_grad, key_nope, preferred_element_type=F32
        )
        query_rope_grad = score_scale * jnp.einsum(
            "hts,sd->thd", score_grad, key_rope, preferred_element_type=F32
        )
        key_nope_grad = score_scale * jnp.einsum(
            "hts,thd->shd", score_grad, query_nope, preferred_element_type=F32
        )
        key_rope_grad = score_scale * jnp.einsum(
            "hts,thd->sd", score_grad, query_rope, preferred_element_type=F32
        )
        values_grad = jnp.einsum(
            "hts,thd->shd", probs_low, attended_grad, preferred_element_type=F32
        )
        (query_nope_grad, query_rope_grad, key_nope_grad, key_rope_grad, values_grad) = yield (
            (query_nope_grad, query_rope_grad, key_nope_grad, key_rope_grad, values_grad),
            None,
        )
        expanded_grad = jnp.concatenate([key_nope_grad, values_grad], axis=2)
        expanded_grad = expanded_grad.reshape(seq, heads * (DN + DV)).astype(BF16)
        latent_back = chips.sum_cores(
            jnp.concatenate([outer_cols(expanded_grad, expand_weight), key_rope_grad], axis=1)
        )
        _, latent_pull = jax.vjp(rms_scale, latent[:, :KVR], gain_latent)
        latent_nope_grad, gain_latent_grad = latent_pull(latent_back[:, :KVR])
        gain_latent_grad = gain_latent_grad / cores
        latent_rope_grad = rotate(latent_back[:, KVR:], cos_table, -sin_table)
        latent_grad = jnp.concatenate([latent_nope_grad, latent_rope_grad], axis=1).astype(BF16)
        query_back = jnp.concatenate(
            [query_nope_grad, rotate(query_rope_grad, cos_table[:, None, :], -sin_table[:, None, :])],
            axis=2,
        )
        query_back = query_back.reshape(seq, heads * (DN + DR)).astype(BF16)
        middle["query_back"] = query_back
        middle["expanded_grad"] = expanded_grad
        middle["latent_grad"] = latent_grad
        middle["gain_latent_grad"] = gain_latent_grad
        yield (query_back, expanded_grad, latent_grad), None

    def projection_grads(rows, name, columns, order):
        yield from idle(3)
        return (yield from chips.weight_grad(rows, middle[name][:, columns], order))

    back_cut = heads * (DN + DR) * 5 // 12 // LANES * LANES

    def input_grads():
        yield from idle(4)
        query_back, latent_grad = yield (middle["query_back"], middle["latent_grad"]), None
        normed_grad = outer_cols(query_back[:, :query_cut], query_parts[0]) + outer_cols(
            query_back[:, query_cut:], query_parts[1]
        )
        normed_grad, latent_grad, latent_rows = yield (normed_grad, latent_grad, latent_own), None
        latent_weight = chips.gather_cores(latent_rows[:, None], axis=1).reshape(D, -1)
        latent_grad_own = lax.dynamic_slice_in_dim(latent_grad, core * SEQ_DEV, SEQ_DEV, 0)
        normed_grad = chips.scatter_cores(normed_grad) + outer_cols(latent_grad_own, latent_weight)
        _, first_pull = jax.vjp(rms_scale, inputs_f, gain_attn)
        input_part, gain_attn_grad = first_pull(normed_grad)
        tokens_grad = (middle["hidden_grad"] + input_part).astype(BF16)
        tokens_grad, gain_attn_grad = yield (tokens_grad, gain_attn_grad), None
        small_grad = jnp.concatenate(
            [
                gain_attn_grad.reshape(n * cores, -1),
                middle["gain"].reshape(n * cores, -1),
                middle["gain_latent_grad"].reshape(n * cores, -1),
                middle["router_grad"].astype(F32).reshape(n * cores, -1),
            ],
            axis=1,
        )
        small_grad = lax.all_to_all(
            small_grad.reshape(n, -1), "expert", split_axis=0, concat_axis=0, tiled=True
        )
        small_grad = jnp.sum(small_grad, axis=0).reshape(cores, -1)
        return tokens_grad, chips.scatter_cores(small_grad).reshape(-1)

    (
        _, _, _, block_sum, _, _, output_grad, query_first_grad, query_last_grad, expand_grad,
        latent_weight_grad, in_grad, second_grad, input_grad,
    ) = chips.lockstep(
        through_norm(ffn_grad),
        *chips.scatter_groups(out_first, sent_out, {}),
        attention_back(),
        output_grads(0),
        output_grads(1),
        projection_grads(normed_halves[0], "query_back", slice(0, back_cut), BACK_QUERY[0]),
        projection_grads(normed_halves[1], "query_back", slice(back_cut, None), BACK_QUERY[1]),
        projection_grads(latent_halves, "expanded_grad", slice(None), BACK_EXPAND),
        projection_grads(normed_part_halves, "latent_grad", slice(None), BACK_LATENT),
        in_grads(
            (kept_first[0], kept_last[0]),
            (grads_first[1], grads_last[1]),
            (grads_first[2], grads_last[2]),
        ),
        second_grads(down_w, down_extra_w),
        input_grads(),
    )
    (gate_grad_w, up_grad_w), shared_in_grad = in_grad
    down_grad_w, shared_down_grad = second_grad
    tokens_grad, small_grad = input_grad
    block_out = (hidden + block_sum).astype(BF16)
    output_grad = chips.swap_cores(output_grad, 0, 1)
    query_grad = jnp.concatenate([query_first_grad, query_last_grad], axis=1)
    query_grad = chips.swap_cores(query_grad, 0, 1)
    expand_grad = chips.swap_cores(expand_grad, 0, 1)
    return (
        block_out,
        tokens_grad,
        small_grad[: small_cut[0]],
        query_grad,
        latent_weight_grad,
        small_grad[small_cut[1] : small_cut[2]],
        expand_grad,
        output_grad,
        small_grad[small_cut[0] : small_cut[1]],
        small_grad[small_cut[2] :].reshape(shard, -1),
        shared_in_grad[0],
        shared_in_grad[1],
        shared_down_grad,
        gate_grad_w,
        up_grad_w,
        down_grad_w,
    )


def solution(mesh):
    rows = P(("expert", "fsdp"), None)
    flat = P(("expert", "fsdp"))
    experts = P("expert", "fsdp", None)
    return jax.shard_map(
        body,
        mesh=mesh,
        in_specs=(
            rows, P("expert"), rows, flat, rows, rows, flat, rows, rows, flat, rows, rows, rows,
            rows, experts, experts, experts, rows,
        ),
        out_specs=(
            rows, rows, flat, rows, rows, flat, rows, rows, flat, rows, rows, rows, rows, experts,
            experts, experts,
        ),
        check_vma=False,
    )
```

```python
import math

import jax
import jax.numpy as jnp
from jax import lax
from jax.experimental import pallas as pl
from jax.experimental.pallas import tpu as pltpu
from jax.sharding import PartitionSpec as P

D = 2048
H = 16
DN = 128
DR = 64
DV = 128
KVR = 512
TOPK = 6
SEQ_DEV = 128

NORM_EPS = 1e-06
ROPE_THETA = 50000.0
GATE_SCALE = 2.446

BF16 = jnp.bfloat16
F32 = jnp.float32
BOTH = ("expert", "fsdp")

ORDER_QUERY = ((8, 4, 1, 2), (8, 2, 4, 1))
ORDER_EXPAND = (8, 1, 2, 4)
ORDER_LATENT = (8, 1, 2, 4)
ORDER_OUTPUT = ((8, 2), (1, 4), (4, 1))
TOKEN_GROUPS = (48, 48, 32)
ORDER_TOKENS = ((2, 1, 4), (1, 4, 2), (4, 2, 1))
FIRST_TOKENS = 8
BACK_QUERY = ((1, 4, 2, 8), (4, 2, 1, 8))
BACK_EXPAND = (2, 1, 4, 8)
BACK_LATENT = (2, 1, 4, 8)
BACK_OUTPUT = ((4, 2), (2, 4), (1, 8))


def rms_scale(values, gain_vec):
    return (
        values * lax.rsqrt(jnp.mean(values * values, axis=-1, keepdims=True) + NORM_EPS) * gain_vec
    )


def rotate(values, cos_table, sin_table):
    middle = values.shape[-1] // 2
    lower_half = values[..., :middle]
    upper_half = values[..., middle:]
    return jnp.concatenate(
        [
            lower_half * cos_table - upper_half * sin_table,
            upper_half * cos_table + lower_half * sin_table,
        ],
        axis=-1,
    )


def rope_tables(positions):
    steps_float = jnp.arange(DR // 2).astype(F32) * (2.0 / DR)
    inverse = jnp.exp(-steps_float * math.log(ROPE_THETA))
    turned = positions.astype(F32)[:, None] * inverse[None, :]
    return (jnp.cos(turned), jnp.sin(turned))


def product(left_side, right_side):
    return jnp.dot(left_side, right_side, preferred_element_type=F32)


def inner_rows(left_side, right_side):
    return lax.dot_general(
        left_side, right_side, (((0,), (0,)), ((), ())), preferred_element_type=F32
    )


def outer_cols(left_side, right_side):
    return lax.dot_general(
        left_side, right_side, (((1,), (1,)), ((), ())), preferred_element_type=F32
    )


def together(*values):
    return lax.optimization_barrier(values)


def swiglu(gate_act, up_act):
    return jax.nn.silu(gate_act) * up_act


WIDE = 512
LANES = 128
VMEM_BYTES = 60 * 2**20


def whole_in_vmem():
    return pl.BlockSpec(memory_space=pltpu.VMEM)


def spans(size):
    return [(start, min(WIDE, size - start)) for start in range(0, size, WIDE)]


def weight_copies(in_hbm, down_hbm, in_refs, down_ref, sems):
    ff = in_hbm[0].shape[1]
    count = 0
    by_span = [[] for _ in spans(down_ref.shape[0])]

    def copy(source, target):
        nonlocal count
        count += 1
        return pltpu.make_async_copy(source, target, sems.at[count - 1])

    for extra, joined in zip(in_hbm[1::2], in_refs):
        by_span[-1].append(copy(extra, joined.at[:, pl.ds(ff, extra.shape[1])]))
    for k, (start, size) in enumerate(spans(ff)):
        for expert, joined in zip(in_hbm[0::2], in_refs):
            there = pl.ds(start, size)
            by_span[k].append(copy(expert.at[:, there], joined.at[:, there]))
    down = [
        copy(down_hbm[0], down_ref.at[pl.ds(0, ff), :]),
        copy(down_hbm[1], down_ref.at[pl.ds(ff, down_hbm[1].shape[0]), :]),
    ]
    return by_span, down


def gated(gate, start, size, ff):
    units = lax.broadcasted_iota(jnp.int32, (1, size), 1) + start
    return jnp.where(units < ff, gate, 1.0)


def row_groups(refs):
    start = 0
    for ref in refs:
        yield ref, pl.ds(start, ref.shape[0])
        start += ref.shape[0]


def forward_kernel(*refs):
    groups = len(TOKEN_GROUPS)
    rows_refs = refs[:groups]
    member_ref, own_ref, gate_w, gate_x, up_w, up_x, down_w, down_x = refs[groups : groups + 8]
    out_refs = refs[groups + 8 : 2 * groups + 8]
    logits_ref, gate_act_ref, up_act_ref, hidden_ref = refs[2 * groups + 8 : 2 * groups + 12]
    gate_all, up_all, down_all, sems = refs[2 * groups + 12 :]
    by_span, down = weight_copies(
        (gate_w, gate_x, up_w, up_x), (down_w, down_x), (gate_all, up_all), down_all, sems
    )
    for copy in by_span[-1] + sum(by_span[:-1], []) + down:
        copy.start()
    ff, units = gate_w.shape[1], down_all.shape[0]
    width = down_all.shape[1]
    order = list(zip(spans(units), by_span))
    order = order[-1:] + order[:-1]
    for rows_ref, here in row_groups(rows_refs):
        first = here.start == 0
        for k, ((start, size), copies) in enumerate(order):
            there = pl.ds(start, size)
            if first:
                for copy in copies:
                    copy.wait()
            gate_act = product(rows_ref[...], gate_all[:, there])
            up_act = product(rows_ref[...], up_all[:, there])
            if k == 0:
                logits_ref[here, :] = gate_act
                chosen = member_ref[here, :] / (1.0 + jnp.exp(-gate_act))
                own = jnp.sum(chosen * own_ref[...], axis=1, keepdims=True)
                gate = GATE_SCALE * own / jnp.sum(chosen, axis=1, keepdims=True)
            gate_act_ref[here, there] = gate_act.astype(BF16)
            up_act_ref[here, there] = up_act.astype(BF16)
            hidden = swiglu(gate_act, up_act) * gated(gate, start, size, ff)
            hidden_ref[here, there] = hidden.astype(BF16)
    for copy in down:
        copy.wait()
    for out_ref, here in row_groups(out_refs):
        for start, size in spans(width):
            there = pl.ds(start, size)
            out_ref[:, there] = product(hidden_ref[here, :], down_all[:, there]).astype(BF16)


def backward_kernel(*refs):
    groups = len(TOKEN_GROUPS)
    cot_refs = refs[:groups]
    member_ref, own_ref, logits_ref, gate_act_ref, up_act_ref = refs[groups : groups + 5]
    gate_w, gate_x, up_w, up_x, down_w, down_x = refs[groups + 5 : groups + 11]
    back_refs = refs[groups + 11 : 2 * groups + 11]
    gate_back_ref, up_back_ref, gate_all, up_all, down_all, sems = refs[2 * groups + 11 :]
    by_span, down = weight_copies(
        (gate_w, gate_x, up_w, up_x), (down_w, down_x), (gate_all, up_all), down_all, sems
    )
    for copy in down + sum(by_span, []):
        copy.start()
    ff, units = gate_w.shape[1], down_all.shape[0]
    width = down_all.shape[1]
    for copy in down:
        copy.wait()
    for cot_ref, here in row_groups(cot_refs):
        sigmoid = 1.0 / (1.0 + jnp.exp(-logits_ref[here, :]))
        chosen = member_ref[here, :] * sigmoid
        own = jnp.sum(chosen * own_ref[...], axis=1, keepdims=True)
        all_chosen = jnp.sum(chosen, axis=1, keepdims=True)
        gate = GATE_SCALE * own / all_chosen
        gate_grad = jnp.zeros_like(gate)
        for start, size in spans(units):
            there = pl.ds(start, size)
            last = start + size == units
            hidden_back = outer_cols(cot_ref[...], down_all[there, :])
            gate_act = gate_act_ref[here, there].astype(F32)
            up_act = up_act_ref[here, there].astype(F32)
            sig = 1.0 / (1.0 + jnp.exp(-gate_act))
            silu = gate_act * sig
            column = lax.broadcasted_iota(jnp.int32, (1, size), 1) + start
            term = jnp.where(column < ff, silu * up_act * hidden_back, 0.0)
            gate_grad = gate_grad + jnp.sum(term, axis=1, keepdims=True)
            scaled = hidden_back * gated(gate, start, size, ff)
            up_back_ref[here, there] = (scaled * silu).astype(BF16)
            gate_back = scaled * up_act * (sig + silu * (1.0 - sig))
            if last:
                named = jnp.sum(member_ref[here, :] * own_ref[...], axis=1, keepdims=True)
                logit_back = GATE_SCALE * named * gate_grad * chosen * (1.0 - sigmoid)
                logit_back = logit_back * (own_ref[...] - own / all_chosen) / all_chosen
                gate_back = jnp.where(member_ref[here, :] > 0.0, logit_back, gate_back)
            gate_back_ref[here, there] = gate_back.astype(BF16)
    for copy in sum(by_span, []):
        copy.wait()
    for back_ref, here in row_groups(back_refs):
        for start, size in spans(width):
            there = pl.ds(start, size)
            back = outer_cols(gate_back_ref[here, :], gate_all[there, :])
            back = back + outer_cols(up_back_ref[here, :], up_all[there, :])
            back_ref[:, there] = back.astype(BF16)


def expert_call(kernel, out_shapes, arrays, weights):
    width, ff = weights[0].shape
    units = ff + weights[1].shape[1]
    tokens = sum(rows.shape[0] for rows in arrays[: len(TOKEN_GROUPS)])
    return pl.pallas_call(
        kernel,
        out_shape=out_shapes,
        in_specs=[whole_in_vmem() for _ in arrays]
        + [pl.BlockSpec(memory_space=pl.ANY) for _ in weights],
        out_specs=[whole_in_vmem() for _ in out_shapes],
        scratch_shapes=[
            pltpu.VMEM((width, units), BF16),
            pltpu.VMEM((width, units), BF16),
            pltpu.VMEM((units, width), BF16),
            pltpu.SemaphoreType.DMA((2 * len(spans(ff)) + 4,)),
        ],
        compiler_params=pltpu.CompilerParams(vmem_limit_bytes=VMEM_BYTES),
        cost_estimate=pl.CostEstimate(
            flops=6 * tokens * width * units,
            bytes_accessed=6 * width * units + 12 * tokens * width,
            transcendentals=tokens * units,
        ),
    )(*arrays, *weights)


def expert_forward(rows, member, own, weights):
    tokens = member.shape[0]
    units = weights[0].shape[1] + weights[1].shape[1]
    shapes = [jax.ShapeDtypeStruct(v.shape, BF16) for v in rows]
    shapes.append(jax.ShapeDtypeStruct(member.shape, F32))
    shapes += [jax.ShapeDtypeStruct((tokens, units), BF16)] * 3
    results = expert_call(forward_kernel, shapes, (*rows, member, own), weights)
    return results[: len(rows)], results[len(rows) :]


def expert_backward(cot, member, own, logits, gate_act, up_act, weights):
    shapes = [jax.ShapeDtypeStruct(v.shape, BF16) for v in cot]
    shapes += [jax.ShapeDtypeStruct(gate_act.shape, BF16)] * 2
    results = expert_call(
        backward_kernel, shapes, (*cot, member, own, logits, gate_act, up_act), weights
    )
    return results[: len(cot)], results[len(cot) :]


def in_weights_kernel(*refs):
    groups = 2 * len(TOKEN_GROUPS)
    rows, (first, last) = refs[:groups], refs[groups : groups + 2]
    out, extra_out, turned = refs[-3:]
    for ref, here in row_groups(rows):
        turned[:, here] = ref[...].T
    tokens = first.shape[0]
    for ref, begin in ((out, 0), (extra_out, out.shape[1])):
        for start, size in spans(ref.shape[1]):
            there = pl.ds(begin + start, size)
            value = product(turned[:, pl.ds(0, tokens)], first[:, there])
            value = value + product(turned[:, pl.ds(tokens, tokens)], last[:, there])
            ref[:, pl.ds(start, size)] = value.astype(ref.dtype)


def in_weights(rows, acts_back, ff, part, earlier=()):
    tokens, units = acts_back[0].shape
    width = rows[0].shape[1]
    first_step, steps = 0, width // WIDE
    if part is not None:
        steps = steps // 2
        first_step = part * steps
    whole = pl.BlockSpec((tokens, units), lambda i: (0, 0), pipeline_mode=pl.Buffered(1))
    outs = [((width, ff), BF16), ((width, units - ff), BF16)]
    given = len(rows) + 2
    return pl.pallas_call(
        in_weights_kernel,
        grid=(steps,),
        out_shape=[jax.ShapeDtypeStruct(*out) for out in outs],
        in_specs=[pl.BlockSpec((v.shape[0], WIDE), lambda i: (0, i + first_step)) for v in rows]
        + [whole] * 2
        + [pl.BlockSpec(memory_space=pl.ANY) for _ in earlier],
        out_specs=[pl.BlockSpec((WIDE, shape[1]), lambda i: (i + first_step, 0)) for shape, _ in outs],
        scratch_shapes=[pltpu.VMEM((WIDE, 2 * tokens), BF16)],
        input_output_aliases={given + k: k for k in range(len(earlier))},
        compiler_params=pltpu.CompilerParams(vmem_limit_bytes=VMEM_BYTES),
        cost_estimate=pl.CostEstimate(
            flops=2 * tokens * width * units,
            bytes_accessed=4 * tokens * (width + units) + width * units,
            transcendentals=0,
        ),
    )(*rows, *acts_back, *earlier)


def down_weights_kernel(hidden_first, hidden_last, *refs):
    groups = 2 * len(TOKEN_GROUPS)
    cot, (out, extra_out), turned = refs[:groups], refs[groups : groups + 2], refs[-1]
    tokens = hidden_first.shape[0]

    @pl.when(pl.program_id(0) == 0)
    def _():
        turned[:, pl.ds(0, tokens)] = hidden_first[...].T
        turned[:, pl.ds(tokens, tokens)] = hidden_last[...].T

    for ref, begin in ((out, 0), (extra_out, out.shape[0])):
        for start, size in spans(ref.shape[0]):
            there = pl.ds(begin + start, size)
            value = sum(product(turned[there, here], group[...]) for group, here in row_groups(cot))
            ref[pl.ds(start, size), :] = value.astype(ref.dtype)


def down_weights(hidden, cot, ff):
    tokens, units = hidden[0].shape
    width = cot[0].shape[1]
    whole = pl.BlockSpec((tokens, units), lambda i: (0, 0), pipeline_mode=pl.Buffered(1))
    outs = [((ff, width), BF16), ((units - ff, width), F32)]
    return pl.pallas_call(
        down_weights_kernel,
        grid=(width // WIDE,),
        out_shape=[jax.ShapeDtypeStruct(*out) for out in outs],
        in_specs=[whole] * 2 + [pl.BlockSpec((v.shape[0], WIDE), lambda i: (0, i)) for v in cot],
        out_specs=[pl.BlockSpec((shape[0], WIDE), lambda i: (0, i)) for shape, _ in outs],
        scratch_shapes=[pltpu.VMEM((units, 2 * tokens), BF16)],
        compiler_params=pltpu.CompilerParams(vmem_limit_bytes=VMEM_BYTES),
        cost_estimate=pl.CostEstimate(
            flops=4 * tokens * width * units,
            bytes_accessed=4 * tokens * (width + units) + 2 * width * units,
            transcendentals=0,
        ),
    )(*hidden, *cot)


class Chips:
    def __init__(self):
        self.n = lax.axis_size("expert")
        self.f = lax.axis_size("fsdp")
        self.chip = lax.axis_index("expert")
        self.core = lax.axis_index("fsdp")

    def bits(self, order):
        return tuple(m for m in order if (m if isinstance(m, int) else m[0]) < self.n)

    def exchange(self, value, mask):
        masks = (mask,) if isinstance(mask, int) else mask
        pairs = [
            (e * self.f + c, (e ^ masks[c % len(masks)]) * self.f + c)
            for e in range(self.n)
            for c in range(self.f)
        ]
        return lax.ppermute(value, BOTH, pairs)

    def other_core(self, value):
        return lax.ppermute(value, "fsdp", [(0, 1), (1, 0)])

    def gather_cores(self, value, axis=0):
        if self.f != 2:
            return lax.all_gather(value, "fsdp", axis=axis, tiled=True)
        other = self.other_core(value)
        first = self.core == 0
        return jnp.concatenate(
            [jnp.where(first, value, other), jnp.where(first, other, value)], axis=axis
        )

    def swap_cores(self, value, split, concat):
        if self.f != 2:
            return lax.all_to_all(value, "fsdp", split_axis=split, concat_axis=concat, tiled=True)
        size = value.shape[split] // 2
        first = self.core == 0
        low = lax.slice_in_dim(value, 0, size, axis=split)
        high = lax.slice_in_dim(value, size, 2 * size, axis=split)
        keep = jnp.where(first, low, high)
        other = self.other_core(jnp.where(first, high, low))
        return jnp.concatenate(
            [jnp.where(first, keep, other), jnp.where(first, other, keep)], axis=concat
        )

    def sum_cores(self, value):
        if self.f != 2:
            return lax.psum(value, "fsdp")
        return value + self.other_core(value)

    def scatter_cores(self, value, axis=0):
        if self.f != 2:
            return lax.psum_scatter(value, "fsdp", scatter_dimension=axis, tiled=True)
        size = value.shape[axis] // 2
        first = self.core == 0
        low = lax.slice_in_dim(value, 0, size, axis=axis)
        high = lax.slice_in_dim(value, size, 2 * size, axis=axis)
        return jnp.where(first, low, high) + self.other_core(jnp.where(first, high, low))

    def lockstep(self, *streams):
        results = [None] * len(streams)
        waiting = {}

        def advance(i, other):
            try:
                waiting[i] = streams[i].send(other)
            except StopIteration as stop:
                waiting.pop(i, None)
                results[i] = stop.value

        for i in range(len(streams)):
            advance(i, None)
        while waiting:
            names = list(waiting)
            over = [i for i in range(len(streams)) if i not in waiting]
            values, kept = together([waiting[i][0] for i in names], [results[i] for i in over])
            for i, result in zip(over, kept):
                results[i] = result
            masks = [waiting[i][1] for i in names]
            others = [v if m is None else self.exchange(v, m) for v, m in zip(values, masks)]
            for i, other in zip(names, others):
                advance(i, other)
        return together(*results)

    def gather_chips(self, value, order, state=()):
        done = list(state)
        for mask in self.bits(order):
            other = yield value, mask
            place = sum(m > mask for m in done)
            high = (self.chip // mask) % 2 == 1
            value = jnp.stack(
                [jnp.where(high, other, value), jnp.where(high, value, other)], axis=place
            )
            done.append(mask)
        if len(done) == len(self.bits((8, 4, 2, 1))):
            value = value.reshape((self.n,) + value.shape[len(done) :])
        return value

    def halves(self, value, mask, width):
        high = (self.chip // mask) % 2 == 1
        run = mask * width
        low_runs = [value[:, i : i + run] for i in range(0, self.n * width, 2 * run)]
        high_runs = [value[:, i : i + run] for i in range(run, self.n * width, 2 * run)]
        pairs = list(zip(low_runs, high_runs))
        keep = [jnp.where(high, h, l) for l, h in pairs]
        send = [jnp.where(high, l, h) for l, h in pairs]
        return jnp.concatenate(keep, axis=1), jnp.concatenate(send, axis=1)

    def scatter_chips(self, value, order, done=()):
        left = [m for m in sorted(self.bits((8, 4, 2, 1)), reverse=True) if m not in done]
        for mask in self.bits(order):
            place = left.index(mask)
            high = (self.chip // mask) % 2 == 1
            rest = value.shape[1:]
            split = value.reshape((2,) * len(left) + rest)
            lower = lax.index_in_dim(split, 0, place, keepdims=False)
            upper = lax.index_in_dim(split, 1, place, keepdims=False)
            keep = jnp.where(high, upper, lower)
            send = jnp.where(high, lower, upper)
            left.remove(mask)
            other = yield send.astype(BF16), mask
            value = keep.astype(F32) + other.astype(F32)
            if left:
                value = value.astype(BF16)
            value = value.reshape((2 ** len(left),) + rest)
        return value if left else value[0]

    def first_halves(self, rows, order):
        return self.halves(rows, self.bits(order)[0], rows.shape[1] // self.n)

    def weight_grad(self, rows, grads, order):
        mask = self.bits(order)[0]
        keep, send = rows
        away = inner_rows(send, grads).astype(BF16)
        other = yield away, mask
        value = inner_rows(keep, grads) + other.astype(F32)
        value = value.astype(BF16).reshape(self.n // 2, -1, grads.shape[1])
        return (yield from self.scatter_chips(value, order[1:], (mask,)))

    def gather_groups(self, value, states):
        for i, order in enumerate(ORDER_TOKENS):
            yield self.gather_tokens(value if i == 0 else None, i, order, states)

    def gather_tokens(self, value, i, order, states):
        if i == 0:
            states["rows"] = jnp.stack([value, (yield value, FIRST_TOKENS)])
        else:
            yield (), None
        start = sum(TOKEN_GROUPS[:i])
        value = states["rows"][:, start : start + TOKEN_GROUPS[i]]
        for mask in self.bits(order)[:-1]:
            other = yield value, mask
            value = jnp.concatenate([value, other], axis=0)
        return value

    def last_groups(self, groups):
        for value, order in zip(groups, ORDER_TOKENS):
            yield self.last_exchange(value, self.bits(order)[-1])

    def last_exchange(self, value, mask):
        return (yield value, mask)

    def scatter_groups(self, groups, others, states):
        for i, (value, other, order) in enumerate(zip(groups, others, ORDER_TOKENS)):
            yield self.scatter_tokens(value, other, i, order, states)

    def scatter_tokens(self, value, other, i, order, states):
        value = value.astype(F32) + other.astype(F32)
        for mask in reversed(self.bits(order)[:-1]):
            half = value.shape[0] // 2
            value = value.astype(BF16)
            received = yield value[half:], mask
            value = value[:half].astype(F32) + received.astype(F32)
        states[i] = value
        if i + 1 < len(TOKEN_GROUPS):
            yield (), None
            return ()
        value = jnp.concatenate([states[k] for k in range(len(TOKEN_GROUPS))], axis=1)
        received = yield value[1].astype(BF16), FIRST_TOKENS
        return value[0] + received.astype(F32)


def body(
    tokens,
    segments,
    routes,
    norm_attn,
    query_proj,
    latent_proj,
    norm_latent,
    expand_proj,
    output_proj,
    norm_ffn,
    router,
    shared_gate,
    shared_up,
    shared_down,
    expert_gate,
    expert_up,
    expert_down,
    cotangent,
):
    chips = Chips()
    n, cores, chip, core = chips.n, chips.f, chips.chip, chips.core
    seq = SEQ_DEV * cores
    heads = H // cores
    shard = D // (n * cores)
    expert_count = n * expert_gate.shape[0]
    small_cut = (shard, 2 * shard, 2 * shard + norm_latent.shape[0])

    tokens_seq = chips.gather_cores(tokens)
    small = jnp.concatenate([norm_attn, norm_ffn, norm_latent, router.reshape(-1)])
    query_own = chips.swap_cores(query_proj, 1, 0)
    query_cut = query_own.shape[1] // 2
    expand_own = chips.swap_cores(expand_proj, 1, 0)
    output_own = chips.swap_cores(output_proj, 1, 0)
    output_cut = output_own.shape[1] // 2
    width = shared_gate.shape[1] // n
    tiny = jnp.concatenate([chips.gather_cores(small[None]).reshape(-1), routes.astype(BF16).reshape(-1)])
    tiny_size = tiny.shape[0]
    columns = latent_proj.shape[1]
    tiny_rows = -(-tiny_size // columns)
    tiny = jnp.pad(tiny, (0, tiny_rows * columns - tiny_size)).reshape(tiny_rows, columns)
    latent_own = jnp.concatenate([latent_proj, tiny], axis=0)
    tokens_seq, query_own, expand_own, output_own, latent_own = together(
        tokens_seq, query_own, expand_own, output_own, latent_own
    )

    def shared_columns(*weights):
        weights = yield weights, None
        shared_in = jnp.stack([w.reshape(shard, n, -1) for w in weights], 2)
        shared_in = shared_in.transpose(1, 0, 2, 3).reshape(n * shard, 2 * width)
        for _ in range(3):
            shared_in = yield shared_in, None
        return lax.all_to_all(shared_in, "expert", split_axis=0, concat_axis=0, tiled=True)

    query_first, query_last, expand_weight, latent_own, shared_in = chips.lockstep(
        chips.gather_chips(query_own[:, :query_cut], ORDER_QUERY[0]),
        chips.gather_chips(query_own[:, query_cut:], ORDER_QUERY[1]),
        chips.gather_chips(expand_own, ORDER_EXPAND),
        chips.gather_chips(latent_own, ORDER_LATENT),
        shared_columns(shared_gate, shared_up),
    )
    (
        query_first, query_last, expand_weight, latent_own, shared_in, tokens_seq, output_own,
        cot_in,
    ) = together(
        query_first, query_last, expand_weight, latent_own, shared_in, tokens_seq, output_own,
        cotangent,
    )
    tiny = latent_own[:, shard:].reshape(n, -1)
    latent_own = latent_own[:, :shard]
    routes_all = tiny[:, cores * small.shape[0] : tiny_size].astype(jnp.int32)
    routes_all = routes_all.reshape(n, SEQ_DEV, TOPK)
    small = tiny[:, : cores * small.shape[0]].reshape(n * cores, -1)
    gain_attn = small[:, : small_cut[0]].reshape(-1).astype(F32)
    gain_ffn = small[:, small_cut[0] : small_cut[1]].reshape(-1).astype(F32)
    gain_latent = small[:, small_cut[1] : small_cut[2]].reshape(-1).astype(F32)
    query_parts = [query_first.reshape(D, -1), query_last.reshape(D, -1)]
    expand_weight = expand_weight.reshape(KVR, -1)
    latent_own_rows = latent_own.reshape(n * shard, -1)
    gate_full, up_full, down_full = (
        lax.all_gather(w[0], "fsdp", axis=0, tiled=True)
        for w in (expert_gate, expert_up, expert_down)
    )
    ff = gate_full.shape[1]

    def idle(rounds):
        for _ in range(rounds):
            yield (), None

    def shared_weights(value):
        value = yield value, None
        return lax.all_gather(
            value.reshape(n, 1, shard, 2 * width), "fsdp", axis=1, tiled=True
        ).reshape(D, 2 * width)

    outputs = {}

    def output_weights(part):
        if part == 0:
            value = yield from chips.gather_chips(output_own, ORDER_OUTPUT[0])
            outputs["first"] = value
        else:
            yield from idle(len(chips.bits(ORDER_OUTPUT[0])))
        value = outputs["first"][..., part * output_cut : (part + 1) * output_cut]
        order = chips.bits(ORDER_OUTPUT[1 + part])
        state = chips.bits(ORDER_OUTPUT[0])
        value = yield from chips.gather_chips(value, order[:-1], state)
        other = yield value, order[-1]
        return value, other

    half = n // 2

    extra = -(-(width + expert_count) // LANES) * LANES
    member_pad = (width + LANES - extra, extra - width - expert_count)

    def expert_members(routes_all):
        turns = []
        for last in (False, True):
            for order in ORDER_TOKENS:
                order = chips.bits((FIRST_TOKENS, *order))
                these = [0]
                for mask in order[:-1]:
                    these = these + [t ^ mask for t in these]
                turns += [t ^ order[-1] if last else t for t in these]
        blocks = routes_all.at[chip ^ jnp.array(turns, jnp.int32)].get(mode="promise_in_bounds")
        blocks = blocks.reshape(2, len(TOKEN_GROUPS), half, SEQ_DEV, TOPK)
        members = []
        for last in range(2):
            parts, start = [], 0
            for i, size in enumerate(TOKEN_GROUPS):
                parts.append(blocks[last, i, :, start : start + size].reshape(half * size, TOPK))
                start += size
            named = jnp.concatenate(parts, axis=0)[:, :, None]
            member = jnp.any(named == jnp.arange(expert_count, dtype=jnp.int32), axis=1)
            members.append(jnp.pad(member.astype(F32), ((0, 0), member_pad)))
        return members

    positions = jnp.arange(seq, dtype=jnp.int32)
    cos_table, sin_table = rope_tables(positions)
    inputs_f = tokens.astype(F32)
    score_scale = (DN + DR) ** (-0.5)

    def attention():
        rows = yield tokens_seq, None
        normed = rms_scale(rows.astype(F32), gain_attn).astype(BF16)
        normed_part = lax.dynamic_index_in_dim(
            normed.reshape(seq, n, cores, shard), core, 2, keepdims=False
        ).reshape(seq, n * shard)
        latent = chips.sum_cores(product(normed_part, latent_own_rows))
        query_all = jnp.concatenate([product(normed, part) for part in query_parts], axis=1)
        query_all = query_all.reshape(seq, heads, DN + DR)
        query_nope = query_all[..., :DN].astype(BF16)
        query_rope = rotate(
            query_all[..., DN:], cos_table[:, None, :], sin_table[:, None, :]
        ).astype(BF16)
        normed, normed_part, latent, query_nope, query_rope = yield (
            (normed, normed_part, latent, query_nope, query_rope),
            None,
        )
        latent_norm = rms_scale(latent[:, :KVR], gain_latent).astype(BF16)
        key_rope = rotate(latent[:, KVR:], cos_table, sin_table).astype(BF16)
        expanded = product(latent_norm, expand_weight).astype(BF16).reshape(seq, heads, DN + DV)
        key_nope = expanded[..., :DN]
        values_all = expanded[..., DN:]
        allowed = (positions[:, None] >= positions[None, :]) & (
            segments[:, None] == segments[None, :]
        )
        scores = jnp.einsum("thd,shd->hts", query_nope, key_nope, preferred_element_type=F32)
        scores = scores + jnp.einsum(
            "thd,sd->hts", query_rope, key_rope, preferred_element_type=F32
        )
        scores = jnp.where(allowed[None], scores * score_scale, -1e30)
        shifted = jnp.exp(scores - jnp.max(scores, axis=-1, keepdims=True))
        probs = shifted / jnp.sum(shifted, axis=-1, keepdims=True)
        latent_norm, key_rope, key_nope, values_all, probs = yield (
            (latent_norm, key_rope, key_nope, values_all, probs),
            None,
        )
        probs_low = probs.astype(BF16)
        attended = jnp.einsum("hts,shd->thd", probs_low, values_all, preferred_element_type=F32)
        attended = attended.reshape(seq, heads * DV).astype(BF16)
        attended = yield chips.gather_cores(attended, axis=1), None
        return (
            normed, normed_part, latent, query_nope, query_rope, latent_norm, key_rope, key_nope, values_all,
            probs, probs_low, attended,
        )

    def joined_output(parts):
        full = []
        for (own_part, other_part), order in zip(parts, ORDER_OUTPUT[1:]):
            mask = chips.bits(order)[-1]
            high = (chip // mask) % 2 == 1
            lower = jnp.where(high, other_part, own_part)
            upper = jnp.where(high, own_part, other_part)
            place = sum(m > mask for m in chips.bits((8, 4, 2, 1)))
            full.append(jnp.stack([lower, upper], axis=place).reshape(D, -1))
        return full

    def late_members(routes_all):
        yield from idle(3)
        routes_all = yield routes_all, None
        return expert_members(routes_all)

    states = {}
    *output_parts, kept_attention, shared_in, members, cot_zero, cot_one, cot_two = chips.lockstep(
        output_weights(0),
        output_weights(1),
        attention(),
        shared_weights(shared_in),
        late_members(routes_all),
        *chips.gather_groups(cot_in, states),
    )
    cot_first = [cot_zero, cot_one, cot_two]
    (
        normed, normed_part, latent, query_nope, query_rope, latent_norm, key_rope, key_nope, values_all,
        probs, probs_low, attended,
    ) = kept_attention
    hidden = []
    for (own_part, other_part), order in zip(output_parts, ORDER_OUTPUT[1:]):
        keep, send = chips.halves(attended, chips.bits(order)[-1], D // n)
        part = product(keep, own_part.reshape(D // 2, -1))
        hidden.append(part + product(send, other_part.reshape(D // 2, -1)))
    hidden = inputs_f + chips.swap_cores(jnp.concatenate(hidden, axis=1), 0, 1)
    normed_ffn = rms_scale(hidden, gain_ffn).astype(BF16)

    def beside(function, *values):
        values = yield values, None
        return function(*values)

    own = (jnp.arange(expert_count, dtype=jnp.int32) == chip).astype(F32)
    own = jnp.pad(own, member_pad)[None]

    def flat(groups):
        return [v.reshape(-1, D) for v in groups]

    def blocks(groups):
        return [v.reshape(half, -1, D) for v in groups]

    def forward(groups, member):
        rows = flat(groups)
        out, (logits, gate_act, up_act, hidden_act) = expert_forward(rows, member, own, weights)
        return blocks(out), (rows, logits, gate_act, up_act, hidden_act)

    def backward(kept, groups, member):
        _, logits, gate_act, up_act, _ = kept
        cot = flat(groups)
        back, (gate_back, up_back) = expert_backward(
            cot, member, own, logits, gate_act, up_act, weights
        )
        return blocks(back), (cot, gate_back, up_back)

    def extra_weights(shared_in, router_all, shared_down_own):
        gate_extra = jnp.concatenate([shared_in[:, :width], router_all], axis=1)
        gate_extra = jnp.pad(gate_extra, ((0, 0), (0, extra - width - expert_count)))
        up_extra = jnp.pad(shared_in[:, width:], ((0, 0), (0, extra - width)))
        down_extra = jnp.pad(chips.gather_cores(shared_down_own), ((0, extra - width), (0, 0)))
        return gate_full, gate_extra, up_full, up_extra, down_full, down_extra

    def backward_halves(attended, normed, latent_norm, normed_part):
        return (
            [chips.first_halves(attended, order) for order in BACK_OUTPUT[:2]],
            [chips.first_halves(normed, order) for order in BACK_QUERY],
            chips.first_halves(latent_norm, BACK_EXPAND),
            chips.first_halves(normed_part, BACK_LATENT),
        )

    *rows_first, halves, output_full, weights = chips.lockstep(
        *chips.gather_groups(normed_ffn, {}),
        beside(backward_halves, attended, normed, latent_norm, normed_part),
        beside(lambda *parts: joined_output(parts), *output_parts),
        beside(extra_weights, shared_in, small[:, small_cut[2] :].reshape(D, -1), shared_down),
    )
    attended_halves, normed_halves, latent_halves, normed_part_halves = halves
    *rows_last, (out_first, kept_first) = chips.lockstep(
        *chips.last_groups(rows_first), beside(forward, rows_first, members[0])
    )
    cot_first, rows_last = together(cot_first, rows_last)
    *cot_last, (out_last, kept_last) = chips.lockstep(
        *chips.last_groups(cot_first), beside(forward, rows_last, members[1])
    )
    *sent_out, (back_last, grads_last) = chips.lockstep(
        *chips.last_groups(out_last), beside(backward, kept_last, cot_last, members[1])
    )
    *sent_back, (back_first, grads_first) = chips.lockstep(
        *chips.last_groups(back_last), beside(backward, kept_first, cot_first, members[0])
    )

    def down_grads(hidden_acts, cots, rows, gate_back):
        rows = [v for groups in rows for v in groups]
        rows, gate_back = yield (rows, gate_back), None
        gate_part = in_weights(rows, gate_back, ff, 0)
        gate_part = yield gate_part, None
        hidden_acts, cots = yield (hidden_acts, cots), None
        down = down_weights(hidden_acts, [v for groups in cots for v in groups], ff)
        return down, gate_part

    *_, ffn_grad, ((down_w, down_extra_w), gate_part) = chips.lockstep(
        *chips.scatter_groups(back_first, sent_back, {}),
        down_grads(
            (kept_first[4], kept_last[4]),
            (grads_first[0], grads_last[0]),
            (kept_first[0], kept_last[0]),
            (grads_first[1], grads_last[1]),
        ),
    )

    middle = {}

    def through_norm(ffn_grad):
        ffn_grad = yield ffn_grad, None
        _, norm_pull = jax.vjp(rms_scale, hidden, gain_ffn)
        hidden_part, gain_ffn_grad = norm_pull(ffn_grad)
        hidden_grad = cotangent.astype(F32) + hidden_part
        middle["attn_grad"] = chips.swap_cores(hidden_grad.astype(BF16), 1, 0)
        middle["hidden_grad"], middle["gain"] = yield (hidden_grad, gain_ffn_grad), None
        return middle["hidden_grad"], middle["gain"]

    def output_grads(part):
        yield from idle(1)
        grads = middle["attn_grad"][:, part * output_cut : (part + 1) * output_cut]
        order = chips.bits(BACK_OUTPUT[part])
        value = yield from chips.weight_grad(attended_halves[part], grads, order)
        middle["output", part] = value
        if part == 0:
            yield from idle(2)
            return ()
        value = jnp.concatenate([middle["output", 0], value], axis=-1)
        return (yield from chips.scatter_chips(value, BACK_OUTPUT[2], order))

    def in_grads(rows, gate_back, up_back, gate_part):
        rows = [v for groups in rows for v in groups]
        yield from idle(2)
        rows, gate_back, gate_part = yield (rows, gate_back, gate_part), None
        gate_w, gate_x = yield in_weights(rows, gate_back, ff, 1, gate_part), None
        middle["router_grad"] = gate_x[:, width : width + expert_count]
        gate_w = lax.psum_scatter(gate_w, "fsdp", scatter_dimension=0, tiled=True)
        rows, up_back = together(rows, up_back, gate_x)[:2]
        up_w, up_x = in_weights(rows, up_back, ff, None)
        gate_w, up_w, gate_x, up_x = yield (gate_w, up_w, gate_x, up_x), None
        gate_w = gate_w.astype(F32)[None]
        up_w = lax.psum_scatter(up_w, "fsdp", scatter_dimension=0, tiled=True)
        shared = jnp.concatenate([gate_x[:, :width], up_x[:, :width]], axis=1)
        shared = chips.scatter_cores(shared.reshape(n, cores * shard, 2 * width), 1)
        shared = yield shared, None
        shared = lax.all_to_all(shared, "expert", split_axis=0, concat_axis=0, tiled=True)
        shared, up_w = yield (shared, up_w), None
        shared = shared.astype(F32).reshape(n, shard, 2, width).transpose(2, 1, 0, 3)
        return (gate_w, up_w.astype(F32)[None]), shared.reshape(2, shard, n * width)

    def second_grads(down_w, down_extra_w):
        down_w, down_extra_w = yield (down_w, down_extra_w), None
        down_w = lax.psum_scatter(down_w, "fsdp", scatter_dimension=0, tiled=True)
        down_extra_w = chips.scatter_cores(down_extra_w[:width])
        down_w, down_extra_w = yield (down_w, down_extra_w), None
        yield from idle(1)
        down_w = yield down_w, None
        return down_w.astype(F32)[None], down_extra_w

    def attention_back():
        yield (), None
        attn_grad = middle["attn_grad"]
        attended_grad = outer_cols(attn_grad[:, :output_cut], output_full[0]) + outer_cols(
            attn_grad[:, output_cut:], output_full[1]
        )
        attended_grad = yield chips.scatter_cores(attended_grad, 1).astype(BF16), None
        attended_grad = attended_grad.reshape(seq, heads, DV)
        prob_grad = jnp.einsum("thd,shd->hts", attended_grad, values_all, preferred_element_type=F32)
        weighted = jnp.sum(probs * prob_grad, axis=-1, keepdims=True)
        score_grad = (probs * (prob_grad - weighted)).astype(BF16)
        query_nope_grad = score_scale * jnp.einsum(
            "hts,shd->thd", score_grad, key_nope, preferred_element_type=F32
        )
        query_rope_grad = score_scale * jnp.einsum(
            "hts,sd->thd", score_grad, key_rope, preferred_element_type=F32
        )
        key_nope_grad = score_scale * jnp.einsum(
            "hts,thd->shd", score_grad, query_nope, preferred_element_type=F32
        )
        key_rope_grad = score_scale * jnp.einsum(
            "hts,thd->sd", score_grad, query_rope, preferred_element_type=F32
        )
        values_grad = jnp.einsum(
            "hts,thd->shd", probs_low, attended_grad, preferred_element_type=F32
        )
        (query_nope_grad, query_rope_grad, key_nope_grad, key_rope_grad, values_grad) = yield (
            (query_nope_grad, query_rope_grad, key_nope_grad, key_rope_grad, values_grad),
            None,
        )
        expanded_grad = jnp.concatenate([key_nope_grad, values_grad], axis=2)
        expanded_grad = expanded_grad.reshape(seq, heads * (DN + DV)).astype(BF16)
        latent_back = chips.sum_cores(
            jnp.concatenate([outer_cols(expanded_grad, expand_weight), key_rope_grad], axis=1)
        )
        _, latent_pull = jax.vjp(rms_scale, latent[:, :KVR], gain_latent)
        latent_nope_grad, gain_latent_grad = latent_pull(latent_back[:, :KVR])
        gain_latent_grad = gain_latent_grad / cores
        latent_rope_grad = rotate(latent_back[:, KVR:], cos_table, -sin_table)
        latent_grad = jnp.concatenate([latent_nope_grad, latent_rope_grad], axis=1).astype(BF16)
        query_back = jnp.concatenate(
            [query_nope_grad, rotate(query_rope_grad, cos_table[:, None, :], -sin_table[:, None, :])],
            axis=2,
        )
        query_back = query_back.reshape(seq, heads * (DN + DR)).astype(BF16)
        middle["query_back"] = query_back
        middle["expanded_grad"] = expanded_grad
        middle["latent_grad"] = latent_grad
        middle["gain_latent_grad"] = gain_latent_grad
        yield (query_back, expanded_grad, latent_grad), None

    def projection_grads(rows, name, columns, order):
        yield from idle(3)
        return (yield from chips.weight_grad(rows, middle[name][:, columns], order))

    back_cut = heads * (DN + DR) * 5 // 12 // LANES * LANES

    def input_grads():
        yield from idle(4)
        query_back, latent_grad = yield (middle["query_back"], middle["latent_grad"]), None
        normed_grad = outer_cols(query_back[:, :query_cut], query_parts[0]) + outer_cols(
            query_back[:, query_cut:], query_parts[1]
        )
        normed_grad, latent_grad, latent_rows = yield (normed_grad, latent_grad, latent_own), None
        latent_weight = chips.gather_cores(latent_rows[:, None], axis=1).reshape(D, -1)
        latent_grad_own = lax.dynamic_slice_in_dim(latent_grad, core * SEQ_DEV, SEQ_DEV, 0)
        normed_grad = chips.scatter_cores(normed_grad) + outer_cols(latent_grad_own, latent_weight)
        _, first_pull = jax.vjp(rms_scale, inputs_f, gain_attn)
        input_part, gain_attn_grad = first_pull(normed_grad)
        tokens_grad = (middle["hidden_grad"] + input_part).astype(BF16)
        tokens_grad, gain_attn_grad = yield (tokens_grad, gain_attn_grad), None
        small_grad = jnp.concatenate(
            [
                gain_attn_grad.reshape(n * cores, -1),
                middle["gain"].reshape(n * cores, -1),
                middle["gain_latent_grad"].reshape(n * cores, -1),
                middle["router_grad"].astype(F32).reshape(n * cores, -1),
            ],
            axis=1,
        )
        small_grad = lax.all_to_all(
            small_grad.reshape(n, -1), "expert", split_axis=0, concat_axis=0, tiled=True
        )
        small_grad = jnp.sum(small_grad, axis=0).reshape(cores, -1)
        return tokens_grad, chips.scatter_cores(small_grad).reshape(-1)

    (
        _, _, _, block_sum, _, _, output_grad, query_first_grad, query_last_grad, expand_grad,
        latent_weight_grad, in_grad, second_grad, input_grad,
    ) = chips.lockstep(
        through_norm(ffn_grad),
        *chips.scatter_groups(out_first, sent_out, {}),
        attention_back(),
        output_grads(0),
        output_grads(1),
        projection_grads(normed_halves[0], "query_back", slice(0, back_cut), BACK_QUERY[0]),
        projection_grads(normed_halves[1], "query_back", slice(back_cut, None), BACK_QUERY[1]),
        projection_grads(latent_halves, "expanded_grad", slice(None), BACK_EXPAND),
        projection_grads(normed_part_halves, "latent_grad", slice(None), BACK_LATENT),
        in_grads(
            (kept_first[0], kept_last[0]),
            (grads_first[1], grads_last[1]),
            (grads_first[2], grads_last[2]),
            gate_part,
        ),
        second_grads(down_w, down_extra_w),
        input_grads(),
    )
    (gate_grad_w, up_grad_w), shared_in_grad = in_grad
    down_grad_w, shared_down_grad = second_grad
    tokens_grad, small_grad = input_grad
    block_out = (hidden + block_sum).astype(BF16)
    output_grad = chips.swap_cores(output_grad, 0, 1)
    query_grad = jnp.concatenate([query_first_grad, query_last_grad], axis=1)
    query_grad = chips.swap_cores(query_grad, 0, 1)
    expand_grad = chips.swap_cores(expand_grad, 0, 1)
    return (
        block_out,
        tokens_grad,
        small_grad[: small_cut[0]],
        query_grad,
        latent_weight_grad,
        small_grad[small_cut[1] : small_cut[2]],
        expand_grad,
        output_grad,
        small_grad[small_cut[0] : small_cut[1]],
        small_grad[small_cut[2] :].reshape(shard, -1),
        shared_in_grad[0],
        shared_in_grad[1],
        shared_down_grad,
        gate_grad_w,
        up_grad_w,
        down_grad_w,
    )


def solution(mesh):
    rows = P(("expert", "fsdp"), None)
    flat = P(("expert", "fsdp"))
    experts = P("expert", "fsdp", None)
    return jax.shard_map(
        body,
        mesh=mesh,
        in_specs=(
            rows, P("expert"), rows, flat, rows, rows, flat, rows, rows, flat, rows, rows, rows,
            rows, experts, experts, experts, rows,
        ),
        out_specs=(
            rows, rows, flat, rows, rows, flat, rows, rows, flat, rows, rows, rows, rows, experts,
            experts, experts,
        ),
        check_vma=False,
    )
```
